32 devices in a mesh: dp: 16 (over z, y, core), mp: 2 (over x).
Axes of the slice: x: 2, y: 2, z: 4, core: 2. Of those that a mesh axis runs over, the one named last changes fastest.
Arguments:
- hidden_in: bfloat16 [32768, 1024], P(('dp', 'mp')), may hold values from -46 to 46
- seq_lengths: int32 [16, 4], P('dp'), may hold values from 0 to 2048, as said below
- ln_scale: float32 [1024], replicated, may hold values from 0.25 to 1.75
- ln_bias: float32 [1024], replicated, may hold values from -3 to 3
- qkv_weight: bfloat16 [1024, 3072], P(None, 'mp'), may hold values from -0.1875 to 0.1875
- out_weight: bfloat16 [1024, 1024], P('mp'), may hold values from -1.5 to 1.5
- in_weight: bfloat16 [1024, 4096], P(None, 'mp'), may hold values from -0.1875 to 0.1875
- down_weight: bfloat16 [4096, 1024], P('mp'), may hold values from -0.09375 to 0.09375
- out_grad: bfloat16 [32768, 1024], P(('dp', 'mp')), may hold values from -6 to 6
Outputs:
- hidden_out: bfloat16 [32768, 1024], P(('dp', 'mp'))
- grad_hidden: float32 [32768, 1024], P(('dp', 'mp'))
- grad_scale: float32 [1024], replicated
- grad_bias: float32 [1024], replicated
- grad_qkv_weight: float32 [1024, 3072], P(None, 'mp')
- grad_out_weight: float32 [1024, 1024], P('mp')
- grad_in_weight: float32 [1024, 4096], P(None, 'mp')
- grad_down_weight: float32 [4096, 1024], P('mp')
- stats: float32 [3], replicated
The draws below stay inside these ranges and needn't reach their ends.
Inputs may be any that keep to these rules, and one draw needn't show every extreme that they name: `seq_lengths`: each group's lengths sum to 2048; every run of 2048 tokens of a group, from the group's start, holds whole sequences of 512, 1024 or 2048 tokens, listed in order, with zeros in the slots that a run leaves unused; some group holds a sequence of 2048 tokens.
All inputs are finite; a program needn't handle non-finite values.
Results may differ from the reference program's by a relative error of at most 0.015.
Values may be sent and summed in bfloat16 or wider, within the bound.
A program may use at most 192 MiB of HBM per device.

```python
import jax
import jax.numpy as jnp
import numpy as np
from jax import lax

D = 1024
HEADS = 16
HEAD = 64
ROT = 16
FF = 4096
SEQ_UNIT = 512
GROUP_TOK = 2048
TOKENS = 32768
N_DP = 16
N_MP = 2


def draw_seq_lengths(key, part):
    key = jax.random.fold_in(key, 11)
    length_table = jnp.asarray(np.array([[4, 0, 0, 0], [2, 2, 0, 0], [2, 1, 1, 0], [1, 1, 2, 0], [1, 1, 1, 1]], dtype=np.int32))
    quad_count = GROUP_TOK // (4 * SEQ_UNIT)
    pattern = jax.random.randint(key, (N_DP, quad_count), 0, 5).astype(jnp.int32)
    pattern = pattern.at[0, 0].set(0)
    lengths = length_table[pattern] * SEQ_UNIT
    return lengths.reshape(N_DP, quad_count * 4).astype(jnp.int32)


def draw_hidden_in(key, part):
    key = jax.random.fold_in(key, 7)
    elem_key, column_key, row_key = jax.random.split(key, 3)
    column_scale = jnp.exp(jax.random.uniform(column_key, (D,), minval=jnp.log(0.3), maxval=jnp.log(3.0)))
    steps_along = jnp.arange(TOKENS, dtype=jnp.float32) / (TOKENS - 1)
    row_ramp = 0.25 + 2.75 * steps_along
    row_scale = row_ramp * jnp.exp(jax.random.uniform(row_key, (TOKENS,), minval=jnp.log(0.8), maxval=jnp.log(1.25)))
    entries = jax.random.truncated_normal(elem_key, -4.0, 4.0, (TOKENS, D))
    return (entries * row_scale[:, None] * column_scale[None, :]).astype(jnp.bfloat16)


def steps_of(rng, dims, shards, smallest, high):
    gain, own = 1.0, jax.random.fold_in(rng, 6)
    for dim, parts in shards:
        heights = jnp.exp(jax.random.uniform(jax.random.fold_in(own, dim), (parts,), jnp.float32, smallest / len(shards), high / len(shards)))
        gain = gain * jnp.repeat(heights, dims[dim] // parts).reshape([-1 if axis == dim else 1 for axis in range(len(dims))])
    return gain


def bell_draw(own_key, shape, width, bound, pieces=(), kind=jnp.bfloat16):
    values = width * jax.random.normal(own_key, shape, jnp.float32)
    if pieces:
        values = values * steps_of(own_key, shape, pieces, -0.22, 0.18)
    return jnp.clip(values, -bound, bound).astype(kind)


def setup_inputs(seed: int = 0) -> dict:
    seeds = jax.random.split(jax.random.key(seed), 10)
    return {
        "hidden_in": draw_hidden_in(jax.random.fold_in(seeds[9], 71), 0),
        "seq_lengths": draw_seq_lengths(jax.random.fold_in(seeds[9], 71), 0),
        "ln_scale": jnp.clip(1.0 + 0.15 * jax.random.normal(seeds[2], (D,), jnp.float32), 0.25, 1.75),
        "ln_bias": bell_draw(seeds[3], (D,), 0.3, 3.0, (), jnp.float32),
        "qkv_weight": bell_draw(seeds[4], (D, 3 * D), D ** -0.5, 0.1875, ((1, 2),)),
        "out_weight": bell_draw(seeds[5], (D, D), (D // 64) ** -0.5, 1.5, ((0, 2),)),
        "in_weight": bell_draw(seeds[6], (D, FF), D ** -0.5, 0.1875, ((1, 2),)),
        "down_weight": bell_draw(seeds[7], (FF, D), FF ** -0.5, 0.09375, ((0, 2),)),
        "out_grad": bell_draw(seeds[8], (TOKENS, D), 1.0, 6.0, ((0, 32),)),
    }


epsilon = 1e-05
rope_base = 10000.0
masked_score = -1e+30

@jax.custom_vjp
def low(v):
    return lax.optimization_barrier(v.astype(jnp.bfloat16)).astype(jnp.float32)

@jax.custom_vjp
def low_back(v):
    return v

def low_keep(v):
    return (low(v), None)

def low_pass(kept, grad):
    return (grad,)

def back_keep(v):
    return (v, None)

def back_low(kept, grad):
    return (low(grad),)
low.defvjp(low_keep, low_pass)
low_back.defvjp(back_keep, back_low)

def matmul_hi(left_side, right_side):
    return jnp.dot(left_side, right_side, precision=lax.Precision.HIGHEST, preferred_element_type=jnp.float32)

def layout(lengths):
    seg_ends = jnp.cumsum(lengths).astype(jnp.int32)
    positions = jnp.arange(GROUP_TOK, dtype=jnp.int32)
    closed = seg_ends[None, :] <= positions[:, None]
    segment = lax.optimization_barrier(jnp.sum(closed.astype(jnp.int32), axis=1)).astype(jnp.int32)
    seg_start = lax.optimization_barrier(jnp.sum(jnp.where(closed, lengths[None, :], 0), axis=1)).astype(jnp.int32)
    return (segment, positions - seg_start)

def rotary_tables(offset):
    half_rot = ROT // 2
    inv_freq = jnp.power(rope_base, -2.0 * jnp.arange(half_rot, dtype=jnp.float32) / ROT)
    angles = offset.astype(jnp.float32)[:, None] * inv_freq[None, :]
    return (jnp.cos(angles), jnp.sin(angles))

def rotate(values, cosine_table, sine_table):
    half_rot = ROT // 2
    front_half = values[..., :half_rot]
    back_half = values[..., half_rot:ROT]
    cosine = cosine_table[:, None, :]
    sine_rows = sine_table[:, None, :]
    return jnp.concatenate([front_half * cosine - back_half * sine_rows, back_half * cosine + front_half * sine_rows, values[..., ROT:]], axis=-1)

def to_items(values, quad_rows):
    group_rows, heads_dev, head_dim = values.shape
    quad_count = group_rows // quad_rows
    return values.reshape(quad_count, quad_rows, heads_dev, head_dim).transpose(2, 0, 1, 3).reshape(heads_dev * quad_count, quad_rows, head_dim)

def from_items(items_arr, heads_dev):
    total_items, quad_rows, head_dim = items_arr.shape
    quad_count = total_items // heads_dev
    return items_arr.reshape(heads_dev, quad_count, quad_rows, head_dim).transpose(1, 2, 0, 3).reshape(quad_count * quad_rows, heads_dev * head_dim)

def attend_item(packed):
    queries, key_rows, values, segment = packed
    raw_score = jnp.dot(queries, key_rows.T, precision=lax.Precision.HIGHEST) * HEAD ** (-0.5)
    positions = jnp.arange(segment.shape[0])
    allowed = (segment[:, None] == segment[None, :]) & (positions[None, :] <= positions[:, None])
    scores = jnp.where(allowed, low_back(raw_score), masked_score)
    row_max = lax.optimization_barrier(jnp.max(scores, axis=1, keepdims=True))
    weight = jnp.exp(scores - row_max)
    attn_prob = weight / lax.optimization_barrier(jnp.sum(weight, axis=1, keepdims=True))
    return jnp.dot(low(attn_prob), values, precision=lax.Precision.HIGHEST)

def group_pass(rows_in, lengths, scale_vec, bias_vec, qkv_mat, out_mat, in_mat, down_mat):
    segment, offset = layout(lengths)
    cosine_table, sine_table = rotary_tables(offset)
    quad_rows = 4 * SEQ_UNIT
    heads_dev = HEADS // N_MP
    head_width = heads_dev * HEAD
    hidden_dev = FF // N_MP
    row_mean = lax.optimization_barrier(jnp.mean(rows_in, axis=1, keepdims=True))
    centred = rows_in - row_mean
    row_var = lax.optimization_barrier(jnp.mean(centred * centred, axis=1, keepdims=True))
    normed = low(centred * lax.rsqrt(row_var + epsilon) * scale_vec + bias_vec)
    item_segment = jnp.tile(segment.reshape(GROUP_TOK // quad_rows, quad_rows), (heads_dev, 1))
    running = jnp.zeros((GROUP_TOK, D), jnp.float32)
    context_sq = jnp.zeros((), jnp.float32)
    active_sq = jnp.zeros((), jnp.float32)
    for slice_index in range(N_MP):
        shared = low_back(normed)
        cols = qkv_mat[:, slice_index * 3 * head_width:(slice_index + 1) * 3 * head_width]
        qkv_rows = low_back(matmul_hi(shared, cols)).reshape(GROUP_TOK, heads_dev, 3, HEAD)
        queries = low(rotate(qkv_rows[:, :, 0], cosine_table, sine_table))
        key_rows = low(rotate(qkv_rows[:, :, 1], cosine_table, sine_table))
        values = low(qkv_rows[:, :, 2])
        packed = (to_items(queries, quad_rows), to_items(key_rows, quad_rows), to_items(values, quad_rows), item_segment)
        context_items = lax.map(jax.checkpoint(attend_item), packed)
        context = low_back(low(from_items(context_items, heads_dev)))
        hidden = low_back(matmul_hi(shared, in_mat[:, slice_index * hidden_dev:(slice_index + 1) * hidden_dev]))
        active = low(jax.nn.gelu(hidden, approximate=False))
        branch = matmul_hi(context, out_mat[slice_index * head_width:(slice_index + 1) * head_width]) + matmul_hi(active, down_mat[slice_index * hidden_dev:(slice_index + 1) * hidden_dev])
        running = running + low(branch)
        context_sq = context_sq + jnp.sum(context * context)
        active_sq = active_sq + jnp.sum(active * active)
    outputs = rows_in + running
    return (outputs, jnp.stack([jnp.sum(outputs * outputs), context_sq, active_sq]))

def reference(hidden_in, seq_lengths, ln_scale, ln_bias, qkv_weight, out_weight, in_weight, down_weight, out_grad):

    def forward(residual, scale_vec, bias_vec, qkv_mat, out_mat, in_mat, down_mat):
        groups = residual.reshape(N_DP, GROUP_TOK, D)

        def scan_step(running, group_item):
            rows_in, lengths = group_item
            outputs, stat_sums = jax.checkpoint(group_pass)(rows_in, lengths, scale_vec, bias_vec, qkv_mat, out_mat, in_mat, down_mat)
            return (running + stat_sums, outputs)
        stat_sums, outputs = lax.scan(scan_step, jnp.zeros((3,), jnp.float32), (groups, seq_lengths))
        return (outputs.reshape(TOKENS, D), stat_sums)
    result, pullback, stat_sums = jax.vjp(forward, hidden_in.astype(jnp.float32), ln_scale.astype(jnp.float32), ln_bias.astype(jnp.float32), qkv_weight.astype(jnp.float32), out_weight.astype(jnp.float32), in_weight.astype(jnp.float32), down_weight.astype(jnp.float32), has_aux=True)
    gradients = pullback(out_grad.astype(jnp.float32))
    counts = jnp.array([TOKENS * D, TOKENS * D, TOKENS * FF], jnp.float32)
    stats = jnp.sqrt(stat_sums / counts)
    return (result.astype(jnp.bfloat16), gradients[0], gradients[1], gradients[2], gradients[3], gradients[4], gradients[5], gradients[6], stats)
```

```python
import functools

import jax
import jax.numpy as jnp
from jax import lax
from jax.experimental import pallas as pl
from jax.experimental.pallas import tpu as pltpu
from jax.sharding import PartitionSpec as P

HEAD = 64
ROT = 16
LANES = 128
TILE = 256
F32 = jnp.float32
BF = jnp.bfloat16

epsilon = 1e-05
rope_base = 10000.0
excluded = -1e20


def nn(a, b):
    return jnp.dot(a, b, preferred_element_type=F32)


def nt(a, b):
    return lax.dot_general(a, b, (((1,), (1,)), ((), ())), preferred_element_type=F32)


def tn(a, b):
    return lax.dot_general(a, b, (((0,), (0,)), ((), ())), preferred_element_type=F32)


def whole(shape):
    zeros = (0,) * len(shape)
    return pl.BlockSpec(shape, lambda *_: zeros, pipeline_mode=pl.Buffered(1))


def struct(shape, dtype):
    return jax.ShapeDtypeStruct(shape, dtype)


def cost(flops, nbytes, trans=0):
    return pl.CostEstimate(flops=int(flops), bytes_accessed=int(nbytes), transcendentals=int(trans))


def params(**kw):
    return pltpu.CompilerParams(vmem_limit_bytes=60 * 2**20, **kw)


def lane_ids(rows):
    return lax.broadcasted_iota(jnp.int32, (rows, LANES), 1)


def turn(x, cos, fwd, back):
    return x * cos + pltpu.roll(x, LANES - ROT // 2, 1) * fwd + pltpu.roll(x, ROT // 2, 1) * back


def gelu_parts(v):
    x = jnp.abs(v)
    bell = jnp.exp(v * v * (-0.5))
    t = 1.0 / (1.0 + x * (0.3275911 * 0.7071067811865476))
    poly = t * (
        0.254829592
        + t * (-0.284496736 + t * (1.421413741 + t * (-1.453152027 + t * 1.061405429)))
    )
    tail = 0.5 * poly * bell
    cdf = jnp.where(v >= 0, 1.0 - tail, tail)
    return v * cdf, cdf + v * bell * 0.3989422804014327


def project_kernel(
    pos, nrm, wqkv, win, cos, fwd, back, hot, neg, *rest
):
    q_out, k_out, v_out, act, slope, sq = rest[-6:]
    rows = nrm.shape[0]
    lane = lane_ids(rows)
    low = lane < HEAD
    x = nrm[...]
    c, f, b = cos[...], fwd[...], back[...]
    for p in range(wqkv.shape[1] // 384):
        y = nn(x, wqkv[:, p * 384 : (p + 1) * 384])
        g0, g1, g2 = y[:, :128], y[:, 128:256], y[:, 256:]
        r1, r2 = pltpu.roll(g1, HEAD, 1), pltpu.roll(g2, HEAD, 1)
        for h, (qk, v) in enumerate(((g0, g1), (jnp.where(low, r1, r2), r2))):
            qk = turn(qk, c, f, b)
            q_out[2 * p + h] = jnp.where(low, qk * HEAD**-0.5, hot[...].astype(F32)).astype(BF)
            k_out[2 * p + h] = jnp.where(low, pltpu.roll(qk, HEAD, 1), neg[...].astype(F32)).astype(BF)
            v_out[2 * p + h] = jnp.where(low, v, jnp.where(lane < HEAD + 2, 1.0, 0.0)).astype(BF)

    @pl.when(pl.program_id(0) == 0)
    def _():
        sq[...] = jnp.zeros_like(sq)

    step = min(512, win.shape[1])
    for j in range(win.shape[1] // step):
        cols = pl.ds(j * step, step)
        a, s = gelu_parts(nn(x, win[:, cols]))
        a = a.astype(BF)
        act[:, cols] = a
        slope[:, cols] = s.astype(BF)
        wide = a.astype(F32)
        sq[...] += jnp.sum((wide * wide).reshape(-1, 8, LANES), axis=0) if False else sum(
            jnp.sum(
                (wide[:, i * LANES : (i + 1) * LANES] ** 2).reshape(rows // 8, 8, LANES), axis=0
            )
            for i in range(step // LANES)
        )


def project(pos, total, heads, prior, nrm, wqkv, win, cos, fwd, back, hot, neg):
    rows, d = nrm.shape
    f = win.shape[1]
    row = lambda w: pl.BlockSpec((TILE, w), lambda i, pos: (i, 0))
    at = lambda w: pl.BlockSpec((TILE, w), lambda i, pos: (pos[0] + i, 0))
    hd = pl.BlockSpec((heads, TILE, LANES), lambda i, pos: (0, pos[0] + i, 0))
    any_ = pl.BlockSpec(memory_space=pl.ANY)
    big = struct((heads, total, LANES), BF)
    return pl.pallas_call(
        project_kernel,
        grid_spec=pltpu.PrefetchScalarGridSpec(
            num_scalar_prefetch=1,
            grid=(rows // TILE,),
            in_specs=[row(d), whole(wqkv.shape), whole(win.shape), at(LANES), at(LANES), at(LANES), at(LANES), at(LANES)]
            + [any_] * len(prior),
            out_specs=[hd, hd, hd, row(f), row(f), pl.BlockSpec((8, LANES), lambda i, pos: (0, 0))],
        ),
        out_shape=[big, big, big, struct((rows, f), BF), struct((rows, f), BF), struct((8, LANES), F32)],
        input_output_aliases={9 + i: i for i in range(len(prior))},
        compiler_params=params(),
        cost_estimate=cost(2 * rows * d * (f + wqkv.shape[1]), 2 * (d * (f + wqkv.shape[1]) + 6 * rows * d)),
        name="project",
    )(pos, nrm, wqkv, win, cos, fwd, back, hot, neg, *prior)


def cotangent_kernel(pos, dy, wout, wdown, slope, *rest):
    do_out, gpre = rest[-2:]
    x = dy[...]
    low = lane_ids(x.shape[0]) < HEAD
    g = nt(x, wout[...])
    for p in range(g.shape[1] // LANES):
        y = g[:, p * LANES : (p + 1) * LANES]
        do_out[2 * p] = jnp.where(low, y, 0.0).astype(BF)
        do_out[2 * p + 1] = jnp.where(low, pltpu.roll(y, HEAD, 1), 0.0).astype(BF)
    f = wdown.shape[0]
    step = min(512, f)
    for j in range(f // step):
        cols = pl.ds(j * step, step)
        gpre[:, cols] = (nt(x, wdown[cols, :]) * slope[:, cols].astype(F32)).astype(BF)


def cotangent(pos, total, heads, prior, dy, wout, wdown, slope):
    rows, d = dy.shape
    f = wdown.shape[0]
    row = lambda w: pl.BlockSpec((TILE, w), lambda i, pos: (i, 0))
    hd = pl.BlockSpec((heads, TILE, LANES), lambda i, pos: (0, pos[0] + i, 0))
    return pl.pallas_call(
        cotangent_kernel,
        grid_spec=pltpu.PrefetchScalarGridSpec(
            num_scalar_prefetch=1,
            grid=(rows // TILE,),
            in_specs=[row(d), whole(wout.shape), whole(wdown.shape), row(f)]
            + [pl.BlockSpec(memory_space=pl.ANY)] * len(prior),
            out_specs=[hd, row(f)],
        ),
        out_shape=[struct((heads, total, LANES), BF), struct((rows, f), BF)],
        input_output_aliases={5 + i: i for i in range(len(prior))},
        compiler_params=params(),
        cost_estimate=cost(2 * rows * d * (f + wout.shape[0]), 2 * (d * (f + wout.shape[0]) + 5 * rows * d)),
        name="cotangent",
    )(pos, dy, wout, wdown, slope, *prior)


def attend_kernel(q_ref, k_ref, v_ref, ctx, wide, keep, sq):
    h = pl.program_id(1)
    total = q_ref.shape[1]
    b = TILE
    tri = lax.broadcasted_iota(jnp.int32, (b, b), 0) >= lax.broadcasted_iota(jnp.int32, (b, b), 1)
    low = lane_ids(b) < HEAD

    @pl.when((h == 0) & (pl.program_id(0) == 0))
    def _():
        sq[...] = jnp.zeros_like(sq)

    for i in range(total // b):
        n = (i + 1) * b
        rows = pl.ds(i * b, b)
        s = nt(q_ref[0, rows, :], k_ref[0, :n, :])
        s_diag = jnp.where(tri, s[:, n - b :], excluded)
        top = jnp.max(s_diag, axis=1, keepdims=True)
        if i:
            top = jnp.maximum(top, jnp.max(s[:, : n - b], axis=1, keepdims=True))
        w = jnp.exp(s_diag - top).astype(BF)
        if i:
            w = jnp.concatenate([jnp.exp(s[:, : n - b] - top).astype(BF), w], axis=1)
        for j in range(i + 1):
            keep[0, i * (i + 1) // 2 + j] = w[:, j * b : (j + 1) * b]
        acc = nn(w, v_ref[0, :n, :])
        inv = 1.0 / acc[:, HEAD : HEAD + 1]
        acc = acc * inv
        wide[0, rows, :] = jnp.where(low, acc, inv)
        out = acc.astype(BF)
        real = jnp.where(low, out.astype(F32), 0.0)
        sq[...] += jnp.sum((real * real).reshape(b // 8, 8, LANES), axis=0)

        @pl.when(h == 0)
        def _():
            ctx[rows, :] = out

        @pl.when(h == 1)
        def _():
            both = jnp.where(low, ctx[rows, :].astype(F32), pltpu.roll(out.astype(F32), HEAD, 1))
            ctx[rows, :] = both.astype(BF)


def attend(q, k, v):
    heads, total, _ = q.shape
    tiles = total // TILE
    tiles = tiles * (tiles + 1) // 2
    hd = pl.BlockSpec((1, total, LANES), lambda p, h: (2 * p + h, 0, 0))
    return pl.pallas_call(
        attend_kernel,
        grid=(heads // 2, 2),
        in_specs=[hd, hd, hd],
        out_specs=[
            pl.BlockSpec((total, LANES), lambda p, h: (0, p)),
            hd,
            pl.BlockSpec((1, tiles, TILE, TILE), lambda p, h: (2 * p + h, 0, 0, 0)),
            pl.BlockSpec((8, LANES), lambda p, h: (0, 0)),
        ],
        out_shape=[
            struct((total, heads * HEAD), BF),
            struct((heads, total, LANES), F32),
            struct((heads, tiles, TILE, TILE), BF),
            struct((8, LANES), F32),
        ],
        compiler_params=params(),
        cost_estimate=cost(4 * heads * tiles * TILE * TILE * 256, heads * total * LANES * 20, heads * tiles * TILE * TILE),
        name="attend",
    )(q, k, v)


def attend_back_kernel(q_ref, k_ref, v_ref, do_ref, wide, keep, cos, fwd, back, out, dk_acc, dv_acc, dq_acc, hold):
    h = pl.program_id(1)
    total = q_ref.shape[1]
    b = TILE
    lane = lane_ids(b)
    low = lane < HEAD
    dk_acc[...] = jnp.zeros_like(dk_acc)
    dv_acc[...] = jnp.zeros_like(dv_acc)
    for i in range(total // b):
        n = (i + 1) * b
        rows = pl.ds(i * b, b)
        q = q_ref[0, rows, :]
        w = [keep[0, i * (i + 1) // 2 + j] for j in range(i + 1)]
        w = w[0] if i == 0 else jnp.concatenate(w, axis=1)
        context = wide[0, rows, :]
        inv = context[:, HEAD : HEAD + 1]
        scaled = (do_ref[0, rows, :].astype(F32) * inv).astype(BF)
        grad = scaled.astype(F32)
        delta = jnp.sum(jnp.where(low, grad * context, 0.0), axis=1, keepdims=True)
        delta_hi = delta.astype(BF).astype(F32)
        delta_lo = delta - delta_hi
        joined = jnp.where(lane == HEAD, -delta_hi, jnp.where(lane == HEAD + 1, -delta_lo, grad)).astype(BF)
        ds = w * nt(joined, v_ref[0, :n, :]).astype(BF)
        dq_acc[rows, :] = nn(ds, k_ref[0, :n, :]) * HEAD**-0.5
        dk_acc[:n, :] += tn(ds, q)
        dv_acc[:n, :] += tn(w, scaled)
    for i in range(total // b):
        rows = pl.ds(i * b, b)
        x = jnp.where(low, dq_acc[rows, :], pltpu.roll(dk_acc[rows, :], HEAD, 1))
        x = turn(x, cos[rows, :], -fwd[rows, :], -back[rows, :])
        dv = dv_acc[rows, :]

        @pl.when(h == 0)
        def _():
            out[rows, :LANES] = x.astype(BF)
            hold[rows, :] = dv

        @pl.when(h == 1)
        def _():
            r = pltpu.roll(x, HEAD, 1)
            out[rows, LANES : 2 * LANES] = jnp.where(low, hold[rows, :], r).astype(BF)
            out[rows, 2 * LANES :] = jnp.where(low, r, pltpu.roll(dv, HEAD, 1)).astype(BF)


def attend_back(q, k, v, do, wide, keep, cos, fwd, back):
    heads, total, _ = q.shape
    hd = pl.BlockSpec((1, total, LANES), lambda p, h: (2 * p + h, 0, 0))
    acc = pltpu.VMEM((total, LANES), F32)
    tiles = keep.shape[1]
    return pl.pallas_call(
        attend_back_kernel,
        grid=(heads // 2, 2),
        in_specs=[hd, hd, hd, hd, hd, pl.BlockSpec((1,) + keep.shape[1:], lambda p, h: (2 * p + h, 0, 0, 0))]
        + [whole(cos.shape)] * 3,
        out_specs=pl.BlockSpec((total, 384), lambda p, h: (0, p)),
        out_shape=struct((total, heads * 3 * HEAD), BF),
        scratch_shapes=[acc] * 4,
        compiler_params=params(),
        cost_estimate=cost(8 * heads * tiles * TILE * TILE * 256, heads * total * LANES * 40),
        name="attend_back",
    )(q, k, v, do, wide, keep, cos, fwd, back)


def pair_kernel(transposed, pos, a, b, c, d, out):
    dot = nt if transposed else nn
    out[...] = (dot(a[...], b[...]) + dot(c[...], d[...])).astype(BF)


def pair_matmul(pos, transposed, a, b, c, d):
    rows = c.shape[0]
    width = b.shape[0] if transposed else b.shape[1]
    return pl.pallas_call(
        functools.partial(pair_kernel, transposed),
        grid_spec=pltpu.PrefetchScalarGridSpec(
            num_scalar_prefetch=1,
            grid=(rows // TILE,),
            in_specs=[
                pl.BlockSpec((TILE, a.shape[1]), lambda i, pos: (pos[0] + i, 0)),
                whole(b.shape),
                pl.BlockSpec((TILE, c.shape[1]), lambda i, pos: (i, 0)),
                whole(d.shape),
            ],
            out_specs=pl.BlockSpec((TILE, width), lambda i, pos: (i, 0)),
        ),
        out_shape=struct((rows, width), BF),
        compiler_params=params(),
        cost_estimate=cost(2 * rows * width * (a.shape[1] + c.shape[1]), 2 * (b.size + d.size + rows * (width + a.shape[1] + c.shape[1]))),
        name="pair_matmul",
    )(pos, a, b, c, d)


def weight_kernel(n, slots, *refs):
    xs, ys, out = refs[:n], refs[n : 2 * n], refs[2 * n]
    d = out.shape[1]
    for c in range(d // 512):
        cols = pl.ds(c * 512, 512)
        out[:, cols] = sum(tn(x[...], y[:, cols]) for x, y in zip(xs, ys)).astype(BF)


def weight_grad(slots, xs, ys, tile=256):
    n = len(ys)
    rows, d = ys[0].shape
    if len(xs) == n and n > 1 or xs[0].shape[0] == rows:
        specs = [pl.BlockSpec((rows, tile), lambda j, slots: (0, j)) for _ in xs]
    else:
        specs = [
            pl.BlockSpec((rows, tile), functools.partial(lambda s, j, slots: (slots[s], j), s))
            for s in range(n)
        ]
        xs = list(xs) * n
    width = xs[0].shape[1]
    return pl.pallas_call(
        functools.partial(weight_kernel, n),
        grid_spec=pltpu.PrefetchScalarGridSpec(
            num_scalar_prefetch=1,
            grid=(width // tile,),
            in_specs=specs + [whole(y.shape) for y in ys],
            out_specs=pl.BlockSpec((tile, d), lambda j, slots: (j, 0)),
        ),
        out_shape=struct((width, d), BF),
        compiler_params=params(),
        cost_estimate=cost(2 * n * rows * d * width, 2 * (n * rows * (d + width) + d * width)),
        name="weight_grad",
    )(slots, *xs, *ys)


def layout(lengths, group_rows):
    seg_ends = jnp.cumsum(lengths)
    positions = jnp.arange(group_rows, dtype=jnp.int32)
    closed = seg_ends[None, :] <= positions[:, None]
    segment = jnp.sum(closed.astype(jnp.int32), axis=1)
    seg_start = jnp.sum(jnp.where(closed, lengths[None, :], 0), axis=1)
    return segment, positions - seg_start


def tables(lengths, group_rows):
    half = ROT // 2
    segment, offset = layout(lengths, group_rows)
    inv_freq = jnp.power(rope_base, -2.0 * jnp.arange(half, dtype=F32) / ROT)
    angles = offset.astype(F32)[:, None] * inv_freq[None, :]
    cos, sin = jnp.cos(angles), jnp.sin(angles)
    ones = jnp.ones((group_rows, HEAD - ROT), F32)
    none = jnp.zeros_like(ones)
    flat = jnp.zeros_like(sin)
    double = lambda parts: jnp.concatenate(parts + parts, axis=1)
    lane = jnp.arange(LANES)[None, :] - HEAD
    same = segment[:, None] == lane
    hot = jnp.where(same, 1.0, 0.0).astype(BF)
    neg = jnp.where(same | (lane < 0) | (lane >= lengths.shape[0]), 0.0, excluded).astype(BF)
    return double([cos, cos, ones]), double([-sin, flat, none]), double([flat, sin, none]), hot, neg


def on_device(hidden_in, seq_lengths, ln_scale, ln_bias, wqkv, wout, win, wdown, out_grad):
    rows, d = hidden_in.shape
    n = lax.axis_size("mp")
    me = lax.axis_index("mp")
    total = rows * n
    heads = wout.shape[0] // HEAD
    f = win.shape[1]
    cos, fwd, back, hot, neg = tables(seq_lengths[0], total)

    residual = hidden_in.astype(F32)
    row_mean = jnp.mean(residual, axis=1, keepdims=True)
    centred = residual - row_mean
    row_var = jnp.mean(centred * centred, axis=1, keepdims=True)
    inv_std = lax.rsqrt(row_var + epsilon)
    unit = centred * inv_std
    normed = (unit * ln_scale + ln_bias).astype(BF)

    ring = lambda s: [((i + s) % n, i) for i in range(n)]
    nrm = [normed] + [lax.ppermute(normed, "mp", ring(s)) for s in range(1, n)]
    dys = [out_grad] + [lax.ppermute(out_grad, "mp", ring(s)) for s in range(1, n)]
    slots = jnp.stack([(me + s) % n for s in range(n)]).astype(jnp.int32)
    pos = [(slots[s : s + 1] * (rows // TILE)).astype(jnp.int32) for s in range(n)]

    qkv, do = [], []
    acts, gpres, act_sq = [], [], 0.0
    slopes = []
    for s in range(n):
        *qkv, a, sl, sq = project(pos[s], total, heads, qkv, nrm[s], wqkv, win, cos, fwd, back, hot, neg)
        acts.append(a)
        slopes.append(sl)
        act_sq = act_sq + jnp.sum(sq)
    context, wide, keep, ctx_sq = attend(*qkv)
    for s in range(n):
        *do, g = cotangent(pos[s], total, heads, do, dys[s], wout, wdown, slopes[s])
        gpres.append(g)
    update = None
    others = [
        lax.ppermute(pair_matmul(pos[s], False, context, wout, acts[s], wdown), "mp", ring(n - s))
        for s in range(1, n)
    ]
    update = pair_matmul(pos[0], False, context, wout, acts[0], wdown).astype(F32)
    for o in others:
        update = update + o.astype(F32)
    gdown = weight_grad(slots, acts, dys)
    gin = weight_grad(slots, gpres, nrm)
    gdown, gin = lax.psum((gdown, gin), "dp")
    gqkv = attend_back(*qkv, do[0], wide, keep, cos, fwd, back)
    backs = [
        lax.ppermute(pair_matmul(pos[s], True, gqkv, wqkv, gpres[s], win), "mp", ring(n - s))
        for s in range(1, n)
    ]
    grad_normed = pair_matmul(pos[0], True, gqkv, wqkv, gpres[0], win).astype(F32)
    gqw = weight_grad(slots, [gqkv], nrm)
    gow = weight_grad(slots, [context], dys)
    gqw, gow = lax.psum((gqw, gow), "dp")
    for o in backs:
        grad_normed = grad_normed + o.astype(F32)

    result = residual + update
    grad_unit = grad_normed * ln_scale
    grad_hidden = out_grad.astype(F32) + inv_std * (
        grad_unit
        - jnp.mean(grad_unit, axis=1, keepdims=True)
        - unit * jnp.mean(grad_unit * unit, axis=1, keepdims=True)
    )
    devices = lax.axis_size("dp") * n
    sums = lax.psum(
        (
            jnp.sum(grad_normed * unit, axis=0),
            jnp.sum(grad_normed, axis=0),
            jnp.stack([jnp.sum(result * result), jnp.sum(ctx_sq), act_sq]),
        ),
        ("dp", "mp"),
    )
    counts = jnp.array([rows * d * devices, rows * d * devices, rows * f * n * devices], F32)
    return (
        result.astype(BF),
        grad_hidden,
        sums[0],
        sums[1],
        gqw.T.astype(F32),
        gow.astype(F32),
        gin.T.astype(F32),
        gdown.astype(F32),
        jnp.sqrt(sums[2] / counts),
    )


def solution(mesh):
    tok = P(("dp", "mp"), None)
    cols, rows = P(None, "mp"), P("mp", None)
    return jax.shard_map(
        on_device,
        mesh=mesh,
        in_specs=(tok, P("dp", None), P(), P(), cols, rows, cols, rows, tok),
        out_specs=(tok, tok, P(), P(), cols, rows, cols, rows, P()),
        check_vma=False,
    )
```

```python
import functools

import jax
import jax.numpy as jnp
from jax import lax
from jax.experimental import pallas as pl
from jax.experimental.pallas import tpu as pltpu
from jax.sharding import PartitionSpec as P

HEAD = 64
ROT = 16
LANES = 128
TILE = 256
F32 = jnp.float32
BF = jnp.bfloat16

epsilon = 1e-05
rope_base = 10000.0
excluded = -1e20


def nn(a, b):
    return jnp.dot(a, b, preferred_element_type=F32)


def nt(a, b):
    return lax.dot_general(a, b, (((1,), (1,)), ((), ())), preferred_element_type=F32)


def tn(a, b):
    return lax.dot_general(a, b, (((0,), (0,)), ((), ())), preferred_element_type=F32)


def whole(shape):
    zeros = (0,) * len(shape)
    return pl.BlockSpec(shape, lambda *_: zeros, pipeline_mode=pl.Buffered(1))


def struct(shape, dtype):
    return jax.ShapeDtypeStruct(shape, dtype)


def cost(flops, nbytes, trans=0):
    return pl.CostEstimate(flops=int(flops), bytes_accessed=int(nbytes), transcendentals=int(trans))


def params(**kw):
    return pltpu.CompilerParams(vmem_limit_bytes=60 * 2**20, **kw)


def lane_ids(rows):
    return lax.broadcasted_iota(jnp.int32, (rows, LANES), 1)


def turn(x, cos, fwd, back):
    return x * cos + pltpu.roll(x, LANES - ROT // 2, 1) * fwd + pltpu.roll(x, ROT // 2, 1) * back


def gelu_parts(v):
    x = jnp.abs(v)
    bell = jnp.exp(v * v * (-0.5))
    t = 1.0 / (1.0 + x * (0.3275911 * 0.7071067811865476))
    poly = t * (
        0.254829592
        + t * (-0.284496736 + t * (1.421413741 + t * (-1.453152027 + t * 1.061405429)))
    )
    tail = 0.5 * poly * bell
    cdf = jnp.where(v >= 0, 1.0 - tail, tail)
    return v * cdf, cdf + v * bell * 0.3989422804014327


def project_kernel(pairs, slot, nrm, wqkv, win, cos, fwd, back, hot, neg, *rest):
    q_out, k_out, v_out, act, slope, sq = rest[-6:]
    j = pl.program_id(0)
    rows = nrm.shape[0]
    chunk = min(TILE, rows)

    @pl.when(j == 0)
    def _():
        sq[...] = jnp.zeros_like(sq)

    @pl.when(j < pairs)
    def _():
        lane = lane_ids(chunk)
        low = lane < HEAD
        one = jnp.where(lane < HEAD + 2, 1.0, 0.0)
        for i in range(rows // chunk):
            r = pl.ds(i * chunk, chunk)
            y = nn(nrm[r, :], wqkv[...])
            g0, g1, g2 = y[:, :128], y[:, 128:256], y[:, 256:]
            r1, r2 = pltpu.roll(g1, HEAD, 1), pltpu.roll(g2, HEAD, 1)
            for h, (qk, v) in enumerate(((g0, g1), (jnp.where(low, r1, r2), r2))):
                qk = turn(qk, cos[r, :], fwd[r, :], back[r, :])
                q_out[h, r, :] = jnp.where(low, qk * HEAD**-0.5, hot[r, :].astype(F32)).astype(BF)
                k_out[h, r, :] = jnp.where(low, pltpu.roll(qk, HEAD, 1), neg[r, :].astype(F32)).astype(BF)
                v_out[h, r, :] = jnp.where(low, v, one).astype(BF)

    @pl.when(j >= pairs)
    def _():
        for i in range(rows // chunk):
            r = pl.ds(i * chunk, chunk)
            a, sl = gelu_parts(nn(nrm[r, :], win[...]))
            a = a.astype(BF)
            act[r, :] = a
            slope[r, :] = sl.astype(BF)
            wide = a.astype(F32)
            sq[...] += jnp.sum((wide * wide).reshape(chunk // 8, 8, -1), axis=0)


def project(slot, total, heads, prior, nrm, wqkv, win, cos, fwd, back, hot, neg):
    rows, d = nrm.shape
    f = win.shape[1]
    pairs = heads // 2
    tile = min(512, f)
    lead = lambda j: jnp.minimum(j, pairs - 1)
    late = lambda j: jnp.maximum(j - pairs, 0)
    at = pl.BlockSpec((rows, LANES), lambda j, slot: (slot[0], 0), pipeline_mode=pl.Buffered(1))
    hd = pl.BlockSpec((2, rows, LANES), lambda j, slot: (lead(j), slot[0], 0))
    ff = pl.BlockSpec((rows, tile), lambda j, slot: (0, late(j)))
    big = struct((heads, total, LANES), BF)
    return pl.pallas_call(
        functools.partial(project_kernel, pairs),
        grid_spec=pltpu.PrefetchScalarGridSpec(
            num_scalar_prefetch=1,
            grid=(pairs + f // tile,),
            in_specs=[
                whole(nrm.shape),
                pl.BlockSpec((d, 384), lambda j, slot: (0, lead(j))),
                pl.BlockSpec((d, tile), lambda j, slot: (0, late(j))),
                at, at, at, at, at,
            ]
            + [pl.BlockSpec(memory_space=pl.ANY)] * len(prior),
            out_specs=[hd, hd, hd, ff, ff, pl.BlockSpec((8, tile), lambda j, slot: (0, 0))],
        ),
        out_shape=[big, big, big, struct((rows, f), BF), struct((rows, f), BF), struct((8, tile), F32)],
        input_output_aliases={9 + i: i for i in range(len(prior))},
        compiler_params=params(),
        cost_estimate=cost(2 * rows * d * (f + wqkv.shape[1]), 2 * (d * (f + wqkv.shape[1]) + 6 * rows * d)),
        name="project",
    )(slot, nrm, wqkv, win, cos, fwd, back, hot, neg, *prior)


def cotangent_kernel(slot, dy, wout, wdown, slope, *rest):
    do_out, gpre = rest[-2:]
    j = pl.program_id(0)
    rows = dy.shape[0]
    chunk = min(512, rows)

    @pl.when(j == 0)
    def _():
        low = lane_ids(chunk) < HEAD
        for i in range(rows // chunk):
            r = pl.ds(i * chunk, chunk)
            g = nt(dy[r, :], wout[...])
            for p in range(g.shape[1] // LANES):
                y = g[:, p * LANES : (p + 1) * LANES]
                do_out[2 * p, r, :] = jnp.where(low, y, 0.0).astype(BF)
                do_out[2 * p + 1, r, :] = jnp.where(low, pltpu.roll(y, HEAD, 1), 0.0).astype(BF)

    @pl.when(j > 0)
    def _():
        for i in range(rows // chunk):
            r = pl.ds(i * chunk, chunk)
            gpre[r, :] = (nt(dy[r, :], wdown[...]) * slope[r, :].astype(F32)).astype(BF)


def cotangent(slot, total, heads, prior, dy, wout, wdown, slope):
    rows, d = dy.shape
    f = wdown.shape[0]
    tile = min(512, f)
    late = lambda j: jnp.maximum(j - 1, 0)
    ff = pl.BlockSpec((rows, tile), lambda j, slot: (0, late(j)))
    return pl.pallas_call(
        cotangent_kernel,
        grid_spec=pltpu.PrefetchScalarGridSpec(
            num_scalar_prefetch=1,
            grid=(1 + f // tile,),
            in_specs=[whole(dy.shape), whole(wout.shape), pl.BlockSpec((tile, d), lambda j, slot: (late(j), 0)), ff]
            + [pl.BlockSpec(memory_space=pl.ANY)] * len(prior),
            out_specs=[pl.BlockSpec((heads, rows, LANES), lambda j, slot: (0, slot[0], 0)), ff],
        ),
        out_shape=[struct((heads, total, LANES), BF), struct((rows, f), BF)],
        input_output_aliases={5 + i: i for i in range(len(prior))},
        compiler_params=params(),
        cost_estimate=cost(2 * rows * d * (f + wout.shape[0]), 2 * (d * (f + wout.shape[0]) + 5 * rows * d)),
        name="cotangent",
    )(slot, dy, wout, wdown, slope, *prior)


def attend_kernel(q_ref, k_ref, v_ref, ctx, wide, keep, sq):
    h = pl.program_id(1)
    total = q_ref.shape[1]
    b = TILE
    tri = lax.broadcasted_iota(jnp.int32, (b, b), 0) >= lax.broadcasted_iota(jnp.int32, (b, b), 1)
    low = lane_ids(b) < HEAD

    @pl.when((h == 0) & (pl.program_id(0) == 0))
    def _():
        sq[...] = jnp.zeros_like(sq)

    for i in range(total // b):
        n = (i + 1) * b
        rows = pl.ds(i * b, b)
        s = nt(q_ref[0, rows, :], k_ref[0, :n, :])
        s_diag = jnp.where(tri, s[:, n - b :], excluded)
        top = jnp.max(s_diag, axis=1, keepdims=True)
        if i:
            top = jnp.maximum(top, jnp.max(s[:, : n - b], axis=1, keepdims=True))
        w = jnp.exp(s_diag - top).astype(BF)
        if i:
            w = jnp.concatenate([jnp.exp(s[:, : n - b] - top).astype(BF), w], axis=1)
        for j in range(i + 1):
            keep[0, i * (i + 1) // 2 + j] = w[:, j * b : (j + 1) * b]
        acc = nn(w, v_ref[0, :n, :])
        inv = 1.0 / acc[:, HEAD : HEAD + 1]
        acc = acc * inv
        wide[0, rows, :] = jnp.where(low, acc, inv)
        out = acc.astype(BF)
        real = jnp.where(low, out.astype(F32), 0.0)
        sq[...] += jnp.sum((real * real).reshape(b // 8, 8, LANES), axis=0)

        @pl.when(h == 0)
        def _():
            ctx[rows, :] = out

        @pl.when(h == 1)
        def _():
            both = jnp.where(low, ctx[rows, :].astype(F32), pltpu.roll(out.astype(F32), HEAD, 1))
            ctx[rows, :] = both.astype(BF)


def attend(q, k, v):
    heads, total, _ = q.shape
    tiles = total // TILE
    tiles = tiles * (tiles + 1) // 2
    hd = pl.BlockSpec((1, total, LANES), lambda p, h: (2 * p + h, 0, 0))
    return pl.pallas_call(
        attend_kernel,
        grid=(heads // 2, 2),
        in_specs=[hd, hd, hd],
        out_specs=[
            pl.BlockSpec((total, LANES), lambda p, h: (0, p)),
            hd,
            pl.BlockSpec((1, tiles, TILE, TILE), lambda p, h: (2 * p + h, 0, 0, 0)),
            pl.BlockSpec((8, LANES), lambda p, h: (0, 0)),
        ],
        out_shape=[
            struct((total, heads * HEAD), BF),
            struct((heads, total, LANES), F32),
            struct((heads, tiles, TILE, TILE), BF),
            struct((8, LANES), F32),
        ],
        compiler_params=params(),
        cost_estimate=cost(4 * heads * tiles * TILE * TILE * 256, heads * total * LANES * 20, heads * tiles * TILE * TILE),
        name="attend",
    )(q, k, v)


def attend_back_kernel(q_ref, k_ref, v_ref, do_ref, wide, keep, cos, fwd, back, out, dk_acc, dv_acc, dq_acc, hold):
    h = pl.program_id(1)
    total = q_ref.shape[1]
    b = TILE
    lane = lane_ids(b)
    low = lane < HEAD
    dk_acc[...] = jnp.zeros_like(dk_acc)
    dv_acc[...] = jnp.zeros_like(dv_acc)
    for i in range(total // b):
        n = (i + 1) * b
        rows = pl.ds(i * b, b)
        q = q_ref[0, rows, :]
        w = [keep[0, i * (i + 1) // 2 + j] for j in range(i + 1)]
        w = w[0] if i == 0 else jnp.concatenate(w, axis=1)
        context = wide[0, rows, :]
        inv = context[:, HEAD : HEAD + 1]
        scaled = (do_ref[0, rows, :].astype(F32) * inv).astype(BF)
        grad = scaled.astype(F32)
        delta = jnp.sum(jnp.where(low, grad * context, 0.0), axis=1, keepdims=True)
        delta_hi = delta.astype(BF).astype(F32)
        delta_lo = delta - delta_hi
        joined = jnp.where(lane == HEAD, -delta_hi, jnp.where(lane == HEAD + 1, -delta_lo, grad)).astype(BF)
        ds = w * nt(joined, v_ref[0, :n, :]).astype(BF)
        dq_acc[rows, :] = nn(ds, k_ref[0, :n, :]) * HEAD**-0.5
        dk_acc[:n, :] += tn(ds, q)
        dv_acc[:n, :] += tn(w, scaled)
    for i in range(total // b):
        rows = pl.ds(i * b, b)
        x = jnp.where(low, dq_acc[rows, :], pltpu.roll(dk_acc[rows, :], HEAD, 1))
        x = turn(x, cos[rows, :], -fwd[rows, :], -back[rows, :])
        dv = dv_acc[rows, :]

        @pl.when(h == 0)
        def _():
            out[rows, :LANES] = x.astype(BF)
            hold[rows, :] = dv

        @pl.when(h == 1)
        def _():
            r = pltpu.roll(x, HEAD, 1)
            out[rows, LANES : 2 * LANES] = jnp.where(low, hold[rows, :], r).astype(BF)
            out[rows, 2 * LANES :] = jnp.where(low, r, pltpu.roll(dv, HEAD, 1)).astype(BF)


def attend_back(q, k, v, do, wide, keep, cos, fwd, back):
    heads, total, _ = q.shape
    hd = pl.BlockSpec((1, total, LANES), lambda p, h: (2 * p + h, 0, 0))
    acc = pltpu.VMEM((total, LANES), F32)
    tiles = keep.shape[1]
    return pl.pallas_call(
        attend_back_kernel,
        grid=(heads // 2, 2),
        in_specs=[hd, hd, hd, hd, hd, pl.BlockSpec((1,) + keep.shape[1:], lambda p, h: (2 * p + h, 0, 0, 0))]
        + [whole(cos.shape)] * 3,
        out_specs=pl.BlockSpec((total, 384), lambda p, h: (0, p)),
        out_shape=struct((total, heads * 3 * HEAD), BF),
        scratch_shapes=[acc] * 4,
        compiler_params=params(),
        cost_estimate=cost(8 * heads * tiles * TILE * TILE * 256, heads * total * LANES * 40),
        name="attend_back",
    )(q, k, v, do, wide, keep, cos, fwd, back)


def pair_kernel(transposed, pos, a, b, c, d, out):
    dot = nt if transposed else nn
    out[...] = (dot(a[...], b[...]) + dot(c[...], d[...])).astype(BF)


def pair_matmul(slot, transposed, a, b, c, d):
    rows = c.shape[0]
    width = b.shape[0] if transposed else b.shape[1]
    tile = 256
    if transposed:
        weight = lambda w: pl.BlockSpec((tile, w.shape[1]), lambda j, slot: (j, 0))
    else:
        weight = lambda w: pl.BlockSpec((w.shape[0], tile), lambda j, slot: (0, j))
    return pl.pallas_call(
        functools.partial(pair_kernel, transposed),
        grid_spec=pltpu.PrefetchScalarGridSpec(
            num_scalar_prefetch=1,
            grid=(width // tile,),
            in_specs=[
                pl.BlockSpec((rows, a.shape[1]), lambda j, slot: (slot[0], 0), pipeline_mode=pl.Buffered(1)),
                weight(b),
                whole(c.shape),
                weight(d),
            ],
            out_specs=pl.BlockSpec((rows, tile), lambda j, slot: (0, j)),
        ),
        out_shape=struct((rows, width), BF),
        compiler_params=params(),
        cost_estimate=cost(2 * rows * width * (a.shape[1] + c.shape[1]), 2 * (b.size + d.size + rows * (width + a.shape[1] + c.shape[1]))),
        name="pair_matmul",
    )(slot, a, b, c, d)


def weight_kernel(n, slots, *refs):
    xs, ys, out = refs[:n], refs[n : 2 * n], refs[2 * n]
    width = out.shape[1]
    step = 512 if width % 512 == 0 else 128
    for c in range(width // step):
        cols = pl.ds(c * step, step)
        out[:, cols] = sum(tn(x[...], y[:, cols]) for x, y in zip(xs, ys)).astype(BF)


def weight_grad(slots, xs, ys, rows):
    n = max(len(xs), len(ys))
    tile = min(256, xs[0].shape[1])
    width = ys[0].shape[1]
    by = lambda s, one, shape, index: pl.BlockSpec(
        shape, (lambda j, slots: (slots[s], index(j))) if one else (lambda j, slots: (0, index(j))),
        **({} if shape[1] == tile else {"pipeline_mode": pl.Buffered(1)})
    )
    specs = [by(s, len(xs) < n, (rows, tile), lambda j: j) for s in range(n)]
    specs += [by(s, len(ys) < n, (rows, width), lambda j: 0) for s in range(n)]
    xs = list(xs) * (n // len(xs))
    ys = list(ys) * (n // len(ys))
    depth = xs[0].shape[1]
    return pl.pallas_call(
        functools.partial(weight_kernel, n),
        grid_spec=pltpu.PrefetchScalarGridSpec(
            num_scalar_prefetch=1,
            grid=(depth // tile,),
            in_specs=specs,
            out_specs=pl.BlockSpec((tile, width), lambda j, slots: (j, 0)),
        ),
        out_shape=struct((depth, width), BF),
        compiler_params=params(),
        cost_estimate=cost(2 * n * rows * depth * width, 2 * (n * rows * (depth + width) + depth * width)),
        name="weight_grad",
    )(slots, *xs, *ys)


def ring_kernel(chips, parts, x, out, near, part, far, core_sem, rs_send, rs_recv, ag_send, ag_recv, fin_send, fin_recv):
    dp = lax.axis_index("dp")
    core, chip = lax.rem(dp, 2), dp // 2
    y, z = lax.rem(chip, 2), chip // 2
    p = z * (1 - y) + (chips - 1 - z) * y

    def device(pos):
        high = pos // (chips // 2)
        return ((1 - high) * 2 * pos + high * (2 * (chips - 1 - pos) + 1)) * 2 + core

    peer = dp + 1 - 2 * core
    ends = [device(lax.rem(p + 1, chips)), device(lax.rem(p + chips - 1, chips))]
    barrier = pltpu.get_barrier_semaphore()
    for t in (*ends, peer):
        pl.semaphore_signal(barrier, inc=1, device_id={"dp": t}, device_id_type=pl.DeviceIdType.MESH)
    pl.semaphore_wait(barrier, 3)

    def remote(src, dst, send, recv, t):
        return pltpu.make_async_remote_copy(
            src_ref=src, dst_ref=dst, send_sem=send, recv_sem=recv,
            device_id={"dp": t}, device_id_type=pl.DeviceIdType.MESH,
        )

    def chunk(s, d):
        return lax.rem(p + 2 * chips - s, chips) if d % 2 == 0 else lax.rem(p + s, chips)

    def add(a, b):
        return (a.astype(F32) + b.astype(F32)).astype(BF)

    swaps = [remote(x.at[1 - core, c], near.at[c], core_sem.at[0, c], core_sem.at[1, c], peer) for c in range(chips)]
    for c in swaps:
        c.start()
    for c in range(chips):
        swaps[c].wait_recv()
        part[c] = add(x[core, c], near[c])

    def reduce(s, d):
        return remote(part.at[chunk(s, d), d], far.at[s, d], rs_send.at[s, d], rs_recv.at[s, d], ends[d % 2])

    def gather(s, d):
        c = chunk(chips - 1 + s, d)
        return remote(out.at[core, c, d], out.at[core, c, d], ag_send.at[s, d], ag_recv.at[s, d], ends[d % 2])

    def across(s, d, half):
        c = chunk(chips - 1 + s, d)
        return remote(out.at[core, c, d], out.at[half, c, d], fin_send.at[s, d], fin_recv.at[s, d], peer)

    for s in range(chips - 1):
        for d in range(parts):
            if s:
                reduce(s - 1, d).wait_recv()
                c = chunk(s, d)
                part[c, d] = add(part[c, d], far[s - 1, d])
            reduce(s, d).start()
    for s in range(chips):
        for d in range(parts):
            if s == 0:
                reduce(chips - 2, d).wait_recv()
                c = chunk(chips - 1, d)
                out[core, c, d] = add(part[c, d], far[chips - 2, d])
            else:
                gather(s - 1, d).wait_recv()
            if s < chips - 1:
                gather(s, d).start()
            across(s, d, core).start()
    for c in swaps:
        c.wait_send()
    for d in range(parts):
        for s in range(chips - 1):
            reduce(s, d).wait_send()
            gather(s, d).wait_send()
        for s in range(chips):
            across(s, d, core).wait_send()
            across(s, d, 1 - core).wait_recv()


def ring_sum(x, collective_id):
    chips = lax.axis_size("dp") // 2
    rows, d = x.shape
    parts = min(8, rows // (32 * chips))
    cut = x.reshape(2, chips, parts, rows // (2 * chips * parts), d)
    dma = pltpu.SemaphoreType.DMA
    vmem = pl.BlockSpec(memory_space=pltpu.VMEM)
    total = pl.pallas_call(
        functools.partial(ring_kernel, chips, parts),
        out_shape=struct(cut.shape, BF),
        in_specs=[vmem],
        out_specs=vmem,
        scratch_shapes=[pltpu.VMEM(cut.shape[1:], BF), pltpu.VMEM(cut.shape[1:], BF), pltpu.VMEM((chips - 1,) + cut.shape[2:], BF)]
        + [dma((2, chips))] + [dma((chips - 1, parts))] * 4 + [dma((chips, parts))] * 2,
        compiler_params=params(collective_id=collective_id, has_side_effects=True),
        cost_estimate=cost(0, 4 * x.size),
        name="ring_sum",
    )(cut)
    return total.reshape(rows, d)


def small_kernel(n_dp, n_mp, x, out, held, send, recv):
    me = lax.axis_index("dp") * n_mp + lax.axis_index("mp")
    count = n_dp * n_mp
    barrier = pltpu.get_barrier_semaphore()

    def target(k):
        t = lax.rem(me + k, count)
        return dict(device_id={"dp": t // n_mp, "mp": lax.rem(t, n_mp)}, device_id_type=pl.DeviceIdType.MESH)

    def greet(k, carry):
        pl.semaphore_signal(barrier, inc=1, **target(k))
        return carry

    lax.fori_loop(1, count, greet, 0)
    pl.semaphore_wait(barrier, count - 1)

    def copy(k):
        return pltpu.make_async_remote_copy(
            src_ref=x, dst_ref=held.at[me], send_sem=send.at[k], recv_sem=recv.at[k], **target(k)
        )

    def begin(k, carry):
        copy(k).start()
        return carry

    lax.fori_loop(1, count, begin, 0)
    held[me] = x[...]

    def end(k, carry):
        copy(k).wait()
        return carry

    lax.fori_loop(1, count, end, 0)
    out[...] = lax.fori_loop(0, count, lambda k, total: total + held[k], jnp.zeros(x.shape, F32))


def small_sum(x, collective_id):
    n_dp, n_mp = lax.axis_size("dp"), lax.axis_size("mp")
    dma = pltpu.SemaphoreType.DMA
    vmem = pl.BlockSpec(memory_space=pltpu.VMEM)
    return pl.pallas_call(
        functools.partial(small_kernel, n_dp, n_mp),
        out_shape=struct(x.shape, F32),
        in_specs=[vmem],
        out_specs=vmem,
        scratch_shapes=[pltpu.VMEM((n_dp * n_mp,) + x.shape, F32), dma((n_dp * n_mp,)), dma((n_dp * n_mp,))],
        compiler_params=params(collective_id=collective_id, has_side_effects=True),
        name="small_sum",
    )(x)


def norm_kernel(x_ref, scale, bias, out):
    x = x_ref[...].astype(F32)
    mean = jnp.mean(x, axis=1, keepdims=True)
    centred = x - mean
    var = jnp.mean(centred * centred, axis=1, keepdims=True)
    out[...] = (centred * lax.rsqrt(var + epsilon) * scale[...] + bias[...]).astype(BF)


def norm(x, scale, bias):
    rows, d = x.shape
    tile = pl.BlockSpec((min(TILE, rows), d), lambda i: (i, 0))
    return pl.pallas_call(
        norm_kernel,
        grid=(rows // min(TILE, rows),),
        in_specs=[tile, whole((1, d)), whole((1, d))],
        out_specs=tile,
        out_shape=struct((rows, d), BF),
        compiler_params=params(),
        cost_estimate=cost(10 * rows * d, 4 * rows * d),
        name="norm",
    )(x, scale, bias)


def output_kernel(n, x_ref, *refs):
    parts, out, sq = refs[:n], refs[n], refs[n + 1]

    @pl.when(pl.program_id(0) == 0)
    def _():
        sq[...] = jnp.zeros_like(sq)

    y = x_ref[...].astype(F32) + sum(p[...].astype(F32) for p in parts)
    out[...] = y.astype(BF)
    sq[...] += jnp.sum((y * y).reshape(y.shape[0] // 8, 8, -1), axis=0)


def output(x, parts):
    rows, d = x.shape
    tile = pl.BlockSpec((min(TILE, rows), d), lambda i: (i, 0))
    return pl.pallas_call(
        functools.partial(output_kernel, len(parts)),
        grid=(rows // min(TILE, rows),),
        in_specs=[tile] * (1 + len(parts)),
        out_specs=[tile, pl.BlockSpec((8, d), lambda i: (0, 0))],
        out_shape=[struct((rows, d), BF), struct((8, d), F32)],
        compiler_params=params(),
        cost_estimate=cost(4 * rows * d, 8 * rows * d),
        name="output",
    )(x, *parts)


def norm_back_kernel(n, x_ref, dy, scale, *refs):
    parts, out, gain, bias = refs[:n], refs[n], refs[n + 1], refs[n + 2]

    @pl.when(pl.program_id(0) == 0)
    def _():
        gain[...] = jnp.zeros_like(gain)
        bias[...] = jnp.zeros_like(bias)

    x = x_ref[...].astype(F32)
    mean = jnp.mean(x, axis=1, keepdims=True)
    centred = x - mean
    var = jnp.mean(centred * centred, axis=1, keepdims=True)
    inv = lax.rsqrt(var + epsilon)
    unit = centred * inv
    grad = sum(p[...].astype(F32) for p in parts)
    g = grad * scale[...]
    out[...] = dy[...].astype(F32) + inv * (
        g - jnp.mean(g, axis=1, keepdims=True) - unit * jnp.mean(g * unit, axis=1, keepdims=True)
    )
    fold = lambda v: jnp.sum(v.reshape(v.shape[0] // 8, 8, -1), axis=0)
    gain[...] += fold(grad * unit)
    bias[...] += fold(grad)


def norm_back(x, dy, scale, parts):
    rows, d = x.shape
    tile = pl.BlockSpec((min(TILE, rows), d), lambda i: (i, 0))
    acc = pl.BlockSpec((8, d), lambda i: (0, 0))
    return pl.pallas_call(
        functools.partial(norm_back_kernel, len(parts)),
        grid=(rows // min(TILE, rows),),
        in_specs=[tile, tile, whole((1, d))] + [tile] * len(parts),
        out_specs=[tile, acc, acc],
        out_shape=[struct((rows, d), F32), struct((8, d), F32), struct((8, d), F32)],
        compiler_params=params(),
        cost_estimate=cost(20 * rows * d, 12 * rows * d),
        name="norm_back",
    )(x, dy, scale, *parts)


def layout(lengths, group_rows):
    seg_ends = jnp.cumsum(lengths)
    positions = jnp.arange(group_rows, dtype=jnp.int32)
    closed = seg_ends[None, :] <= positions[:, None]
    segment = jnp.sum(closed.astype(jnp.int32), axis=1)
    seg_start = jnp.sum(jnp.where(closed, lengths[None, :], 0), axis=1)
    return segment, positions - seg_start


def table_kernel(ends_ref, lens_ref, freq, cos, fwd, back, hot, neg):
    rows = cos.shape[0]
    lane = lane_ids(rows)
    where = lax.broadcasted_iota(jnp.int32, (rows, LANES), 0) + pl.program_id(0) * rows
    segment = jnp.zeros((rows, LANES), jnp.int32)
    start = jnp.zeros((rows, LANES), jnp.int32)
    for j in range(ends_ref.shape[0]):
        closed = where >= ends_ref[j]
        segment = segment + closed.astype(jnp.int32)
        start = start + jnp.where(closed, lens_ref[j], 0)
    angle = (where - start).astype(F32) * freq[...]
    dim = lax.rem(lane, HEAD)
    sin = jnp.sin(angle)
    cos[...] = jnp.where(dim < ROT, jnp.cos(angle), 1.0)
    fwd[...] = jnp.where(dim < ROT // 2, -sin, 0.0)
    back[...] = jnp.where((dim >= ROT // 2) & (dim < ROT), sin, 0.0)
    same = lane - HEAD == segment
    hot[...] = jnp.where(same, 1.0, 0.0).astype(BF)
    neg[...] = jnp.where(same | (lane < HEAD) | (lane >= HEAD + ends_ref.shape[0]), 0.0, excluded).astype(BF)


def tables(lengths, group_rows):
    half = ROT // 2
    freq = jnp.power(rope_base, -2.0 * jnp.arange(half, dtype=F32) / ROT)
    freq = jnp.pad(jnp.tile(freq, 2), (0, HEAD - ROT))
    freq = jnp.tile(freq, LANES // HEAD)[None, :]
    block = pl.BlockSpec((TILE, LANES), lambda i, *_: (i, 0))
    return pl.pallas_call(
        table_kernel,
        grid_spec=pltpu.PrefetchScalarGridSpec(
            num_scalar_prefetch=2,
            grid=(group_rows // TILE,),
            in_specs=[whole((1, LANES))],
            out_specs=[block] * 5,
        ),
        out_shape=[struct((group_rows, LANES), F32)] * 3 + [struct((group_rows, LANES), BF)] * 2,
        compiler_params=params(),
        name="tables",
    )(jnp.cumsum(lengths).astype(jnp.int32), lengths, freq)


def on_device(hidden_in, seq_lengths, ln_scale, ln_bias, wqkv, wout, win, wdown, out_grad):
    rows, d = hidden_in.shape
    n = lax.axis_size("mp")
    me = lax.axis_index("mp")
    total = rows * n
    heads = wout.shape[0] // HEAD
    f = win.shape[1]
    after = lambda x, *deps: lax.optimization_barrier((x, *deps))[0]

    normed = norm(hidden_in, ln_scale[None, :], ln_bias[None, :])
    ring = lambda s: [((i + s) % n, i) for i in range(n)]
    nrm = [normed] + [lax.ppermute(normed, "mp", ring(s)) for s in range(1, n)]
    early = after(out_grad, *nrm[1:])
    dys = [out_grad] + [lax.ppermute(early, "mp", ring(s)) for s in range(1, n)]
    slots = jnp.stack([(me + s) % n for s in range(n)]).astype(jnp.int32)
    pos = [slots[s : s + 1] for s in range(n)]
    table = tables(seq_lengths[0], total)

    qkv, do = [], []
    acts, slopes, gpres, act_sq = [], [], [], []
    for s in range(n):
        *qkv, a, sl, sq = project(pos[s], total, heads, qkv, nrm[s], wqkv, win, *table)
        acts.append(a)
        slopes.append(sl)
        act_sq.append(sq)
        if s == 0:
            *do, g = cotangent(pos[0], total, heads, do, dys[0], wout, wdown, slopes[0])
            gpres.append(g)
    context, wide, keep, ctx_sq = attend(*qkv)
    others = [
        lax.ppermute(pair_matmul(pos[s], False, context, wout, acts[s], wdown), "mp", ring(n - s))
        for s in range(1, n)
    ]
    for s in range(1, n):
        *do, g = cotangent(pos[s], total, heads, do, dys[s], wout, wdown, slopes[s])
        gpres.append(g)
    gdown = weight_grad(slots, acts, dys, rows)
    gdown = lax.psum(gdown, "dp")
    gin = weight_grad(slots, nrm, gpres, rows)
    gow = weight_grad(slots, [context], dys, rows)
    update = pair_matmul(pos[0], False, context, wout, acts[0], wdown)
    gqkv = attend_back(*qkv, do[0], wide, keep, *table[:3])
    gin, gow = lax.psum((after(gin, gdown), after(gow, gdown)), "dp")
    backs = [
        lax.ppermute(pair_matmul(pos[s], True, gqkv, wqkv, gpres[s], win), "mp", ring(n - s))
        for s in range(1, n)
    ]
    result, res_sq = output(hidden_in, [update] + others)
    gqw = weight_grad(slots, nrm, [gqkv], rows)
    own = pair_matmul(pos[0], True, gqkv, wqkv, gpres[0], win)
    gqw = ring_sum(after(gqw, own), 1)
    grad_hidden, gain, bias = norm_back(hidden_in, out_grad, ln_scale[None, :], [own] + backs)

    stats = jnp.stack([jnp.sum(res_sq), jnp.sum(ctx_sq), sum(jnp.sum(s) for s in act_sq)])
    packed = jnp.concatenate(
        [jnp.sum(gain, axis=0)[None], jnp.sum(bias, axis=0)[None], jnp.pad(stats, (0, d - 3))[None], jnp.zeros((5, d), F32)]
    )
    sums = small_sum(packed, 2)
    devices = lax.axis_size("dp") * n
    counts = jnp.array([rows * d * devices, rows * d * devices, rows * f * n * devices], F32)
    return (
        result,
        grad_hidden,
        sums[0],
        sums[1],
        gqw.astype(F32),
        gow.astype(F32),
        gin.astype(F32),
        gdown.astype(F32),
        jnp.sqrt(sums[2, :3] / counts),
    )


def solution(mesh):
    tok = P(("dp", "mp"), None)
    cols, rows = P(None, "mp"), P("mp", None)
    return jax.shard_map(
        on_device,
        mesh=mesh,
        in_specs=(tok, P("dp", None), P(), P(), cols, rows, cols, rows, tok),
        out_specs=(tok, tok, P(), P(), cols, rows, cols, rows, P()),
        check_vma=False,
    )
```

```python
import functools

import jax
import jax.numpy as jnp
from jax import lax
from jax.experimental import pallas as pl
from jax.experimental.pallas import tpu as pltpu
from jax.sharding import PartitionSpec as P

HEAD = 64
ROT = 16
LANES = 128
TILE = 256
CHUNK = 512
POINTS = 2
F32 = jnp.float32
BF = jnp.bfloat16

epsilon = 1e-05
rope_base = 10000.0
excluded = -1e20


def nn(a, b):
    return jnp.dot(a, b, preferred_element_type=F32)


def nt(a, b):
    return lax.dot_general(a, b, (((1,), (1,)), ((), ())), preferred_element_type=F32)


def tn(a, b):
    return lax.dot_general(a, b, (((0,), (0,)), ((), ())), preferred_element_type=F32)


def whole(shape):
    zeros = (0,) * len(shape)
    return pl.BlockSpec(shape, lambda *_: zeros, pipeline_mode=pl.Buffered(1))


def struct(shape, dtype):
    return jax.ShapeDtypeStruct(shape, dtype)


def cost(flops, nbytes, trans=0):
    return pl.CostEstimate(flops=int(flops), bytes_accessed=int(nbytes), transcendentals=int(trans))


def params(**kw):
    return pltpu.CompilerParams(vmem_limit_bytes=60 * 2**20, **kw)


def lane_ids(rows):
    return lax.broadcasted_iota(jnp.int32, (rows, LANES), 1)


def turn(x, cos, fwd, back):
    return x * cos + pltpu.roll(x, LANES - ROT // 2, 1) * fwd + pltpu.roll(x, ROT // 2, 1) * back


def gelu_parts(v):
    x = jnp.abs(v)
    bell = jnp.exp(v * v * (-0.5))
    base = 1.0 + x * (0.3275911 * 0.7071067811865476)
    t = pl.reciprocal(base, approx=True)
    poly = t * (
        0.254829592
        + t * (-0.284496736 + t * (1.421413741 + t * (-1.453152027 + t * 1.061405429)))
    )
    tail = 0.5 * poly * bell
    cdf = jnp.where(v >= 0, 1.0 - tail, tail)
    return v * cdf, cdf + v * bell * 0.3989422804014327


def ahead(count, product, use):
    held = product(0)
    for i in range(count):
        later = product(i + 1) if i + 1 < count else None
        use(i, held)
        held = later


def project_kernel(slot, nrm, wqkv, cos, fwd, back, hot, neg, *rest):
    q_out, k_out, v_out = rest[-3:]
    rows = nrm.shape[0]
    chunk = min(CHUNK, rows)
    lane = lane_ids(chunk)
    low = lane < HEAD
    one = jnp.where(lane < HEAD + 2, 1.0, 0.0)

    def place(y, r):
        blocks = [y[:, i : i + LANES] for i in range(0, y.shape[1], LANES)]
        sides = []
        for g0, g1, g2 in zip(blocks[::3], blocks[1::3], blocks[2::3]):
            r1, r2 = pltpu.roll(g1, HEAD, 1), pltpu.roll(g2, HEAD, 1)
            sides += [(g0, g1), (jnp.where(low, r1, r2), r2)]
        for h, (qk, v) in enumerate(sides):
            qk = turn(qk, cos[r, :], fwd[r, :], back[r, :])
            q_out[h, r, :] = jnp.where(low, qk * HEAD**-0.5, hot[r, :].astype(F32)).astype(BF)
            k_out[h, r, :] = jnp.where(low, pltpu.roll(qk, HEAD, 1), neg[r, :].astype(F32)).astype(BF)
            v_out[h, r, :] = jnp.where(low, v, one).astype(BF)

    ahead(
        rows // chunk,
        lambda i: nn(nrm[i * chunk : (i + 1) * chunk, :], wqkv[...]),
        lambda i, y: place(y, pl.ds(i * chunk, chunk)),
    )


def project(slot, total, heads, prior, nrm, wqkv, cos, fwd, back, hot, neg):
    rows, d = nrm.shape
    per = 4 if heads % 4 == 0 else 2
    at = pl.BlockSpec((rows, LANES), lambda j, slot: (slot[0], 0), pipeline_mode=pl.Buffered(1))
    hd = pl.BlockSpec((per, rows, LANES), lambda j, slot: (j, slot[0], 0))
    big = struct((heads, total, LANES), BF)
    return pl.pallas_call(
        project_kernel,
        grid_spec=pltpu.PrefetchScalarGridSpec(
            num_scalar_prefetch=1,
            grid=(heads // per,),
            in_specs=[whole(nrm.shape), pl.BlockSpec((d, per * 3 * HEAD), lambda j, slot: (0, j)), at, at, at, at, at]
            + [pl.BlockSpec(memory_space=pl.ANY)] * len(prior),
            out_specs=[hd, hd, hd],
        ),
        out_shape=[big, big, big],
        input_output_aliases={8 + i: i for i in range(len(prior))},
        compiler_params=params(),
        cost_estimate=cost(2 * rows * d * wqkv.shape[1], 2 * (d * wqkv.shape[1] + 6 * rows * d)),
        name="project",
    )(slot, nrm, wqkv, cos, fwd, back, hot, neg, *prior)


def feed_kernel(extra, slot, nrm, dy, win, wdown, wout, *refs):
    prior = refs[:2] if extra else ()
    do_out, update, back, gdown, gin, sq, turned, act, gpre = refs[extra:]
    j = pl.program_id(0)
    rows, d = nrm.shape
    chunk = min(TILE, rows)
    span = [pl.ds(i * chunk, chunk) for i in range(rows // chunk)]

    @pl.when(j == 0)
    def _():
        sq[...] = jnp.zeros_like(sq)
        update[...] = jnp.zeros_like(update)
        back[...] = jnp.zeros_like(back)
        turned[...] = jnp.transpose(nrm[...])
        low = lane_ids(chunk) < HEAD
        for r in span:
            g = nt(dy[r, :], wout[...])
            for p in range(g.shape[1] // LANES):
                y = g[:, p * LANES : (p + 1) * LANES]
                do_out[2 * p, r, :] = jnp.where(low, y, 0.0).astype(BF)
                do_out[2 * p + 1, r, :] = jnp.where(low, pltpu.roll(y, HEAD, 1), 0.0).astype(BF)

    def products(i):
        return nn(nrm[span[i], :], win[...]), nt(dy[span[i], :], wdown[...])

    def use(i, held):
        r = span[i]
        a, slope = gelu_parts(held[0])
        a = a.astype(BF)
        g = (held[1] * slope).astype(BF)
        act[r, :] = a
        gpre[r, :] = g
        wide = a.astype(F32)
        sq[...] += jnp.sum((wide * wide).reshape(chunk // 8, 8, -1), axis=0)
        pass

    ahead(len(span), products, use)
    update[...] += nn(act[...], wdown[...])
    back[...] += nt(gpre[...], win[...])
    down, into = tn(act[...], dy[...]), nn(turned[...], gpre[...])
    if extra:
        down, into = down + prior[0][...].astype(F32), into + prior[1][...].astype(F32)
    gdown[...] = down.astype(BF)
    gin[...] = into.astype(BF)


def feed(slot, piece, pieces, total, heads, prior, nrm, dy, win, wdown, wout):
    rows, d = nrm.shape
    f = win.shape[1]
    tile = min(512, f)
    by_row = pl.BlockSpec((tile, d), lambda j, slot: (j, 0))
    by_col = pl.BlockSpec((d, tile), lambda j, slot: (0, j))
    stay = pl.BlockSpec((rows, d), lambda j, slot: (piece, 0), pipeline_mode=pl.Buffered(1))
    any_ = pl.BlockSpec(memory_space=pl.ANY)
    return pl.pallas_call(
        functools.partial(feed_kernel, len(prior)),
        grid_spec=pltpu.PrefetchScalarGridSpec(
            num_scalar_prefetch=1,
            grid=(f // tile,),
            in_specs=[whole(nrm.shape), whole(dy.shape), by_col, by_row, whole(wout.shape)]
            + [by_row, by_col, any_, any_, any_][: len(prior)],
            out_specs=[
                pl.BlockSpec((heads, rows, LANES), lambda j, slot: (0, slot[0], 0), pipeline_mode=pl.Buffered(1)),
                stay, stay, by_row, by_col,
                pl.BlockSpec((8, tile), lambda j, slot: (0, 0)),
            ],
            scratch_shapes=[pltpu.VMEM((d, rows), BF), pltpu.VMEM((rows, tile), BF), pltpu.VMEM((rows, tile), BF)],
        ),
        out_shape=[
            struct((heads, total, LANES), BF),
            struct((rows * pieces, d), F32), struct((rows * pieces, d), F32),
            struct((f, d), BF), struct((d, f), BF),
            struct((8, tile), F32),
        ],
        input_output_aliases={8 + i: i for i in range(len(prior) - 2)},
        compiler_params=params(),
        cost_estimate=cost(12 * rows * d * f, 12 * d * f + 20 * rows * d),
        name="feed",
    )(slot, nrm, dy, win, wdown, wout, *prior)


def attend_kernel(pairs, shapes, q_ref, k_ref, v_ref, *refs):
    count = len(shapes)
    xs, (ctx, wide, keep, sq), done, refs = refs[:count], refs[count : count + 4], refs[count + 4 : 2 * count + 4], refs[2 * count + 4 :]
    hold, (sems,), refs = refs[:count], refs[count : count + 1], refs[count + 1 :]
    names = Ring.SUM
    rings = [
        Ring(shape, x=xs[k], **dict(zip(names, refs[k * len(names) : (k + 1) * len(names)])))
        for k, shape in enumerate(shapes)
    ]
    chips = rings[0].chips

    def advance(s):
        for k, ring in enumerate(rings):

            def place(d, value, k=k):
                hold[k][d] = value

            ring.sum_step(s, place)

    @pl.when(pl.program_id(0) == 0)
    def _():
        rings[0].meet()
        for ring in rings:
            ring.sum_begin()

    total = q_ref.shape[1]
    b = TILE
    tri = lax.broadcasted_iota(jnp.int32, (b, b), 0) >= lax.broadcasted_iota(jnp.int32, (b, b), 1)
    low = lane_ids(b) < HEAD

    @pl.when(pl.program_id(0) == 0)
    def _():
        sq[...] = jnp.zeros_like(sq)

    def scores(h, i):
        return nt(q_ref[h, i * b : (i + 1) * b, :], k_ref[h, : (i + 1) * b, :])

    def weights(s, h, i):
        s_diag = jnp.where(tri, s[:, i * b :], excluded)
        top = jnp.max(s_diag, axis=1, keepdims=True)
        if i:
            top = jnp.maximum(top, jnp.max(s[:, : i * b], axis=1, keepdims=True))
        w = jnp.exp(s_diag - top).astype(BF)
        if i:
            w = jnp.concatenate([jnp.exp(s[:, : i * b] - top).astype(BF), w], axis=1)
        for j in range(i + 1):
            keep[h, i * (i + 1) // 2 + j] = w[:, j * b : (j + 1) * b]
        return w

    def finish(w, h, i):
        rows = pl.ds(i * b, b)
        acc = nn(w, v_ref[h, : (i + 1) * b, :])
        inv = 1.0 / acc[:, HEAD : HEAD + 1]
        acc = acc * inv
        wide[h, rows, :] = jnp.where(low, acc, inv)
        return acc

    items = [(h, i) for i in range(total // b) for h in range(2)]
    places = Places(sum(i + 1 for _, i in items), pairs, chips, advance)
    s = scores(*items[0])
    left = None
    for t, (h, i) in enumerate(items):
        s_next = scores(*items[t + 1]) if t + 1 < len(items) else None
        acc = finish(weights(s, h, i), h, i)
        if h == 0:
            left = acc
        else:
            both = jnp.where(low, left, pltpu.roll(acc, HEAD, 1)).astype(BF)
            ctx[i * b : (i + 1) * b, :] = both
            both = both.astype(F32)
            sq[...] += jnp.sum((both * both).reshape(b // 8, 8, LANES), axis=0)
        s = s_next
        places.add(i + 1)

    @pl.when(pl.program_id(0) == pairs - 1)
    def _():
        out = [pltpu.make_async_copy(hold[k], done[k], sems.at[k]) for k in range(count)]
        for c in out:
            c.start()
        for ring in rings:
            ring.sum_finish()
        for c in out:
            c.wait()


def attend(q, k, v, xs, collective_id):
    cuts = [Ring.cut(x) for x in xs]
    shapes = [c.shape for c in cuts]
    any_ = pl.BlockSpec(memory_space=pl.ANY)
    heads, total, _ = q.shape
    tiles = total // TILE
    tiles = tiles * (tiles + 1) // 2
    hd = pl.BlockSpec((2, total, LANES), lambda p: (p, 0, 0))
    return pl.pallas_call(
        functools.partial(attend_kernel, heads // 2, shapes),
        grid=(heads // 2,),
        in_specs=[hd, hd, hd] + [any_] * len(xs),
        out_specs=[
            pl.BlockSpec((total, LANES), lambda p: (0, p)),
            hd,
            pl.BlockSpec((2, tiles, TILE, TILE), lambda p: (p, 0, 0, 0)),
            pl.BlockSpec((8, LANES), lambda p: (0, 0)),
        ]
        + [any_] * len(xs),
        out_shape=[
            struct((total, heads * HEAD), BF),
            struct((heads, total, LANES), F32),
            struct((heads, tiles, TILE, TILE), BF),
            struct((8, LANES), F32),
        ]
        + [struct(c[2:], BF) for c in shapes],
        scratch_shapes=[pltpu.VMEM(c[2:], BF) for c in shapes]
        + [pltpu.SemaphoreType.DMA((len(xs),))]
        + [r for c in shapes for r in Ring.sum_scratch(c)],
        compiler_params=params(collective_id=collective_id, has_side_effects=True),
        cost_estimate=cost(4 * heads * tiles * TILE * TILE * 256, heads * total * LANES * 20, heads * tiles * TILE * TILE),
        name="attend",
    )(q, k, v, *cuts)


def attend_back_kernel(pairs, shapes, q_ref, k_ref, v_ref, do_ref, wide, keep, cos, fwd, back, *refs):
    count = len(shapes)
    done, out, totals, refs = refs[:count], refs[count], refs[count + 1 : 2 * count + 1], refs[2 * count + 1 :]
    (dk_acc, dv_acc, dq_acc, sems), refs = refs[:4], refs[4:]
    hold, refs = refs[:count], refs[count:]
    names = Ring.SPREAD
    rings = [
        Ring(shape, out=totals[k], **dict(zip(names, refs[k * len(names) : (k + 1) * len(names)])))
        for k, shape in enumerate(shapes)
    ]
    chips = rings[0].chips

    @pl.when(pl.program_id(0) == 0)
    def _():
        loads = [pltpu.make_async_copy(done[k], hold[k], sems.at[k]) for k in range(count)]
        for c in loads:
            c.start()
        rings[0].meet()
        for k, ring in enumerate(rings):
            loads[k].wait()
            for d in range(ring.parts):
                ring.full[ring.chunk(chips - 1, d), d] = hold[k][d]
                ring.spread_part(d)

    def advance(s):
        for ring in rings:
            ring.spread_step(s + 1)

    total = q_ref.shape[1]
    b = TILE
    lane = lane_ids(b)
    low = lane < HEAD

    def probs(h, i):
        w = [keep[h, i * (i + 1) // 2 + j] for j in range(i + 1)]
        return w[0] if i == 0 else jnp.concatenate(w, axis=1)

    def begin(h, i):
        rows = pl.ds(i * b, b)
        context = wide[h, rows, :]
        inv = context[:, HEAD : HEAD + 1]
        scaled = (do_ref[h, rows, :].astype(F32) * inv).astype(BF)
        grad = scaled.astype(F32)
        delta = jnp.sum(jnp.where(low, grad * context, 0.0), axis=1, keepdims=True)
        delta_hi = delta.astype(BF).astype(F32)
        delta_lo = delta - delta_hi
        joined = jnp.where(lane == HEAD, -delta_hi, jnp.where(lane == HEAD + 1, -delta_lo, grad)).astype(BF)
        return scaled, nt(joined, v_ref[h, : (i + 1) * b, :])

    def finish(h, i, scaled, dp):
        n = (i + 1) * b
        rows = pl.ds(i * b, b)
        w = probs(h, i)
        ds = w * dp.astype(BF)
        dq_acc[h, rows, :] = nn(ds, k_ref[h, :n, :]) * HEAD**-0.5
        dk = tn(ds, q_ref[h, rows, :])
        dv = tn(w, scaled)
        if i:
            dk_acc[h, : i * b, :] += dk[: i * b]
            dv_acc[h, : i * b, :] += dv[: i * b]
        dk_acc[h, rows, :] = dk[i * b :]
        dv_acc[h, rows, :] = dv[i * b :]

    items = [(h, i) for i in range(total // b) for h in range(2)]
    places = Places(sum(i + 1 for _, i in items), pairs, chips - 1, advance)
    state = begin(*items[0])
    for t, item in enumerate(items):
        later = begin(*items[t + 1]) if t + 1 < len(items) else None
        finish(*item, *state)
        state = later
        places.add(item[1] + 1)
    for i in range(total // b):
        rows = pl.ds(i * b, b)
        x = [
            turn(
                jnp.where(low, dq_acc[h, rows, :], pltpu.roll(dk_acc[h, rows, :], HEAD, 1)),
                cos[rows, :], -fwd[rows, :], -back[rows, :],
            )
            for h in range(2)
        ]
        r = pltpu.roll(x[1], HEAD, 1)
        out[rows, :LANES] = x[0].astype(BF)
        out[rows, LANES : 2 * LANES] = jnp.where(low, dv_acc[0, rows, :], r).astype(BF)
        out[rows, 2 * LANES :] = jnp.where(low, r, pltpu.roll(dv_acc[1, rows, :], HEAD, 1)).astype(BF)

    @pl.when(pl.program_id(0) == pairs - 1)
    def _():
        for ring in rings:
            ring.spread_finish()


def attend_back(q, k, v, do, wide, keep, cos, fwd, back, done, likes, collective_id):
    shapes = [jax.eval_shape(Ring.cut, x).shape for x in likes]
    any_ = pl.BlockSpec(memory_space=pl.ANY)
    heads, total, _ = q.shape
    hd = pl.BlockSpec((2, total, LANES), lambda p: (p, 0, 0))
    acc = pltpu.VMEM((2, total, LANES), F32)
    tiles = keep.shape[1]
    grad, *totals = pl.pallas_call(
        functools.partial(attend_back_kernel, heads // 2, shapes),
        grid=(heads // 2,),
        in_specs=[hd, hd, hd, hd, hd, pl.BlockSpec((2,) + keep.shape[1:], lambda p: (p, 0, 0, 0))]
        + [whole(cos.shape)] * 3
        + [any_] * len(done),
        out_specs=[pl.BlockSpec((total, 384), lambda p: (0, p))] + [any_] * len(done),
        out_shape=[struct((total, heads * 3 * HEAD), BF)] + [struct(c, BF) for c in shapes],
        scratch_shapes=[acc] * 3
        + [pltpu.SemaphoreType.DMA((len(done),))]
        + [pltpu.VMEM(c[2:], BF) for c in shapes]
        + [r for c in shapes for r in Ring.spread_scratch(c)],
        compiler_params=params(collective_id=collective_id, has_side_effects=True),
        cost_estimate=cost(8 * heads * tiles * TILE * TILE * 256, heads * total * LANES * 40),
        name="attend_back",
    )(q, k, v, do, wide, keep, cos, fwd, back, *done)
    return grad, *[t.reshape(x.shape) for t, x in zip(totals, likes)]


def join_kernel(transposed, slot, a, b, c, out):
    out[...] = ((nt if transposed else nn)(a[...], b[...]) + c[...]).astype(BF)


def join(slot, transposed, a, b, c):
    rows, width = c.shape
    tile = min(CHUNK, rows)
    step = pl.BlockSpec((tile, width), lambda i, slot: (i, 0))
    return pl.pallas_call(
        functools.partial(join_kernel, transposed),
        grid_spec=pltpu.PrefetchScalarGridSpec(
            num_scalar_prefetch=1,
            grid=(rows // tile,),
            in_specs=[
                pl.BlockSpec((tile, a.shape[1]), lambda i, slot: (slot[0] * (rows // tile) + i, 0)),
                whole(b.shape),
                step,
            ],
            out_specs=step,
        ),
        out_shape=struct((rows, width), BF),
        compiler_params=params(),
        cost_estimate=cost(2 * rows * width * a.shape[1], 2 * (b.size + rows * (3 * width + a.shape[1]))),
        name="join",
    )(slot, a, b, c)


def weight_kernel(n, index, *refs):
    groups, outs = [refs[i * n : (i + 1) * n] for i in range(4)], refs[4 * n :]
    for xs, ys, out in ((groups[0], groups[1], outs[0]), (groups[2], groups[3], outs[1])):
        width = out.shape[1]
        step = 512 if width % 512 == 0 else 128
        for c in range(width // step):
            cols = pl.ds(c * step, step)
            out[:, cols] = sum(tn(x[...], y[:, cols]) for x, y in zip(xs, ys)).astype(BF)


def weight_grads(index, x1, y1, x2, y2):
    n, d = len(x1), x1[0].shape[1]
    tile = 256
    left = [pl.BlockSpec((x.shape[0], tile), lambda j, index: (0, j)) for x in x1]
    right = lambda y: [
        pl.BlockSpec(
            (x.shape[0], y.shape[1]), functools.partial(lambda s, j, index: (index[s], 0), s), pipeline_mode=pl.Buffered(1)
        )
        for s, x in enumerate(x1)
    ]
    widths = (y1.shape[1], y2.shape[1])
    return pl.pallas_call(
        functools.partial(weight_kernel, n),
        grid_spec=pltpu.PrefetchScalarGridSpec(
            num_scalar_prefetch=1,
            grid=(d // tile,),
            in_specs=left + right(y1) + left + right(y2),
            out_specs=[pl.BlockSpec((tile, w), lambda j, index: (j, 0)) for w in widths],
        ),
        out_shape=[struct((d, w), BF) for w in widths],
        compiler_params=params(),
        cost_estimate=cost(2 * y1.shape[0] * d * sum(widths), 2 * y1.shape[0] * (2 * d + sum(widths)) + 2 * d * sum(widths)),
        name="weight_grads",
    )(index, *x1, *[y1] * n, *x2, *[y2] * n)


class Ring:
    SUM = ("near", "part", "far", "own_sem", "core_sem", "rs_send", "rs_recv")
    SPREAD = ("full", "keep_sem", "ag_send", "ag_recv", "fin_send", "fin_recv")

    def __init__(self, shape, **refs):
        self.__dict__.update(refs)
        self.chips, self.parts = shape[1], shape[2]
        dp = lax.axis_index("dp")
        self.core, chip = lax.rem(dp, 2), dp // 2
        y, z = lax.rem(chip, 2), chip // 2
        self.p = z * (1 - y) + (self.chips - 1 - z) * y
        self.peer = dp + 1 - 2 * self.core
        self.ends = [self.device(lax.rem(self.p + 1, self.chips)), self.device(lax.rem(self.p + self.chips - 1, self.chips))]

    @staticmethod
    def sum_scratch(shape):
        chips, parts = shape[1], shape[2]
        dma = pltpu.SemaphoreType.DMA
        half = pltpu.VMEM(shape[1:], BF)
        return [half, half, pltpu.VMEM((chips - 1,) + shape[2:], BF), dma((1,)), dma((2, chips)), dma((chips - 1, parts)), dma((chips - 1, parts))]

    @staticmethod
    def spread_scratch(shape):
        chips, parts = shape[1], shape[2]
        dma = pltpu.SemaphoreType.DMA
        return [pltpu.VMEM(shape[1:], BF), dma((1,))] + [dma((chips - 1, parts))] * 2 + [dma((chips, parts))] * 2

    @staticmethod
    def cut(x):
        chips = lax.axis_size("dp") // 2
        rows, d = x.shape
        parts = min(8, rows // (32 * chips))
        return x.reshape(2, chips, parts, rows // (2 * chips * parts), d)

    def device(self, pos):
        high = pos // (self.chips // 2)
        return ((1 - high) * 2 * pos + high * (2 * (self.chips - 1 - pos) + 1)) * 2 + self.core

    def remote(self, src, dst, send, recv, t):
        return pltpu.make_async_remote_copy(
            src_ref=src, dst_ref=dst, send_sem=send, recv_sem=recv,
            device_id={"dp": t}, device_id_type=pl.DeviceIdType.MESH,
        )

    def chunk(self, s, d):
        return lax.rem(self.p + 2 * self.chips - s, self.chips) if d % 2 == 0 else lax.rem(self.p + s, self.chips)

    def swap(self, c):
        return self.remote(
            self.x.at[1 - self.core, c], self.near.at[c], self.core_sem.at[0, c], self.core_sem.at[1, c], self.peer
        )

    def reduce(self, s, d):
        return self.remote(
            self.part.at[self.chunk(s, d), d], self.far.at[s, d], self.rs_send.at[s, d], self.rs_recv.at[s, d], self.ends[d % 2]
        )

    def gather(self, s, d):
        ref = self.full.at[self.chunk(self.chips - 1 + s, d), d]
        return self.remote(ref, ref, self.ag_send.at[s, d], self.ag_recv.at[s, d], self.ends[d % 2])

    def across(self, s, d, half):
        c = self.chunk(self.chips - 1 + s, d)
        return self.remote(self.full.at[c, d], self.out.at[half, c, d], self.fin_send.at[s, d], self.fin_recv.at[s, d], self.peer)

    def mine(self):
        return pltpu.make_async_copy(self.x.at[self.core], self.part, self.own_sem.at[0])

    def keep(self):
        return pltpu.make_async_copy(self.full, self.out.at[self.core], self.keep_sem.at[0])

    @staticmethod
    def add(a, b):
        return (a.astype(F32) + b.astype(F32)).astype(BF)

    def meet(self):
        barrier = pltpu.get_barrier_semaphore()
        for t in (*self.ends, self.peer):
            pl.semaphore_signal(barrier, inc=1, device_id={"dp": t}, device_id_type=pl.DeviceIdType.MESH)
        pl.semaphore_wait(barrier, 3)

    def sum_begin(self):
        self.mine().start()
        for c in range(self.chips):
            self.swap(c).start()

    def sum_step(self, s, place):
        chips, parts, part, far = self.chips, range(self.parts), self.part, self.far

        @pl.when(s == 0)
        def _():
            self.mine().wait()

            def settle(c, carry):
                self.swap(c).wait_recv()
                part[c] = self.add(part[c], self.near[c])
                return carry

            lax.fori_loop(0, chips, settle, 0)
            for d in parts:
                self.reduce(0, d).start()

        @pl.when((s > 0) & (s < chips - 1))
        def _():
            for d in parts:
                self.reduce(s - 1, d).wait_recv()
                c = self.chunk(s, d)
                part[c, d] = self.add(part[c, d], far[s - 1, d])
                self.reduce(s, d).start()

        @pl.when(s == chips - 1)
        def _():
            for d in parts:
                self.reduce(chips - 2, d).wait_recv()
                place(d, self.add(part[self.chunk(chips - 1, d), d], far[chips - 2, d]))

    def sum_finish(self):
        for c in range(self.chips):
            self.swap(c).wait_send()
        for d in range(self.parts):
            for s in range(self.chips - 1):
                self.reduce(s, d).wait_send()

    def spread_part(self, d):
        self.gather(0, d).start()
        self.across(0, d, self.core).start()

    def spread_step(self, s):
        chips, parts = self.chips, range(self.parts)

        @pl.when((s > 0) & (s < chips - 1))
        def _():
            for d in parts:
                self.gather(s - 1, d).wait_recv()
                self.gather(s, d).start()
                self.across(s, d, self.core).start()

        @pl.when(s == chips - 1)
        def _():
            for d in parts:
                self.gather(chips - 2, d).wait_recv()
                self.across(chips - 1, d, self.core).start()

    def spread_finish(self):
        self.keep().start()
        for d in range(self.parts):
            for s in range(self.chips - 1):
                self.gather(s, d).wait_send()
            for s in range(self.chips):
                self.across(s, d, self.core).wait_send()
                self.across(s, d, 1 - self.core).wait_recv()
        self.keep().wait()


def paced(place, places, limit, step):
    lax.fori_loop((place * limit) // places, ((place + 1) * limit) // places, lambda s, carry: (step(s), carry)[1], 0)


class Places:
    def __init__(self, work, per_grid, limit, step):
        self.work, self.total, self.limit, self.step, self.done, self.point = work, POINTS * per_grid, limit, step, 0, 0

    def add(self, work):
        self.done += work
        if self.done * POINTS >= (self.point + 1) * self.work:
            paced(pl.program_id(0) * POINTS + self.point, self.total, self.limit, self.step)
            self.point += 1


def tail_kernel(steps, others, shapes, gqkv, context, wqkv, wout, back, update, hidden, *refs):
    count = len(shapes)
    sent, refs = refs[:others], refs[others:]
    xs, (share, result, sq), refs = refs[:count], refs[count : count + 3], refs[count + 3 :]
    outs, refs = refs[:count], refs[count:]
    (own_grad, own_context, sems), refs = refs[:3], refs[3:]
    rings = []
    for k, shape in enumerate(shapes):
        names = Ring.SUM + Ring.SPREAD
        rings.append(Ring(shape, x=xs[k], out=outs[k], **dict(zip(names, refs[k * len(names) : (k + 1) * len(names)]))))
    chips = rings[0].chips
    i = pl.program_id(0)
    rows = own_grad.shape[0]
    height = back.shape[0]
    limit = 2 * chips - 1
    base = pl.ds(lax.axis_index("mp") * rows, rows)
    fetch = [
        pltpu.make_async_copy(gqkv.at[base], own_grad, sems.at[0]),
        pltpu.make_async_copy(context.at[base], own_context, sems.at[1]),
    ]

    @pl.when(i == 0)
    def _():
        for c in fetch:
            c.start()
        rings[0].meet()
        for ring in rings:
            ring.sum_begin()
        sq[...] = jnp.zeros_like(sq)
        for c in fetch:
            c.wait()

    def advance(s):
        for ring in rings:

            def place(d, value, ring=ring):
                ring.full[ring.chunk(chips - 1, d), d] = value
                ring.spread_part(d)

            ring.sum_step(s, place)
            ring.spread_step(s - (chips - 1))

    paced(i, steps, limit, advance)
    here = pl.ds(i * height, height)
    share[...] = (nt(own_grad[here, :], wqkv[...]) + back[...]).astype(BF)
    y = (nn(own_context[here, :], wout[...]) + update[...]).astype(BF).astype(F32)
    y = hidden[...].astype(F32) + (y + sum(p[...].astype(F32) for p in sent))
    result[...] = y.astype(BF)
    sq[...] += jnp.sum((y * y).reshape(height // 8, 8, -1), axis=0)

    @pl.when(i == steps - 1)
    def _():
        for ring in rings:
            ring.sum_finish()
            ring.spread_finish()


def tail(xs, gqkv, context, wqkv, wout, back, update, hidden, sent, collective_id):
    cuts = [Ring.cut(x) for x in xs]
    shapes = [c.shape for c in cuts]
    rows, d = hidden.shape
    steps = 16
    any_ = pl.BlockSpec(memory_space=pl.ANY)
    row = pl.BlockSpec((rows // steps, d), lambda i: (i, 0))
    share, result, sq, *totals = pl.pallas_call(
        functools.partial(tail_kernel, steps, len(sent), shapes),
        grid=(steps,),
        in_specs=[any_, any_, whole(wqkv.shape), whole(wout.shape), row, row, row] + [row] * len(sent) + [any_] * len(xs),
        out_specs=[row, row, pl.BlockSpec((8, d), lambda i: (0, 0))] + [any_] * len(xs),
        out_shape=[struct((rows, d), BF), struct((rows, d), BF), struct((8, d), F32)] + [struct(c, BF) for c in shapes],
        scratch_shapes=[
            pltpu.VMEM((rows, gqkv.shape[1]), BF), pltpu.VMEM((rows, context.shape[1]), BF), pltpu.SemaphoreType.DMA((2,)),
        ]
        + [r for c in shapes for r in Ring.sum_scratch(c) + Ring.spread_scratch(c)],
        compiler_params=params(collective_id=collective_id, has_side_effects=True),
        cost_estimate=cost(2 * rows * d * (gqkv.shape[1] + context.shape[1]), sum(4 * x.size for x in xs) + 20 * rows * d),
        name="tail",
    )(gqkv, context, wqkv, wout, back, update, hidden, *sent, *cuts)
    return share, result, sq, *[t.reshape(x.shape) for t, x in zip(totals, xs)]


def small_kernel(n_dp, n_mp, x, out, held, kept, send, recv):
    me = lax.axis_index("dp") * n_mp + lax.axis_index("mp")
    rounds = held.shape[0]

    def target(k):
        t = me + 2**k * (1 - 2 * lax.rem(me // 2**k, 2))
        return dict(device_id={"dp": t // n_mp, "mp": lax.rem(t, n_mp)}, device_id_type=pl.DeviceIdType.MESH)

    barrier = pltpu.get_barrier_semaphore()
    for k in range(rounds):
        pl.semaphore_signal(barrier, inc=1, **target(k))
    pl.semaphore_wait(barrier, rounds)
    kept[0] = x[...]
    for k in range(rounds):
        copy = pltpu.make_async_remote_copy(
            src_ref=kept.at[k], dst_ref=held.at[k], send_sem=send.at[k], recv_sem=recv.at[k], **target(k)
        )
        copy.start()
        copy.wait()
        kept[k + 1] = kept[k] + held[k]
    out[...] = kept[rounds]


def small_sum(x, collective_id):
    n_dp, n_mp = lax.axis_size("dp"), lax.axis_size("mp")
    rounds = (n_dp * n_mp).bit_length() - 1
    dma = pltpu.SemaphoreType.DMA
    vmem = pl.BlockSpec(memory_space=pltpu.VMEM)
    return pl.pallas_call(
        functools.partial(small_kernel, n_dp, n_mp),
        out_shape=struct(x.shape, F32),
        in_specs=[vmem],
        out_specs=vmem,
        scratch_shapes=[
            pltpu.VMEM((rounds,) + x.shape, F32), pltpu.VMEM((rounds + 1,) + x.shape, F32), dma((rounds,)), dma((rounds,)),
        ],
        compiler_params=params(collective_id=collective_id, has_side_effects=True),
        name="small_sum",
    )(x)


def norm_kernel(x_ref, scale, bias, out):
    x = x_ref[...].astype(F32)
    mean = jnp.mean(x, axis=1, keepdims=True)
    centred = x - mean
    var = jnp.mean(centred * centred, axis=1, keepdims=True)
    out[...] = (centred * lax.rsqrt(var + epsilon) * scale[...] + bias[...]).astype(BF)


def norm(x, scale, bias):
    rows, d = x.shape
    tile = pl.BlockSpec((min(TILE, rows), d), lambda i: (i, 0))
    return pl.pallas_call(
        norm_kernel,
        grid=(rows // min(TILE, rows),),
        in_specs=[tile, whole((1, d)), whole((1, d))],
        out_specs=tile,
        out_shape=struct((rows, d), BF),
        compiler_params=params(),
        cost_estimate=cost(10 * rows * d, 4 * rows * d),
        name="norm",
    )(x, scale, bias)


def norm_back_kernel(n, x_ref, dy, scale, *refs):
    parts, out, gain, bias = refs[:n], refs[n], refs[n + 1], refs[n + 2]

    @pl.when(pl.program_id(0) == 0)
    def _():
        gain[...] = jnp.zeros_like(gain)
        bias[...] = jnp.zeros_like(bias)

    x = x_ref[...].astype(F32)
    mean = jnp.mean(x, axis=1, keepdims=True)
    centred = x - mean
    var = jnp.mean(centred * centred, axis=1, keepdims=True)
    inv = lax.rsqrt(var + epsilon)
    unit = centred * inv
    grad = sum(p[...].astype(F32) for p in parts)
    g = grad * scale[...]
    out[...] = dy[...].astype(F32) + inv * (
        g - jnp.mean(g, axis=1, keepdims=True) - unit * jnp.mean(g * unit, axis=1, keepdims=True)
    )
    fold = lambda v: jnp.sum(v.reshape(v.shape[0] // 8, 8, -1), axis=0)
    gain[...] += fold(grad * unit)
    bias[...] += fold(grad)


def norm_back(x, dy, scale, parts):
    rows, d = x.shape
    tile = pl.BlockSpec((min(TILE, rows), d), lambda i: (i, 0))
    acc = pl.BlockSpec((8, d), lambda i: (0, 0))
    return pl.pallas_call(
        functools.partial(norm_back_kernel, len(parts)),
        grid=(rows // min(TILE, rows),),
        in_specs=[tile, tile, whole((1, d))] + [tile] * len(parts),
        out_specs=[tile, acc, acc],
        out_shape=[struct((rows, d), F32), struct((8, d), F32), struct((8, d), F32)],
        compiler_params=params(),
        cost_estimate=cost(20 * rows * d, 12 * rows * d),
        name="norm_back",
    )(x, dy, scale, *parts)


def layout(lengths, group_rows):
    seg_ends = jnp.cumsum(lengths)
    positions = jnp.arange(group_rows, dtype=jnp.int32)
    closed = seg_ends[None, :] <= positions[:, None]
    segment = jnp.sum(closed.astype(jnp.int32), axis=1)
    seg_start = jnp.sum(jnp.where(closed, lengths[None, :], 0), axis=1)
    return segment, positions - seg_start


def table_kernel(ends_ref, lens_ref, freq, cos, fwd, back, hot, neg):
    rows = cos.shape[0]
    lane = lane_ids(rows)
    where = lax.broadcasted_iota(jnp.int32, (rows, LANES), 0) + pl.program_id(0) * rows
    segment = jnp.zeros((rows, LANES), jnp.int32)
    start = jnp.zeros((rows, LANES), jnp.int32)
    for j in range(ends_ref.shape[0]):
        closed = where >= ends_ref[j]
        segment = segment + closed.astype(jnp.int32)
        start = start + jnp.where(closed, lens_ref[j], 0)
    angle = (where - start).astype(F32) * freq[...]
    dim = lax.rem(lane, HEAD)
    sin = jnp.sin(angle)
    cos[...] = jnp.where(dim < ROT, jnp.cos(angle), 1.0)
    fwd[...] = jnp.where(dim < ROT // 2, -sin, 0.0)
    back[...] = jnp.where((dim >= ROT // 2) & (dim < ROT), sin, 0.0)
    same = lane - HEAD == segment
    hot[...] = jnp.where(same, 1.0, 0.0).astype(BF)
    neg[...] = jnp.where(same | (lane < HEAD) | (lane >= HEAD + ends_ref.shape[0]), 0.0, excluded).astype(BF)


def tables(lengths, group_rows):
    half = ROT // 2
    freq = jnp.power(rope_base, -2.0 * jnp.arange(half, dtype=F32) / ROT)
    freq = jnp.pad(jnp.tile(freq, 2), (0, HEAD - ROT))
    freq = jnp.tile(freq, LANES // HEAD)[None, :]
    block = pl.BlockSpec((TILE, LANES), lambda i, *_: (i, 0))
    return pl.pallas_call(
        table_kernel,
        grid_spec=pltpu.PrefetchScalarGridSpec(
            num_scalar_prefetch=2,
            grid=(group_rows // TILE,),
            in_specs=[whole((1, LANES))],
            out_specs=[block] * 5,
        ),
        out_shape=[struct((group_rows, LANES), F32)] * 3 + [struct((group_rows, LANES), BF)] * 2,
        compiler_params=params(),
        name="tables",
    )(jnp.cumsum(lengths).astype(jnp.int32), lengths, freq)


def on_device(hidden_in, seq_lengths, ln_scale, ln_bias, wqkv, wout, win, wdown, out_grad):
    rows, d = hidden_in.shape
    n = lax.axis_size("mp")
    me = lax.axis_index("mp")
    total = rows * n
    heads = wout.shape[0] // HEAD
    f = win.shape[1]
    after = lambda x, *deps: lax.optimization_barrier((x, *deps))[0]

    normed = norm(hidden_in, ln_scale[None, :], ln_bias[None, :])
    pieces = 2 if rows >= 2 * CHUNK else 1
    high = rows // pieces
    ring = lambda s: [((i + s) % n, i) for i in range(n)]
    slot = [((me + s) % n).astype(jnp.int32)[None] for s in range(n)]
    x_all, dy_all, place = [normed], [out_grad], [slot[0]]
    gate = None
    for s in range(1, n):
        for p in range(pieces):
            mine = [v[p * high : (p + 1) * high] for v in (normed, out_grad)]
            if gate is not None:
                mine = list(lax.optimization_barrier((*mine, *gate))[:2])
            gate = [lax.ppermute(v, "mp", ring(s)) for v in mine]
            x_all.append(gate[0])
            dy_all.append(gate[1])
            place.append(slot[s] * pieces + p)
    index = jnp.concatenate(place)
    table = None

    do, up, back, gdown, gin, sq = feed(slot[0], 0, 1, total, heads, [], normed, out_grad, win, wdown, wout)
    ups, backs, sqs = [up], [back], [sq]
    qkv = []
    order = gdown
    for k in range(1, len(x_all)):
        s, p = 1 + (k - 1) // pieces, (k - 1) % pieces
        last = k == len(x_all) - 1
        if last:
            table = tables(after(seq_lengths[0], order), total)
            for t in range(k):
                qkv = project(place[t], total, heads, qkv, after(x_all[t], order), wqkv, *table)
        prior = [gdown, gin, after(do, *qkv[:1])] + ([ups[s], backs[s]] if p else [])
        do, up, back, gdown, gin, sq = feed(
            place[k], p, pieces, total, heads, prior, x_all[k], dy_all[k], win, wdown, wout
        )
        order = gdown
        ups[s:] = [up]
        backs[s:] = [back]
        sqs.append(sq)
        if last:
            qkv = project(place[k], total, heads, qkv, after(x_all[k], order), wqkv, *table)
    context, wide, keep, ctx_sq, *done = attend(*qkv, [gdown, gin], 4)
    joined = [join(slot[s], False, context, wout, ups[s]) for s in range(1, n)]
    sent = [lax.ppermute(v, "mp", ring(n - s)) for s, v in enumerate(joined, 1)]
    gqkv, gdown, gin = attend_back(*qkv, after(do, *joined), wide, keep, *table[:3], done, [gdown, gin], 3)
    returned = [lax.ppermute(join(slot[s], True, gqkv, wqkv, backs[s]), "mp", ring(n - s)) for s in range(1, n)]
    gqw, gow = weight_grads(index, x_all, gqkv, dy_all, context)
    own, result, res_sq, gqw, gow = tail(
        [gqw, gow], gqkv, context, wqkv, wout, backs[0], ups[0], hidden_in, sent, 1
    )
    grad_hidden, gain, bias = norm_back(hidden_in, out_grad, ln_scale[None, :], [own] + returned)

    stats = jnp.stack([jnp.sum(res_sq), jnp.sum(ctx_sq), sum(jnp.sum(s) for s in sqs)])
    packed = jnp.concatenate([jnp.sum(gain, axis=0), jnp.sum(bias, axis=0), jnp.pad(stats, (0, 8 * LANES - 3))])
    sums = small_sum(packed.reshape(-1, LANES), 2).reshape(-1)
    devices = lax.axis_size("dp") * n
    counts = jnp.array([rows * d * devices, rows * d * devices, rows * f * n * devices], F32)
    return (
        result,
        grad_hidden,
        sums[:d],
        sums[d : 2 * d],
        gqw.astype(F32),
        gow.T.astype(F32),
        gin.astype(F32),
        gdown.astype(F32),
        jnp.sqrt(sums[2 * d : 2 * d + 3] / counts),
    )


def solution(mesh):
    tok = P(("dp", "mp"), None)
    cols, rows = P(None, "mp"), P("mp", None)
    return jax.shard_map(
        on_device,
        mesh=mesh,
        in_specs=(tok, P("dp", None), P(), P(), cols, rows, cols, rows, tok),
        out_specs=(tok, tok, P(), P(), cols, rows, cols, rows, P()),
        check_vma=False,
    )
```

```python
import functools

import jax
import jax.numpy as jnp
from jax import lax
from jax.experimental import pallas as pl
from jax.experimental.pallas import tpu as pltpu
from jax.sharding import PartitionSpec as P

HEAD = 64
ROT = 16
LANES = 128
TILE = 256
CHUNK = 512
POINTS = 2
BACK_POINTS = 2
F32 = jnp.float32
BF = jnp.bfloat16

epsilon = 1e-05
rope_base = 10000.0
excluded = -1e20


def nn(a, b):
    return jnp.dot(a, b, preferred_element_type=F32)


def nt(a, b):
    return lax.dot_general(a, b, (((1,), (1,)), ((), ())), preferred_element_type=F32)


def tn(a, b):
    return lax.dot_general(a, b, (((0,), (0,)), ((), ())), preferred_element_type=F32)


def whole(shape):
    zeros = (0,) * len(shape)
    return pl.BlockSpec(shape, lambda *_: zeros, pipeline_mode=pl.Buffered(1))


def struct(shape, dtype):
    return jax.ShapeDtypeStruct(shape, dtype)


def cost(flops, nbytes, trans=0):
    return pl.CostEstimate(flops=int(flops), bytes_accessed=int(nbytes), transcendentals=int(trans))


def params(**kw):
    return pltpu.CompilerParams(vmem_limit_bytes=60 * 2**20, **kw)


def lane_ids(rows):
    return lax.broadcasted_iota(jnp.int32, (rows, LANES), 1)


def turn(x, cos, fwd, back):
    return x * cos + pltpu.roll(x, LANES - ROT // 2, 1) * fwd + pltpu.roll(x, ROT // 2, 1) * back


def gelu_parts(v):
    cdf = 0.5 + 0.5 * lax.erf(v * 0.7071067811865476)
    return v * cdf, cdf + v * jnp.exp(v * v * (-0.5)) * 0.3989422804014327


def ahead(count, product, use):
    held = product(0)
    for i in range(count):
        later = product(i + 1) if i + 1 < count else None
        use(i, held)
        held = later


def project_kernel(slot, nrm, wqkv, cos, fwd, back, hot, neg, *rest):
    q_out, k_out, v_out = rest[-3:]
    rows = nrm.shape[0]
    chunk = min(CHUNK, rows)
    lane = lane_ids(chunk)
    low = lane < HEAD
    one = jnp.where(lane < HEAD + 2, 1.0, 0.0)

    def place(y, r):
        blocks = [y[:, i : i + LANES] for i in range(0, y.shape[1], LANES)]
        sides = []
        for g0, g1, g2 in zip(blocks[::3], blocks[1::3], blocks[2::3]):
            r1, r2 = pltpu.roll(g1, HEAD, 1), pltpu.roll(g2, HEAD, 1)
            sides += [(g0, g1), (jnp.where(low, r1, r2), r2)]
        for h, (qk, v) in enumerate(sides):
            qk = turn(qk, cos[r, :], fwd[r, :], back[r, :])
            q_out[h, r, :] = jnp.where(low, qk * HEAD**-0.5, hot[r, :].astype(F32)).astype(BF)
            k_out[h, r, :] = jnp.where(low, pltpu.roll(qk, HEAD, 1), neg[r, :].astype(F32)).astype(BF)
            v_out[h, r, :] = jnp.where(low, v, one).astype(BF)

    ahead(
        rows // chunk,
        lambda i: nn(nrm[i * chunk : (i + 1) * chunk, :], wqkv[...]),
        lambda i, y: place(y, pl.ds(i * chunk, chunk)),
    )


def project(slot, total, heads, prior, nrm, wqkv, cos, fwd, back, hot, neg):
    rows, d = nrm.shape
    per = 4 if heads % 4 == 0 else 2
    at = pl.BlockSpec((rows, LANES), lambda j, slot: (slot[0], 0), pipeline_mode=pl.Buffered(1))
    hd = pl.BlockSpec((per, rows, LANES), lambda j, slot: (j, slot[0], 0))
    big = struct((heads, total, LANES), BF)
    return pl.pallas_call(
        project_kernel,
        grid_spec=pltpu.PrefetchScalarGridSpec(
            num_scalar_prefetch=1,
            grid=(heads // per,),
            in_specs=[whole(nrm.shape), pl.BlockSpec((d, per * 3 * HEAD), lambda j, slot: (0, j)), at, at, at, at, at]
            + [pl.BlockSpec(memory_space=pl.ANY)] * len(prior),
            out_specs=[hd, hd, hd],
        ),
        out_shape=[big, big, big],
        input_output_aliases={8 + i: i for i in range(len(prior))},
        compiler_params=params(),
        cost_estimate=cost(2 * rows * d * wqkv.shape[1], 2 * (d * wqkv.shape[1] + 6 * rows * d)),
        name="project",
    )(slot, nrm, wqkv, cos, fwd, back, hot, neg, *prior)


def feed_kernel(extra, slot, nrm, dy, win, wdown, wout, *refs):
    prior = refs[:2] if extra else ()
    do_out, update, back, gdown, gin, sq, turned, act, gpre = refs[extra:]
    j = pl.program_id(0)
    rows, d = nrm.shape
    chunk = min(TILE, rows)
    span = [pl.ds(i * chunk, chunk) for i in range(rows // chunk)]

    @pl.when(j == 0)
    def _():
        sq[...] = jnp.zeros_like(sq)
        update[...] = jnp.zeros_like(update)
        back[...] = jnp.zeros_like(back)
        turned[...] = jnp.transpose(nrm[...])
        low = lane_ids(chunk) < HEAD
        for r in span:
            g = nt(dy[r, :], wout[...])
            for p in range(g.shape[1] // LANES):
                y = g[:, p * LANES : (p + 1) * LANES]
                do_out[2 * p, r, :] = jnp.where(low, y, 0.0).astype(BF)
                do_out[2 * p + 1, r, :] = jnp.where(low, pltpu.roll(y, HEAD, 1), 0.0).astype(BF)

    def products(i):
        return nn(nrm[span[i], :], win[...]), nt(dy[span[i], :], wdown[...])

    def use(i, held):
        r = span[i]
        a, slope = gelu_parts(held[0])
        a = a.astype(BF)
        g = (held[1] * slope).astype(BF)
        act[r, :] = a
        gpre[r, :] = g
        wide = a.astype(F32)
        sq[...] += jnp.sum((wide * wide).reshape(chunk // 8, 8, -1), axis=0)
        pass

    ahead(len(span), products, use)
    update[...] += nn(act[...], wdown[...])
    back[...] += nt(gpre[...], win[...])
    down, into = tn(act[...], dy[...]), nn(turned[...], gpre[...])
    if extra:
        down, into = down + prior[0][...].astype(F32), into + prior[1][...].astype(F32)
    gdown[...] = down.astype(BF)
    gin[...] = into.astype(BF)


def feed(slot, piece, pieces, total, heads, prior, nrm, dy, win, wdown, wout):
    rows, d = nrm.shape
    f = win.shape[1]
    tile = min(512, f)
    by_row = pl.BlockSpec((tile, d), lambda j, slot: (j, 0))
    by_col = pl.BlockSpec((d, tile), lambda j, slot: (0, j))
    stay = pl.BlockSpec((rows, d), lambda j, slot: (piece, 0), pipeline_mode=pl.Buffered(1))
    any_ = pl.BlockSpec(memory_space=pl.ANY)
    return pl.pallas_call(
        functools.partial(feed_kernel, len(prior)),
        grid_spec=pltpu.PrefetchScalarGridSpec(
            num_scalar_prefetch=1,
            grid=(f // tile,),
            in_specs=[whole(nrm.shape), whole(dy.shape), by_col, by_row, whole(wout.shape)]
            + [by_row, by_col, any_, any_, any_][: len(prior)],
            out_specs=[
                pl.BlockSpec((heads, rows, LANES), lambda j, slot: (0, slot[0], 0), pipeline_mode=pl.Buffered(1)),
                stay, stay, by_row, by_col,
                pl.BlockSpec((8, tile), lambda j, slot: (0, 0)),
            ],
            scratch_shapes=[pltpu.VMEM((d, rows), BF), pltpu.VMEM((rows, tile), BF), pltpu.VMEM((rows, tile), BF)],
        ),
        out_shape=[
            struct((heads, total, LANES), BF),
            struct((rows * pieces, d), F32), struct((rows * pieces, d), F32),
            struct((f, d), BF), struct((d, f), BF),
            struct((8, tile), F32),
        ],
        input_output_aliases={8 + i: i for i in range(len(prior) - 2)},
        compiler_params=params(),
        cost_estimate=cost(12 * rows * d * f, 12 * d * f + 20 * rows * d),
        name="feed",
    )(slot, nrm, dy, win, wdown, wout, *prior)


def attend_kernel(pairs, shapes, q_ref, k_ref, v_ref, *refs):
    count = len(shapes)
    xs, (ctx, wide, keep, sq), done, refs = refs[:count], refs[count : count + 4], refs[count + 4 : 2 * count + 4], refs[2 * count + 4 :]
    hold, (sems,), refs = refs[:count], refs[count : count + 1], refs[count + 1 :]
    names = Ring.SUM
    rings = [
        Ring(shape, x=xs[k], **dict(zip(names, refs[k * len(names) : (k + 1) * len(names)])))
        for k, shape in enumerate(shapes)
    ]
    chips = rings[0].chips

    def advance(s):
        for k, ring in enumerate(rings):

            def place(d, value, k=k):
                hold[k][d] = value

            ring.sum_step(s, place)

    @pl.when(pl.program_id(0) == 0)
    def _():
        rings[0].meet()
        for ring in rings:
            ring.sum_begin()

    total = q_ref.shape[1]
    b = TILE
    tri = lax.broadcasted_iota(jnp.int32, (b, b), 0) >= lax.broadcasted_iota(jnp.int32, (b, b), 1)
    low = lane_ids(b) < HEAD

    @pl.when(pl.program_id(0) == 0)
    def _():
        sq[...] = jnp.zeros_like(sq)

    def scores(h, i):
        return nt(q_ref[h, i * b : (i + 1) * b, :], k_ref[h, : (i + 1) * b, :])

    def weights(s, h, i):
        s_diag = jnp.where(tri, s[:, i * b :], excluded)
        top = jnp.max(s_diag, axis=1, keepdims=True)
        if i:
            top = jnp.maximum(top, jnp.max(s[:, : i * b], axis=1, keepdims=True))
        w = jnp.exp(s_diag - top).astype(BF)
        if i:
            w = jnp.concatenate([jnp.exp(s[:, : i * b] - top).astype(BF), w], axis=1)
        for j in range(i + 1):
            keep[h, i * (i + 1) // 2 + j] = w[:, j * b : (j + 1) * b]
        return w

    def finish(w, h, i):
        rows = pl.ds(i * b, b)
        acc = nn(w, v_ref[h, : (i + 1) * b, :])
        inv = 1.0 / acc[:, HEAD : HEAD + 1]
        acc = acc * inv
        wide[h, rows, :] = jnp.where(low, acc, inv)
        return acc

    items = [(h, i) for i in range(total // b) for h in range(2)]
    places = Places(POINTS, sum(i + 1 for _, i in items), pairs, chips, advance)
    s = scores(*items[0])
    left = None
    for t, (h, i) in enumerate(items):
        s_next = scores(*items[t + 1]) if t + 1 < len(items) else None
        acc = finish(weights(s, h, i), h, i)
        if h == 0:
            left = acc
        else:
            both = jnp.where(low, left, pltpu.roll(acc, HEAD, 1)).astype(BF)
            ctx[i * b : (i + 1) * b, :] = both
            both = both.astype(F32)
            sq[...] += jnp.sum((both * both).reshape(b // 8, 8, LANES), axis=0)
        s = s_next
        places.add(i + 1)

    @pl.when(pl.program_id(0) == pairs - 1)
    def _():
        out = [pltpu.make_async_copy(hold[k], done[k], sems.at[k]) for k in range(count)]
        for c in out:
            c.start()
        for ring in rings:
            ring.sum_finish()
        for c in out:
            c.wait()


def attend(q, k, v, xs, collective_id):
    cuts = [Ring.cut(x) for x in xs]
    shapes = [c.shape for c in cuts]
    any_ = pl.BlockSpec(memory_space=pl.ANY)
    heads, total, _ = q.shape
    tiles = total // TILE
    tiles = tiles * (tiles + 1) // 2
    hd = pl.BlockSpec((2, total, LANES), lambda p: (p, 0, 0))
    return pl.pallas_call(
        functools.partial(attend_kernel, heads // 2, shapes),
        grid=(heads // 2,),
        in_specs=[hd, hd, hd] + [any_] * len(xs),
        out_specs=[
            pl.BlockSpec((total, LANES), lambda p: (0, p)),
            hd,
            pl.BlockSpec((2, tiles, TILE, TILE), lambda p: (p, 0, 0, 0)),
            pl.BlockSpec((8, LANES), lambda p: (0, 0)),
        ]
        + [any_] * len(xs),
        out_shape=[
            struct((total, heads * HEAD), BF),
            struct((heads, total, LANES), F32),
            struct((heads, tiles, TILE, TILE), BF),
            struct((8, LANES), F32),
        ]
        + [struct(c[2:], BF) for c in shapes],
        scratch_shapes=[pltpu.VMEM(c[2:], BF) for c in shapes]
        + [pltpu.SemaphoreType.DMA((len(xs),))]
        + [r for c in shapes for r in Ring.sum_scratch(c)],
        compiler_params=params(collective_id=collective_id, has_side_effects=True),
        cost_estimate=cost(4 * heads * tiles * TILE * TILE * 256, heads * total * LANES * 20, heads * tiles * TILE * TILE),
        name="attend",
    )(q, k, v, *cuts)


def attend_back_kernel(pairs, shapes, q_ref, k_ref, v_ref, do_ref, wide, keep, cos, fwd, back, *refs):
    count = len(shapes)
    done, out, totals, refs = refs[:count], refs[count], refs[count + 1 : 2 * count + 1], refs[2 * count + 1 :]
    (dk_acc, dv_acc, dq_acc, sems), refs = refs[:4], refs[4:]
    hold, refs = refs[:count], refs[count:]
    names = Ring.SPREAD
    rings = [
        Ring(shape, out=totals[k], **dict(zip(names, refs[k * len(names) : (k + 1) * len(names)])))
        for k, shape in enumerate(shapes)
    ]
    chips = rings[0].chips

    @pl.when(pl.program_id(0) == 0)
    def _():
        loads = [pltpu.make_async_copy(done[k], hold[k], sems.at[k]) for k in range(count)]
        for c in loads:
            c.start()
        rings[0].meet()
        for k, ring in enumerate(rings):
            loads[k].wait()
            for d in range(ring.parts):
                ring.full[ring.chunk(chips - 1, d), d] = hold[k][d]
                ring.spread_part(d)

    def advance(s):
        for ring in rings:
            ring.spread_step(s + 1)

    total = q_ref.shape[1]
    b = TILE
    lane = lane_ids(b)
    low = lane < HEAD

    def probs(h, i):
        w = [keep[h, i * (i + 1) // 2 + j] for j in range(i + 1)]
        return w[0] if i == 0 else jnp.concatenate(w, axis=1)

    def begin(h, i):
        rows = pl.ds(i * b, b)
        context = wide[h, rows, :]
        inv = context[:, HEAD : HEAD + 1]
        scaled = (do_ref[h, rows, :].astype(F32) * inv).astype(BF)
        grad = scaled.astype(F32)
        delta = jnp.sum(jnp.where(low, grad * context, 0.0), axis=1, keepdims=True)
        delta_hi = delta.astype(BF).astype(F32)
        delta_lo = delta - delta_hi
        joined = jnp.where(lane == HEAD, -delta_hi, jnp.where(lane == HEAD + 1, -delta_lo, grad)).astype(BF)
        return scaled, nt(joined, v_ref[h, : (i + 1) * b, :])

    def finish(h, i, scaled, dp):
        n = (i + 1) * b
        rows = pl.ds(i * b, b)
        w = probs(h, i)
        ds = w * dp.astype(BF)
        dq_acc[h, rows, :] = nn(ds, k_ref[h, :n, :]) * HEAD**-0.5
        dk = tn(ds, q_ref[h, rows, :])
        dv = tn(w, scaled)
        if i:
            dk_acc[h, : i * b, :] += dk[: i * b]
            dv_acc[h, : i * b, :] += dv[: i * b]
        dk_acc[h, rows, :] = dk[i * b :]
        dv_acc[h, rows, :] = dv[i * b :]

    items = [(h, i) for i in range(total // b) for h in range(2)]
    places = Places(BACK_POINTS, sum(i + 1 for _, i in items), pairs, chips - 1, advance)
    state = begin(*items[0])
    for t, item in enumerate(items):
        later = begin(*items[t + 1]) if t + 1 < len(items) else None
        finish(*item, *state)
        state = later
        places.add(item[1] + 1)
    for i in range(total // b):
        rows = pl.ds(i * b, b)
        x = [
            turn(
                jnp.where(low, dq_acc[h, rows, :], pltpu.roll(dk_acc[h, rows, :], HEAD, 1)),
                cos[rows, :], -fwd[rows, :], -back[rows, :],
            )
            for h in range(2)
        ]
        r = pltpu.roll(x[1], HEAD, 1)
        out[rows, :LANES] = x[0].astype(BF)
        out[rows, LANES : 2 * LANES] = jnp.where(low, dv_acc[0, rows, :], r).astype(BF)
        out[rows, 2 * LANES :] = jnp.where(low, r, pltpu.roll(dv_acc[1, rows, :], HEAD, 1)).astype(BF)

    @pl.when(pl.program_id(0) == pairs - 1)
    def _():
        for ring in rings:
            ring.spread_finish()


def attend_back(q, k, v, do, wide, keep, cos, fwd, back, done, likes, collective_id):
    shapes = [jax.eval_shape(Ring.cut, x).shape for x in likes]
    any_ = pl.BlockSpec(memory_space=pl.ANY)
    heads, total, _ = q.shape
    hd = pl.BlockSpec((2, total, LANES), lambda p: (p, 0, 0))
    acc = pltpu.VMEM((2, total, LANES), F32)
    tiles = keep.shape[1]
    grad, *totals = pl.pallas_call(
        functools.partial(attend_back_kernel, heads // 2, shapes),
        grid=(heads // 2,),
        in_specs=[hd, hd, hd, hd, hd, pl.BlockSpec((2,) + keep.shape[1:], lambda p: (p, 0, 0, 0))]
        + [whole(cos.shape)] * 3
        + [any_] * len(done),
        out_specs=[pl.BlockSpec((total, 384), lambda p: (0, p))] + [any_] * len(done),
        out_shape=[struct((total, heads * 3 * HEAD), BF)] + [struct(c, BF) for c in shapes],
        scratch_shapes=[acc] * 3
        + [pltpu.SemaphoreType.DMA((len(done),))]
        + [pltpu.VMEM(c[2:], BF) for c in shapes]
        + [r for c in shapes for r in Ring.spread_scratch(c)],
        compiler_params=params(collective_id=collective_id, has_side_effects=True),
        cost_estimate=cost(8 * heads * tiles * TILE * TILE * 256, heads * total * LANES * 40),
        name="attend_back",
    )(q, k, v, do, wide, keep, cos, fwd, back, *done)
    return grad, *[t.reshape(x.shape) for t, x in zip(totals, likes)]


def join_kernel(transposed, slot, a, b, c, out):
    out[...] = ((nt if transposed else nn)(a[...], b[...]) + c[...]).astype(BF)


def join(slot, transposed, a, b, c):
    rows, width = c.shape
    tile = min(CHUNK, rows)
    step = pl.BlockSpec((tile, width), lambda i, slot: (i, 0))
    return pl.pallas_call(
        functools.partial(join_kernel, transposed),
        grid_spec=pltpu.PrefetchScalarGridSpec(
            num_scalar_prefetch=1,
            grid=(rows // tile,),
            in_specs=[
                pl.BlockSpec((tile, a.shape[1]), lambda i, slot: (slot[0] * (rows // tile) + i, 0)),
                whole(b.shape),
                step,
            ],
            out_specs=step,
        ),
        out_shape=struct((rows, width), BF),
        compiler_params=params(),
        cost_estimate=cost(2 * rows * width * a.shape[1], 2 * (b.size + rows * (3 * width + a.shape[1]))),
        name="join",
    )(slot, a, b, c)


def weight_kernel(n, index, *refs):
    groups, (widen, outs) = [refs[i * n : (i + 1) * n] for i in range(4)], (refs[4 * n : 4 * n + 2], refs[4 * n + 2 :])
    for x, out in zip(widen, outs[2:]):
        out[...] = x[...].astype(F32)
    for xs, ys, out in ((groups[0], groups[1], outs[0]), (groups[2], groups[3], outs[1])):
        width = out.shape[1]
        step = 512 if width % 512 == 0 else 128
        for c in range(width // step):
            cols = pl.ds(c * step, step)
            out[:, cols] = sum(tn(x[...], y[:, cols]) for x, y in zip(xs, ys)).astype(BF)


def weight_grads(index, x1, y1, x2, y2, widen):
    n, d = len(x1), x1[0].shape[1]
    tile = 256
    left = [pl.BlockSpec((x.shape[0], tile), lambda j, index: (0, j)) for x in x1]
    right = lambda y: [
        pl.BlockSpec(
            (x.shape[0], y.shape[1]), functools.partial(lambda s, j, index: (index[s], 0), s), pipeline_mode=pl.Buffered(1)
        )
        for s, x in enumerate(x1)
    ]
    widths = (y1.shape[1], y2.shape[1])
    wide = [pl.BlockSpec((x.shape[0] * tile // d, x.shape[1]), lambda j, index: (j, 0)) for x in widen]
    return pl.pallas_call(
        functools.partial(weight_kernel, n),
        grid_spec=pltpu.PrefetchScalarGridSpec(
            num_scalar_prefetch=1,
            grid=(d // tile,),
            in_specs=left + right(y1) + left + right(y2) + wide,
            out_specs=[pl.BlockSpec((tile, w), lambda j, index: (j, 0)) for w in widths] + wide,
        ),
        out_shape=[struct((d, w), BF) for w in widths] + [struct(x.shape, F32) for x in widen],
        compiler_params=params(),
        cost_estimate=cost(2 * y1.shape[0] * d * sum(widths), 2 * y1.shape[0] * (2 * d + sum(widths)) + 2 * d * sum(widths)),
        name="weight_grads",
    )(index, *x1, *[y1] * n, *x2, *[y2] * n, *widen)


class Ring:
    SUM = ("near", "part", "far", "own_sem", "core_sem", "rs_send", "rs_recv")
    SPREAD = ("full", "keep_sem", "ag_send", "ag_recv", "fin_send", "fin_recv")

    def __init__(self, shape, **refs):
        self.__dict__.update(refs)
        self.chips, self.parts = shape[1], shape[2]
        dp = lax.axis_index("dp")
        self.core, chip = lax.rem(dp, 2), dp // 2
        y, z = lax.rem(chip, 2), chip // 2
        self.p = z * (1 - y) + (self.chips - 1 - z) * y
        self.peer = dp + 1 - 2 * self.core
        self.ends = [self.device(lax.rem(self.p + 1, self.chips)), self.device(lax.rem(self.p + self.chips - 1, self.chips))]

    @staticmethod
    def sum_scratch(shape):
        chips, parts = shape[1], shape[2]
        dma = pltpu.SemaphoreType.DMA
        half = pltpu.VMEM(shape[1:], BF)
        return [half, half, pltpu.VMEM((chips - 1,) + shape[2:], BF), dma((1,)), dma((2, chips)), dma((chips - 1, parts)), dma((chips - 1, parts))]

    @staticmethod
    def spread_scratch(shape):
        chips, parts = shape[1], shape[2]
        dma = pltpu.SemaphoreType.DMA
        return [pltpu.VMEM(shape[1:], BF), dma((1,))] + [dma((chips - 1, parts))] * 2 + [dma((chips, parts))] * 2

    @staticmethod
    def cut(x):
        chips = lax.axis_size("dp") // 2
        rows, d = x.shape
        parts = min(4, rows // (32 * chips))
        return x.reshape(2, chips, parts, rows // (2 * chips * parts), d)

    def device(self, pos):
        high = pos // (self.chips // 2)
        return ((1 - high) * 2 * pos + high * (2 * (self.chips - 1 - pos) + 1)) * 2 + self.core

    def remote(self, src, dst, send, recv, t):
        return pltpu.make_async_remote_copy(
            src_ref=src, dst_ref=dst, send_sem=send, recv_sem=recv,
            device_id={"dp": t}, device_id_type=pl.DeviceIdType.MESH,
        )

    def chunk(self, s, d):
        return lax.rem(self.p + 2 * self.chips - s, self.chips) if d % 2 == 0 else lax.rem(self.p + s, self.chips)

    def swap(self, c):
        return self.remote(
            self.x.at[1 - self.core, c], self.near.at[c], self.core_sem.at[0, c], self.core_sem.at[1, c], self.peer
        )

    def reduce(self, s, d):
        return self.remote(
            self.part.at[self.chunk(s, d), d], self.far.at[s, d], self.rs_send.at[s, d], self.rs_recv.at[s, d], self.ends[d % 2]
        )

    def gather(self, s, d):
        ref = self.full.at[self.chunk(self.chips - 1 + s, d), d]
        return self.remote(ref, ref, self.ag_send.at[s, d], self.ag_recv.at[s, d], self.ends[d % 2])

    def across(self, s, d, half):
        c = self.chunk(self.chips - 1 + s, d)
        return self.remote(self.full.at[c, d], self.out.at[half, c, d], self.fin_send.at[s, d], self.fin_recv.at[s, d], self.peer)

    def mine(self):
        return pltpu.make_async_copy(self.x.at[self.core], self.part, self.own_sem.at[0])

    def keep(self):
        return pltpu.make_async_copy(self.full, self.out.at[self.core], self.keep_sem.at[0])

    @staticmethod
    def add(a, b):
        return (a.astype(F32) + b.astype(F32)).astype(BF)

    def meet(self):
        barrier = pltpu.get_barrier_semaphore()
        for t in (*self.ends, self.peer):
            pl.semaphore_signal(barrier, inc=1, device_id={"dp": t}, device_id_type=pl.DeviceIdType.MESH)
        pl.semaphore_wait(barrier, 3)

    def sum_begin(self):
        self.mine().start()
        for c in range(self.chips):
            self.swap(c).start()

    def sum_step(self, s, place):
        chips, parts, part, far = self.chips, range(self.parts), self.part, self.far

        @pl.when(s == 0)
        def _():
            self.mine().wait()

            def settle(c, carry):
                self.swap(c).wait_recv()
                part[c] = self.add(part[c], self.near[c])
                return carry

            lax.fori_loop(0, chips, settle, 0)
            for d in parts:
                self.reduce(0, d).start()

        @pl.when((s > 0) & (s < chips - 1))
        def _():
            for d in parts:
                self.reduce(s - 1, d).wait_recv()
                c = self.chunk(s, d)
                part[c, d] = self.add(part[c, d], far[s - 1, d])
                self.reduce(s, d).start()

        @pl.when(s == chips - 1)
        def _():
            for d in parts:
                self.reduce(chips - 2, d).wait_recv()
                place(d, self.add(part[self.chunk(chips - 1, d), d], far[chips - 2, d]))

    def sum_finish(self):
        for c in range(self.chips):
            self.swap(c).wait_send()
        for d in range(self.parts):
            for s in range(self.chips - 1):
                self.reduce(s, d).wait_send()

    def spread_part(self, d):
        self.gather(0, d).start()
        self.across(0, d, self.core).start()

    def spread_step(self, s):
        chips, parts = self.chips, range(self.parts)

        @pl.when((s > 0) & (s < chips - 1))
        def _():
            for d in parts:
                self.gather(s - 1, d).wait_recv()
                self.gather(s, d).start()
                self.across(s, d, self.core).start()

        @pl.when(s == chips - 1)
        def _():
            for d in parts:
                self.gather(chips - 2, d).wait_recv()
                self.across(chips - 1, d, self.core).start()

    def spread_finish(self):
        self.keep().start()
        for d in range(self.parts):
            for s in range(self.chips - 1):
                self.gather(s, d).wait_send()
            for s in range(self.chips):
                self.across(s, d, self.core).wait_send()
                self.across(s, d, 1 - self.core).wait_recv()
        self.keep().wait()


def paced(place, places, limit, step):
    upto = lambda k: (k * limit + places - 1) // places
    lax.fori_loop(upto(place), upto(place + 1), lambda s, carry: (step(s), carry)[1], 0)


class Places:
    def __init__(self, points, work, per_grid, limit, step):
        self.points, self.total, self.work, self.limit, self.step = points, points * per_grid, work, limit, step
        self.done = self.point = 0

    def add(self, work):
        self.done += work
        if self.done * self.points >= (self.point + 1) * self.work:
            paced(pl.program_id(0) * self.points + self.point, self.total, self.limit, self.step)
            self.point += 1


def tail_kernel(steps, n_dp, n_mp, counts, shapes, gqkv, context, wqkv, wout, scale, back, update, hidden, again, dy, *refs):
    refs = list(refs)
    take = lambda k: [refs.pop(0) for _ in range(k)]
    others, squares = n_mp - 1, counts
    sent, shares, acts, (ctx_sq,), xs = take(others), take(others), take(squares), take(1), take(len(shapes))
    result, grad, sums = take(3)
    outs = take(len(shapes))
    own_grad, own_context, sems, share, got, ex_send, ex_recv, sq, gain, bias, held, kept, send, recv = take(14)
    names = Ring.SUM + Ring.SPREAD
    rings = [Ring(shape, x=x, out=out, **dict(zip(names, take(len(names))))) for shape, x, out in zip(shapes, xs, outs)]
    chips = rings[0].chips
    i = pl.program_id(0)
    rows, d = share.shape
    height, tall = back.shape[0], again.shape[0]
    first, late = rows // height, steps - rows // tall
    mp = lax.axis_index("mp")
    me = lax.axis_index("dp") * n_mp + mp
    rounds = held.shape[0]
    base = pl.ds(mp * rows, rows)
    fetch = [
        pltpu.make_async_copy(gqkv.at[base], own_grad, sems.at[0]),
        pltpu.make_async_copy(context.at[base], own_context, sems.at[1]),
    ]

    def owner(s):
        return dict(device_id={"mp": lax.rem(mp + s, n_mp)}, device_id_type=pl.DeviceIdType.MESH)

    def partner(k):
        t = me + 2**k * (1 - 2 * lax.rem(me // 2**k, 2))
        return dict(device_id={"dp": t // n_mp, "mp": lax.rem(t, n_mp)}, device_id_type=pl.DeviceIdType.MESH)

    exchange = [
        pltpu.make_async_remote_copy(
            src_ref=shares[s - 1], dst_ref=got.at[s - 1], send_sem=ex_send.at[s - 1], recv_sem=ex_recv.at[s - 1], **owner(s)
        )
        for s in range(1, n_mp)
    ]

    @pl.when(i == 0)
    def _():
        for c in fetch:
            c.start()
        barrier = pltpu.get_barrier_semaphore()
        for t in (*rings[0].ends, rings[0].peer):
            pl.semaphore_signal(barrier, inc=1, device_id={"dp": t}, device_id_type=pl.DeviceIdType.MESH)
        for t in [owner(s) for s in range(1, n_mp)] + [partner(k) for k in range(rounds)]:
            pl.semaphore_signal(barrier, inc=1, **t)
        pl.semaphore_wait(barrier, 3 + others + rounds)
        for ring in rings:
            ring.sum_begin()
        for c in exchange:
            c.start()
        for ref in (sq, gain, bias):
            ref[...] = jnp.zeros_like(ref)
        for c in fetch:
            c.wait()

    def advance(s):
        for ring in rings:

            def place(d, value, ring=ring):
                ring.full[ring.chunk(chips - 1, d), d] = value
                ring.spread_part(d)

            ring.sum_step(s, place)
            ring.spread_step(s - (chips - 1))

    fold = lambda v: jnp.sum(v.reshape(v.shape[0] // 8, 8, -1), axis=0)
    paced(i, steps, 2 * chips - 1, advance)

    @pl.when(i < first)
    def _():
        here = pl.ds(i * height, height)
        share[here, :] = (nt(own_grad[here, :], wqkv[...]) + back[...]).astype(BF)
        y = (nn(own_context[here, :], wout[...]) + update[...]).astype(BF).astype(F32)
        y = hidden[...].astype(F32) + (y + sum(p[...].astype(F32) for p in sent))
        result[...] = y.astype(BF)
        sq[...] += fold(y * y)

    @pl.when(i == late)
    def _():
        for c in exchange:
            c.wait()

    @pl.when(i >= late)
    def _():
        here = pl.ds((i - late) * tall, tall)
        x = again[...].astype(F32)
        mean = jnp.mean(x, axis=1, keepdims=True)
        centred = x - mean
        var = jnp.mean(centred * centred, axis=1, keepdims=True)
        inv = lax.rsqrt(var + epsilon)
        unit = centred * inv
        full = share[here, :].astype(F32) + sum(got[s, here, :].astype(F32) for s in range(others))
        g = full * scale[...]
        grad[...] = dy[...].astype(F32) + inv * (
            g - jnp.mean(g, axis=1, keepdims=True) - unit * jnp.mean(g * unit, axis=1, keepdims=True)
        )
        gain[...] += fold(full * unit)
        bias[...] += fold(full)

    @pl.when(i == steps - 1)
    def _():
        lane = lax.broadcasted_iota(jnp.int32, (1, d), 1)
        stats = [jnp.sum(sq[...]), jnp.sum(ctx_sq[...]), sum(jnp.sum(a[...]) for a in acts)]
        kept[0, 0:1, :] = jnp.sum(gain[...], axis=0, keepdims=True)
        kept[0, 1:2, :] = jnp.sum(bias[...], axis=0, keepdims=True)
        kept[0, 2:3, :] = jnp.where(lane == 0, stats[0], jnp.where(lane == 1, stats[1], jnp.where(lane == 2, stats[2], 0.0)))
        kept[0, 3:8, :] = jnp.zeros((5, d), F32)
        for k in range(rounds):
            copy = pltpu.make_async_remote_copy(
                src_ref=kept.at[k], dst_ref=held.at[k], send_sem=send.at[k], recv_sem=recv.at[k], **partner(k)
            )
            copy.start()
            copy.wait()
            kept[k + 1] = kept[k] + held[k]
        sums[...] = kept[rounds]
        for ring in rings:
            ring.sum_finish()
            ring.spread_finish()


def tail(xs, gqkv, context, wqkv, wout, scale, back, update, hidden, dy, sent, shares, acts, ctx_sq, collective_id):
    n_dp, n_mp = lax.axis_size("dp"), lax.axis_size("mp")
    rounds = (n_dp * n_mp).bit_length() - 1
    cuts = [Ring.cut(x) for x in xs]
    shapes = [c.shape for c in cuts]
    rows, d = hidden.shape
    steps, first, late = 16, 8, 4
    any_ = pl.BlockSpec(memory_space=pl.ANY)
    early = pl.BlockSpec((rows // first, d), lambda i: (jnp.minimum(i, first - 1), 0))
    after = pl.BlockSpec((rows // late, d), lambda i: (jnp.maximum(i - (steps - late), 0), 0))
    dma = pltpu.SemaphoreType.DMA
    acc = pltpu.VMEM((8, d), F32)
    result, grad, sums, *totals = pl.pallas_call(
        functools.partial(tail_kernel, steps, n_dp, n_mp, len(acts), shapes),
        grid=(steps,),
        in_specs=[any_, any_, whole(wqkv.shape), whole(wout.shape), whole(scale.shape), early, early, early, after, after]
        + [early] * len(sent) + [any_] * len(shares)
        + [whole(a.shape) for a in acts] + [whole(ctx_sq.shape)] + [any_] * len(xs),
        out_specs=[early, after, pl.BlockSpec((8, d), lambda i: (0, 0))] + [any_] * len(xs),
        out_shape=[struct((rows, d), BF), struct((rows, d), F32), struct((8, d), F32)] + [struct(c, BF) for c in shapes],
        scratch_shapes=[
            pltpu.VMEM((rows, gqkv.shape[1]), BF), pltpu.VMEM((rows, context.shape[1]), BF), dma((2,)),
            pltpu.VMEM((rows, d), BF), pltpu.VMEM((n_mp - 1, rows, d), BF), dma((n_mp - 1,)), dma((n_mp - 1,)),
            acc, acc, acc,
            pltpu.VMEM((rounds, 8, d), F32), pltpu.VMEM((rounds + 1, 8, d), F32), dma((rounds,)), dma((rounds,)),
        ]
        + [r for c in shapes for r in Ring.sum_scratch(c) + Ring.spread_scratch(c)],
        compiler_params=params(collective_id=collective_id, has_side_effects=True),
        cost_estimate=cost(2 * rows * d * (gqkv.shape[1] + context.shape[1]), sum(4 * x.size for x in xs) + 30 * rows * d),
        name="tail",
    )(gqkv, context, wqkv, wout, scale, back, update, hidden, hidden, dy, *sent, *shares, *acts, ctx_sq, *cuts)
    return result, grad, sums, *[t.reshape(x.shape) for t, x in zip(totals, xs)]


def norm_kernel(x_ref, scale, bias, out):
    x = x_ref[...].astype(F32)
    mean = jnp.mean(x, axis=1, keepdims=True)
    centred = x - mean
    var = jnp.mean(centred * centred, axis=1, keepdims=True)
    out[...] = (centred * lax.rsqrt(var + epsilon) * scale[...] + bias[...]).astype(BF)


def norm(x, scale, bias):
    rows, d = x.shape
    tile = pl.BlockSpec((min(TILE, rows), d), lambda i: (i, 0))
    return pl.pallas_call(
        norm_kernel,
        grid=(rows // min(TILE, rows),),
        in_specs=[tile, whole((1, d)), whole((1, d))],
        out_specs=tile,
        out_shape=struct((rows, d), BF),
        compiler_params=params(),
        cost_estimate=cost(10 * rows * d, 4 * rows * d),
        name="norm",
    )(x, scale, bias)


def table_kernel(ends_ref, lens_ref, freq, cos, fwd, back, hot, neg):
    rows = cos.shape[0]
    half = ROT // 2

    def segments(where):
        segment = jnp.zeros(where.shape, jnp.int32)
        start = jnp.zeros(where.shape, jnp.int32)
        for j in range(ends_ref.shape[0]):
            closed = where >= ends_ref[j]
            segment = segment + closed.astype(jnp.int32)
            start = start + jnp.where(closed, lens_ref[j], 0)
        return segment, where - start

    _, offset = segments(lax.broadcasted_iota(jnp.int32, (half, rows), 1))
    angle = offset.astype(F32) * freq[...]
    dim = lax.rem(lax.broadcasted_iota(jnp.int32, (half, LANES), 1), HEAD)
    unit = lax.broadcasted_iota(jnp.int32, (half, LANES), 0)

    def spread(table, mask):
        return lax.dot_general(
            table, jnp.where(mask, 1.0, 0.0), (((0,), (0,)), ((), ())),
            precision=lax.Precision.HIGHEST, preferred_element_type=F32,
        )

    sin = jnp.sin(angle)
    lane = lane_ids(rows)
    cos[...] = jnp.where(lax.rem(lane, HEAD) < ROT, spread(jnp.cos(angle), (dim == unit) | (dim == unit + half)), 1.0)
    fwd[...] = spread(-sin, dim == unit)
    back[...] = spread(sin, dim == unit + half)
    segment, _ = segments(lax.broadcasted_iota(jnp.int32, (rows, LANES), 0))
    same = lane - HEAD == segment
    hot[...] = jnp.where(same, 1.0, 0.0).astype(BF)
    neg[...] = jnp.where(same | (lane < HEAD) | (lane >= HEAD + ends_ref.shape[0]), 0.0, excluded).astype(BF)


def tables(lengths, group_rows):
    half = ROT // 2
    freq = jnp.power(rope_base, -2.0 * jnp.arange(half, dtype=F32) / ROT)[:, None]
    block = pl.BlockSpec((group_rows, LANES), lambda i, *_: (0, 0))
    return pl.pallas_call(
        table_kernel,
        grid_spec=pltpu.PrefetchScalarGridSpec(
            num_scalar_prefetch=2,
            grid=(1,),
            in_specs=[whole((half, 1))],
            out_specs=[block] * 5,
        ),
        out_shape=[struct((group_rows, LANES), F32)] * 3 + [struct((group_rows, LANES), BF)] * 2,
        compiler_params=params(),
        name="tables",
    )(jnp.cumsum(lengths).astype(jnp.int32), lengths, freq)


def on_device(hidden_in, seq_lengths, ln_scale, ln_bias, wqkv, wout, win, wdown, out_grad):
    rows, d = hidden_in.shape
    n = lax.axis_size("mp")
    me = lax.axis_index("mp")
    total = rows * n
    heads = wout.shape[0] // HEAD
    f = win.shape[1]
    after = lambda x, *deps: lax.optimization_barrier((x, *deps))[0]

    normed = norm(hidden_in, ln_scale[None, :], ln_bias[None, :])
    pieces = 2 if rows >= 2 * CHUNK else 1
    high = rows // pieces
    ring = lambda s: [((i + s) % n, i) for i in range(n)]
    slot = [((me + s) % n).astype(jnp.int32)[None] for s in range(n)]
    x_all, dy_all, place = [normed], [out_grad], [slot[0]]
    gate = None
    for s in range(1, n):
        for p in range(pieces):
            mine = [v[p * high : (p + 1) * high] for v in (normed, out_grad)]
            if gate is not None:
                mine = list(lax.optimization_barrier((*mine, *gate))[:2])
            gate = [lax.ppermute(v, "mp", ring(s)) for v in mine]
            x_all.append(gate[0])
            dy_all.append(gate[1])
            place.append(slot[s] * pieces + p)
    index = jnp.concatenate(place)
    table = None

    do, up, back, gdown, gin, sq = feed(slot[0], 0, 1, total, heads, [], normed, out_grad, win, wdown, wout)
    ups, backs, sqs = [up], [back], [sq]
    qkv = []
    order = gdown
    for k in range(1, len(x_all)):
        s, p = 1 + (k - 1) // pieces, (k - 1) % pieces
        last = k == len(x_all) - 1
        if last:
            table = tables(after(seq_lengths[0], order), total)
            for t in range(k):
                qkv = project(place[t], total, heads, qkv, after(x_all[t], order), wqkv, *table)
        prior = [gdown, gin, after(do, *qkv[:1])] + ([ups[s], backs[s]] if p else [])
        do, up, back, gdown, gin, sq = feed(
            place[k], p, pieces, total, heads, prior, x_all[k], dy_all[k], win, wdown, wout
        )
        order = gdown
        ups[s:] = [up]
        backs[s:] = [back]
        sqs.append(sq)
        if last:
            qkv = project(place[k], total, heads, qkv, after(x_all[k], order), wqkv, *table)
    context, wide, keep, ctx_sq, *done = attend(*qkv, [gdown, gin], 4)
    joined = [join(slot[s], False, context, wout, ups[s]) for s in range(1, n)]
    sent = [lax.ppermute(v, "mp", ring(n - s)) for s, v in enumerate(joined, 1)]
    gqkv, gdown, gin = attend_back(*qkv, after(do, *joined), wide, keep, *table[:3], done, [gdown, gin], 3)
    shares = [join(slot[s], True, gqkv, wqkv, backs[s]) for s in range(1, n)]
    gqw, gow, gdown, gin = weight_grads(index, x_all, gqkv, dy_all, context, [gdown, gin])
    result, grad_hidden, sums, gqw, gow = tail(
        [gqw, gow], gqkv, context, wqkv, wout, ln_scale[None, :], backs[0], ups[0], hidden_in, out_grad,
        sent, shares, sqs, ctx_sq, 1,
    )
    devices = lax.axis_size("dp") * n
    counts = jnp.array([rows * d * devices, rows * d * devices, rows * f * n * devices], F32)
    return (
        result,
        grad_hidden,
        sums[0],
        sums[1],
        gqw.astype(F32),
        gow.T.astype(F32),
        gin,
        gdown,
        jnp.sqrt(sums[2, :3] / counts),
    )


def solution(mesh):
    tok = P(("dp", "mp"), None)
    cols, rows = P(None, "mp"), P("mp", None)
    return jax.shard_map(
        on_device,
        mesh=mesh,
        in_specs=(tok, P("dp", None), P(), P(), cols, rows, cols, rows, tok),
        out_specs=(tok, tok, P(), P(), cols, rows, cols, rows, P()),
        check_vma=False,
    )
```

```python
import functools

import jax
import jax.numpy as jnp
from jax import lax
from jax.experimental import pallas as pl
from jax.experimental.pallas import tpu as pltpu
from jax.sharding import PartitionSpec as P

HEAD = 64
ROT = 16
LANES = 128
TILE = 256
CHUNK = 512
POINTS = 2
BACK_POINTS = 2
F32 = jnp.float32
BF = jnp.bfloat16

epsilon = 1e-05
rope_base = 10000.0
excluded = -1e20


def nn(a, b):
    return jnp.dot(a, b, preferred_element_type=F32)


def nt(a, b):
    return lax.dot_general(a, b, (((1,), (1,)), ((), ())), preferred_element_type=F32)


def tn(a, b):
    return lax.dot_general(a, b, (((0,), (0,)), ((), ())), preferred_element_type=F32)


def whole(shape):
    zeros = (0,) * len(shape)
    return pl.BlockSpec(shape, lambda *_: zeros, pipeline_mode=pl.Buffered(1))


def struct(shape, dtype):
    return jax.ShapeDtypeStruct(shape, dtype)


def cost(flops, nbytes, trans=0):
    return pl.CostEstimate(flops=int(flops), bytes_accessed=int(nbytes), transcendentals=int(trans))


def params(**kw):
    return pltpu.CompilerParams(vmem_limit_bytes=60 * 2**20, **kw)


def lane_ids(rows):
    return lax.broadcasted_iota(jnp.int32, (rows, LANES), 1)


def turn(x, cos, fwd, back):
    return x * cos + pltpu.roll(x, LANES - ROT // 2, 1) * fwd + pltpu.roll(x, ROT // 2, 1) * back


def gelu_parts(v):
    cdf = 0.5 + 0.5 * lax.erf(v * 0.7071067811865476)
    return v * cdf, cdf + v * jnp.exp(v * v * (-0.5)) * 0.3989422804014327


def ahead(count, product, use):
    held = product(0)
    for i in range(count):
        later = product(i + 1) if i + 1 < count else None
        use(i, held)
        held = later


def project_kernel(slot, nrm, wqkv, cos, fwd, back, hot, neg, *rest):
    q_out, k_out, v_out = rest[-3:]
    rows = nrm.shape[0]
    chunk = min(CHUNK, rows)
    lane = lane_ids(chunk)
    low = lane < HEAD
    one = jnp.where(lane < HEAD + 2, 1.0, 0.0)

    def place(y, r):
        blocks = [y[:, i : i + LANES] for i in range(0, y.shape[1], LANES)]
        sides = []
        for g0, g1, g2 in zip(blocks[::3], blocks[1::3], blocks[2::3]):
            r1, r2 = pltpu.roll(g1, HEAD, 1), pltpu.roll(g2, HEAD, 1)
            sides += [(g0, g1), (jnp.where(low, r1, r2), r2)]
        for h, (qk, v) in enumerate(sides):
            qk = turn(qk, cos[r, :], fwd[r, :], back[r, :])
            q_out[h, r, :] = jnp.where(low, qk * HEAD**-0.5, hot[r, :].astype(F32)).astype(BF)
            k_out[h, r, :] = jnp.where(low, pltpu.roll(qk, HEAD, 1), neg[r, :].astype(F32)).astype(BF)
            v_out[h, r, :] = jnp.where(low, v, one).astype(BF)

    ahead(
        rows // chunk,
        lambda i: nn(nrm[i * chunk : (i + 1) * chunk, :], wqkv[...]),
        lambda i, y: place(y, pl.ds(i * chunk, chunk)),
    )


def project(slot, total, heads, prior, nrm, wqkv, cos, fwd, back, hot, neg):
    rows, d = nrm.shape
    per = 4 if heads % 4 == 0 else 2
    at = pl.BlockSpec((rows, LANES), lambda j, slot: (slot[0], 0), pipeline_mode=pl.Buffered(1))
    hd = pl.BlockSpec((per, rows, LANES), lambda j, slot: (j, slot[0], 0))
    big = struct((heads, total, LANES), BF)
    return pl.pallas_call(
        project_kernel,
        grid_spec=pltpu.PrefetchScalarGridSpec(
            num_scalar_prefetch=1,
            grid=(heads // per,),
            in_specs=[whole(nrm.shape), pl.BlockSpec((d, per * 3 * HEAD), lambda j, slot: (0, j)), at, at, at, at, at]
            + [pl.BlockSpec(memory_space=pl.ANY)] * len(prior),
            out_specs=[hd, hd, hd],
        ),
        out_shape=[big, big, big],
        input_output_aliases={8 + i: i for i in range(len(prior))},
        compiler_params=params(),
        cost_estimate=cost(2 * rows * d * wqkv.shape[1], 2 * (d * wqkv.shape[1] + 6 * rows * d)),
        name="project",
    )(slot, nrm, wqkv, cos, fwd, back, hot, neg, *prior)


def feed_kernel(extra, slot, nrm, dy, win, wdown, wout, *refs):
    prior = refs[:2] if extra else ()
    do_out, update, back, gdown, gin, sq, turned, act, gpre = refs[extra:]
    j = pl.program_id(0)
    rows, d = nrm.shape
    chunk = min(TILE, rows)
    span = [pl.ds(i * chunk, chunk) for i in range(rows // chunk)]

    @pl.when(j == 0)
    def _():
        sq[...] = jnp.zeros_like(sq)
        update[...] = jnp.zeros_like(update)
        back[...] = jnp.zeros_like(back)
        turned[...] = jnp.transpose(nrm[...])
        low = lane_ids(chunk) < HEAD
        for r in span:
            g = nt(dy[r, :], wout[...])
            for p in range(g.shape[1] // LANES):
                y = g[:, p * LANES : (p + 1) * LANES]
                do_out[2 * p, r, :] = jnp.where(low, y, 0.0).astype(BF)
                do_out[2 * p + 1, r, :] = jnp.where(low, pltpu.roll(y, HEAD, 1), 0.0).astype(BF)

    def products(i):
        return nn(nrm[span[i], :], win[...]), nt(dy[span[i], :], wdown[...])

    def use(i, held):
        r = span[i]
        a, slope = gelu_parts(held[0])
        a = a.astype(BF)
        g = (held[1] * slope).astype(BF)
        act[r, :] = a
        gpre[r, :] = g
        wide = a.astype(F32)
        sq[...] += jnp.sum((wide * wide).reshape(chunk // 8, 8, -1), axis=0)
        pass

    ahead(len(span), products, use)
    update[...] += nn(act[...], wdown[...])
    back[...] += nt(gpre[...], win[...])
    down, into = tn(act[...], dy[...]), nn(turned[...], gpre[...])
    if extra:
        down, into = down + prior[0][...].astype(F32), into + prior[1][...].astype(F32)
    gdown[...] = down.astype(BF)
    gin[...] = into.astype(BF)


def feed(slot, piece, pieces, total, heads, prior, nrm, dy, win, wdown, wout):
    rows, d = nrm.shape
    f = win.shape[1]
    tile = min(512, f)
    by_row = pl.BlockSpec((tile, d), lambda j, slot: (j, 0))
    by_col = pl.BlockSpec((d, tile), lambda j, slot: (0, j))
    stay = pl.BlockSpec((rows, d), lambda j, slot: (piece, 0), pipeline_mode=pl.Buffered(1))
    any_ = pl.BlockSpec(memory_space=pl.ANY)
    return pl.pallas_call(
        functools.partial(feed_kernel, len(prior)),
        grid_spec=pltpu.PrefetchScalarGridSpec(
            num_scalar_prefetch=1,
            grid=(f // tile,),
            in_specs=[whole(nrm.shape), whole(dy.shape), by_col, by_row, whole(wout.shape)]
            + [by_row, by_col, any_, any_, any_][: len(prior)],
            out_specs=[
                pl.BlockSpec((heads, rows, LANES), lambda j, slot: (0, slot[0], 0), pipeline_mode=pl.Buffered(1)),
                stay, stay, by_row, by_col,
                pl.BlockSpec((8, tile), lambda j, slot: (0, 0)),
            ],
            scratch_shapes=[pltpu.VMEM((d, rows), BF), pltpu.VMEM((rows, tile), BF), pltpu.VMEM((rows, tile), BF)],
        ),
        out_shape=[
            struct((heads, total, LANES), BF),
            struct((rows * pieces, d), F32), struct((rows * pieces, d), F32),
            struct((f, d), BF), struct((d, f), BF),
            struct((8, tile), F32),
        ],
        input_output_aliases={8 + i: i for i in range(len(prior) - 2)},
        compiler_params=params(),
        cost_estimate=cost(12 * rows * d * f, 12 * d * f + 20 * rows * d),
        name="feed",
    )(slot, nrm, dy, win, wdown, wout, *prior)


def attend_kernel(pairs, shapes, q_ref, k_ref, v_ref, *refs):
    count = len(shapes)
    xs, (ctx, wide, keep, sq), done, refs = refs[:count], refs[count : count + 4], refs[count + 4 : 2 * count + 4], refs[2 * count + 4 :]
    hold, (sems,), refs = refs[:count], refs[count : count + 1], refs[count + 1 :]
    names = Ring.SUM
    rings = [
        Ring(shape, x=xs[k], **dict(zip(names, refs[k * len(names) : (k + 1) * len(names)])))
        for k, shape in enumerate(shapes)
    ]
    chips = rings[0].chips

    def advance(s):
        for k, ring in enumerate(rings):

            def place(d, value, k=k):
                hold[k][d] = value

            ring.sum_step(s, place)

    @pl.when(pl.program_id(0) == 0)
    def _():
        rings[0].meet()
        for ring in rings:
            ring.sum_begin()

    total = q_ref.shape[1]
    b = TILE
    tri = lax.broadcasted_iota(jnp.int32, (b, b), 0) >= lax.broadcasted_iota(jnp.int32, (b, b), 1)
    low = lane_ids(b) < HEAD

    @pl.when(pl.program_id(0) == 0)
    def _():
        sq[...] = jnp.zeros_like(sq)

    def scores(h, i):
        return nt(q_ref[h, i * b : (i + 1) * b, :], k_ref[h, : (i + 1) * b, :])

    def weights(s, h, i):
        s_diag = jnp.where(tri, s[:, i * b :], excluded)
        top = jnp.max(s_diag, axis=1, keepdims=True)
        if i:
            top = jnp.maximum(top, jnp.max(s[:, : i * b], axis=1, keepdims=True))
        w = jnp.exp(s_diag - top).astype(BF)
        if i:
            w = jnp.concatenate([jnp.exp(s[:, : i * b] - top).astype(BF), w], axis=1)
        for j in range(i + 1):
            keep[h, i * (i + 1) // 2 + j] = w[:, j * b : (j + 1) * b]
        return w

    def finish(w, h, i):
        rows = pl.ds(i * b, b)
        acc = nn(w, v_ref[h, : (i + 1) * b, :])
        inv = 1.0 / acc[:, HEAD : HEAD + 1]
        acc = acc * inv
        wide[h, rows, :] = jnp.where(low, acc, inv)
        return acc

    items = [(h, i) for i in range(total // b) for h in range(2)]
    places = Places(POINTS, sum(i + 1 for _, i in items), pairs, chips, advance)
    s = scores(*items[0])
    left = None
    for t, (h, i) in enumerate(items):
        s_next = scores(*items[t + 1]) if t + 1 < len(items) else None
        acc = finish(weights(s, h, i), h, i)
        if h == 0:
            left = acc
        else:
            both = jnp.where(low, left, pltpu.roll(acc, HEAD, 1)).astype(BF)
            ctx[i * b : (i + 1) * b, :] = both
            both = both.astype(F32)
            sq[...] += jnp.sum((both * both).reshape(b // 8, 8, LANES), axis=0)
        s = s_next
        places.add(i + 1)

    @pl.when(pl.program_id(0) == pairs - 1)
    def _():
        out = [pltpu.make_async_copy(hold[k], done[k], sems.at[k]) for k in range(count)]
        for c in out:
            c.start()
        for ring in rings:
            ring.sum_finish()
        for c in out:
            c.wait()


def attend(q, k, v, xs, collective_id):
    cuts = [Ring.cut(x) for x in xs]
    shapes = [c.shape for c in cuts]
    any_ = pl.BlockSpec(memory_space=pl.ANY)
    heads, total, _ = q.shape
    tiles = total // TILE
    tiles = tiles * (tiles + 1) // 2
    hd = pl.BlockSpec((2, total, LANES), lambda p: (p, 0, 0))
    return pl.pallas_call(
        functools.partial(attend_kernel, heads // 2, shapes),
        grid=(heads // 2,),
        in_specs=[hd, hd, hd] + [any_] * len(xs),
        out_specs=[
            pl.BlockSpec((total, LANES), lambda p: (0, p)),
            hd,
            pl.BlockSpec((2, tiles, TILE, TILE), lambda p: (p, 0, 0, 0)),
            pl.BlockSpec((8, LANES), lambda p: (0, 0)),
        ]
        + [any_] * len(xs),
        out_shape=[
            struct((total, heads * HEAD), BF),
            struct((heads, total, LANES), F32),
            struct((heads, tiles, TILE, TILE), BF),
            struct((8, LANES), F32),
        ]
        + [struct(c[2:], BF) for c in shapes],
        scratch_shapes=[pltpu.VMEM(c[2:], BF) for c in shapes]
        + [pltpu.SemaphoreType.DMA((len(xs),))]
        + [r for c in shapes for r in Ring.sum_scratch(c)],
        compiler_params=params(collective_id=collective_id, has_side_effects=True),
        cost_estimate=cost(4 * heads * tiles * TILE * TILE * 256, heads * total * LANES * 20, heads * tiles * TILE * TILE),
        name="attend",
    )(q, k, v, *cuts)


def attend_back_kernel(pairs, shapes, q_ref, k_ref, v_ref, do_ref, wide, keep, cos, fwd, back, *refs):
    count = len(shapes)
    done, out, totals, refs = refs[:count], refs[count], refs[count + 1 : 2 * count + 1], refs[2 * count + 1 :]
    (dk_acc, dv_acc, dq_acc, sems), refs = refs[:4], refs[4:]
    hold, refs = refs[:count], refs[count:]
    names = Ring.SPREAD
    rings = [
        Ring(shape, out=totals[k], **dict(zip(names, refs[k * len(names) : (k + 1) * len(names)])))
        for k, shape in enumerate(shapes)
    ]
    chips = rings[0].chips

    @pl.when(pl.program_id(0) == 0)
    def _():
        loads = [pltpu.make_async_copy(done[k], hold[k], sems.at[k]) for k in range(count)]
        for c in loads:
            c.start()
        rings[0].meet()
        for k, ring in enumerate(rings):
            loads[k].wait()
            for d in range(ring.parts):
                ring.full[ring.chunk(chips - 1, d), d] = hold[k][d]
                ring.spread_part(d)

    def advance(s):
        for ring in rings:
            ring.spread_step(s + 1)

    total = q_ref.shape[1]
    b = TILE
    lane = lane_ids(b)
    low = lane < HEAD

    def probs(h, i):
        w = [keep[h, i * (i + 1) // 2 + j] for j in range(i + 1)]
        return w[0] if i == 0 else jnp.concatenate(w, axis=1)

    def begin(h, i):
        rows = pl.ds(i * b, b)
        context = wide[h, rows, :]
        inv = context[:, HEAD : HEAD + 1]
        scaled = (do_ref[h, rows, :].astype(F32) * inv).astype(BF)
        grad = scaled.astype(F32)
        delta = jnp.sum(jnp.where(low, grad * context, 0.0), axis=1, keepdims=True)
        delta_hi = delta.astype(BF).astype(F32)
        delta_lo = delta - delta_hi
        joined = jnp.where(lane == HEAD, -delta_hi, jnp.where(lane == HEAD + 1, -delta_lo, grad)).astype(BF)
        return scaled, nt(joined, v_ref[h, : (i + 1) * b, :])

    def finish(h, i, scaled, dp):
        n = (i + 1) * b
        rows = pl.ds(i * b, b)
        w = probs(h, i)
        ds = w * dp.astype(BF)
        dq_acc[h, rows, :] = nn(ds, k_ref[h, :n, :]) * HEAD**-0.5
        dk = tn(ds, q_ref[h, rows, :])
        dv = tn(w, scaled)
        if i:
            dk_acc[h, : i * b, :] += dk[: i * b]
            dv_acc[h, : i * b, :] += dv[: i * b]
        dk_acc[h, rows, :] = dk[i * b :]
        dv_acc[h, rows, :] = dv[i * b :]

    items = [(h, i) for i in range(total // b) for h in range(2)]
    places = Places(BACK_POINTS, sum(i + 1 for _, i in items), pairs, chips - 1, advance)
    state = begin(*items[0])
    for t, item in enumerate(items):
        later = begin(*items[t + 1]) if t + 1 < len(items) else None
        finish(*item, *state)
        state = later
        places.add(item[1] + 1)
    for i in range(total // b):
        rows = pl.ds(i * b, b)
        x = [
            turn(
                jnp.where(low, dq_acc[h, rows, :], pltpu.roll(dk_acc[h, rows, :], HEAD, 1)),
                cos[rows, :], -fwd[rows, :], -back[rows, :],
            )
            for h in range(2)
        ]
        r = pltpu.roll(x[1], HEAD, 1)
        out[rows, :LANES] = x[0].astype(BF)
        out[rows, LANES : 2 * LANES] = jnp.where(low, dv_acc[0, rows, :], r).astype(BF)
        out[rows, 2 * LANES :] = jnp.where(low, r, pltpu.roll(dv_acc[1, rows, :], HEAD, 1)).astype(BF)

    @pl.when(pl.program_id(0) == pairs - 1)
    def _():
        for ring in rings:
            ring.keep().start()
        for ring in rings:
            ring.spread_finish()


def attend_back(q, k, v, do, wide, keep, cos, fwd, back, done, likes, collective_id):
    shapes = [jax.eval_shape(Ring.cut, x).shape for x in likes]
    any_ = pl.BlockSpec(memory_space=pl.ANY)
    heads, total, _ = q.shape
    hd = pl.BlockSpec((2, total, LANES), lambda p: (p, 0, 0))
    acc = pltpu.VMEM((2, total, LANES), F32)
    tiles = keep.shape[1]
    grad, *totals = pl.pallas_call(
        functools.partial(attend_back_kernel, heads // 2, shapes),
        grid=(heads // 2,),
        in_specs=[hd, hd, hd, hd, hd, pl.BlockSpec((2,) + keep.shape[1:], lambda p: (p, 0, 0, 0))]
        + [whole(cos.shape)] * 3
        + [any_] * len(done),
        out_specs=[pl.BlockSpec((total, 384), lambda p: (0, p))] + [any_] * len(done),
        out_shape=[struct((total, heads * 3 * HEAD), BF)] + [struct(c, BF) for c in shapes],
        scratch_shapes=[acc] * 3
        + [pltpu.SemaphoreType.DMA((len(done),))]
        + [pltpu.VMEM(c[2:], BF) for c in shapes]
        + [r for c in shapes for r in Ring.spread_scratch(c)],
        compiler_params=params(collective_id=collective_id, has_side_effects=True),
        cost_estimate=cost(8 * heads * tiles * TILE * TILE * 256, heads * total * LANES * 40),
        name="attend_back",
    )(q, k, v, do, wide, keep, cos, fwd, back, *done)
    return grad, *[t.reshape(x.shape) for t, x in zip(totals, likes)]


def join_kernel(transposed, slot, a, b, c, out):
    out[...] = ((nt if transposed else nn)(a[...], b[...]) + c[...]).astype(BF)


def join(slot, transposed, a, b, c):
    rows, width = c.shape
    tile = min(CHUNK, rows)
    step = pl.BlockSpec((tile, width), lambda i, slot: (i, 0))
    return pl.pallas_call(
        functools.partial(join_kernel, transposed),
        grid_spec=pltpu.PrefetchScalarGridSpec(
            num_scalar_prefetch=1,
            grid=(rows // tile,),
            in_specs=[
                pl.BlockSpec((tile, a.shape[1]), lambda i, slot: (slot[0] * (rows // tile) + i, 0)),
                whole(b.shape),
                step,
            ],
            out_specs=step,
        ),
        out_shape=struct((rows, width), BF),
        compiler_params=params(),
        cost_estimate=cost(2 * rows * width * a.shape[1], 2 * (b.size + rows * (3 * width + a.shape[1]))),
        name="join",
    )(slot, a, b, c)


def weight_kernel(n, index, *refs):
    groups, (widen, outs) = [refs[i * n : (i + 1) * n] for i in range(4)], (refs[4 * n : 4 * n + 2], refs[4 * n + 2 :])
    for x, out in zip(widen, outs[2:]):
        out[...] = x[...].astype(F32)
    for xs, ys, out in ((groups[0], groups[1], outs[0]), (groups[2], groups[3], outs[1])):
        width = out.shape[1]
        step = 512 if width % 512 == 0 else 128
        for c in range(width // step):
            cols = pl.ds(c * step, step)
            out[:, cols] = sum(tn(x[...], y[:, cols]) for x, y in zip(xs, ys)).astype(BF)


def weight_grads(index, x1, y1, x2, y2, widen):
    n, d = len(x1), x1[0].shape[1]
    tile = 256
    left = [pl.BlockSpec((x.shape[0], tile), lambda j, index: (0, j)) for x in x1]
    right = lambda y: [
        pl.BlockSpec(
            (x.shape[0], y.shape[1]), functools.partial(lambda s, j, index: (index[s], 0), s), pipeline_mode=pl.Buffered(1)
        )
        for s, x in enumerate(x1)
    ]
    widths = (y1.shape[1], y2.shape[1])
    wide = [pl.BlockSpec((x.shape[0] * tile // d, x.shape[1]), lambda j, index: (j, 0)) for x in widen]
    return pl.pallas_call(
        functools.partial(weight_kernel, n),
        grid_spec=pltpu.PrefetchScalarGridSpec(
            num_scalar_prefetch=1,
            grid=(d // tile,),
            in_specs=left + right(y1) + left + right(y2) + wide,
            out_specs=[pl.BlockSpec((tile, w), lambda j, index: (j, 0)) for w in widths] + wide,
        ),
        out_shape=[struct((d, w), BF) for w in widths] + [struct(x.shape, F32) for x in widen],
        compiler_params=params(),
        cost_estimate=cost(2 * y1.shape[0] * d * sum(widths), 2 * y1.shape[0] * (2 * d + sum(widths)) + 2 * d * sum(widths)),
        name="weight_grads",
    )(index, *x1, *[y1] * n, *x2, *[y2] * n, *widen)


class Ring:
    SUM = ("near", "part", "far", "own_sem", "core_sem", "rs_send", "rs_recv")
    SPREAD = ("full", "keep_sem", "ag_send", "ag_recv", "fin_send", "fin_recv")

    def __init__(self, shape, **refs):
        self.__dict__.update(refs)
        self.chips, self.parts = shape[1], shape[2]
        dp = lax.axis_index("dp")
        self.core, chip = lax.rem(dp, 2), dp // 2
        y, z = lax.rem(chip, 2), chip // 2
        self.p = z * (1 - y) + (self.chips - 1 - z) * y
        self.peer = dp + 1 - 2 * self.core
        self.ends = [self.device(lax.rem(self.p + 1, self.chips)), self.device(lax.rem(self.p + self.chips - 1, self.chips))]

    @staticmethod
    def sum_scratch(shape):
        chips, parts = shape[1], shape[2]
        dma = pltpu.SemaphoreType.DMA
        half = pltpu.VMEM(shape[1:], BF)
        return [half, half, pltpu.VMEM((chips - 1,) + shape[2:], BF), dma((1,)), dma((2, chips)), dma((chips - 1, parts)), dma((chips - 1, parts))]

    @staticmethod
    def spread_scratch(shape):
        chips, parts = shape[1], shape[2]
        dma = pltpu.SemaphoreType.DMA
        return [pltpu.VMEM(shape[1:], BF), dma((1,))] + [dma((chips - 1, parts))] * 2 + [dma((chips, parts))] * 2

    @staticmethod
    def cut(x):
        chips = lax.axis_size("dp") // 2
        rows, d = x.shape
        parts = min(4, rows // (32 * chips))
        return x.reshape(2, chips, parts, rows // (2 * chips * parts), d)

    def device(self, pos):
        high = pos // (self.chips // 2)
        return ((1 - high) * 2 * pos + high * (2 * (self.chips - 1 - pos) + 1)) * 2 + self.core

    def remote(self, src, dst, send, recv, t):
        return pltpu.make_async_remote_copy(
            src_ref=src, dst_ref=dst, send_sem=send, recv_sem=recv,
            device_id={"dp": t}, device_id_type=pl.DeviceIdType.MESH,
        )

    def chunk(self, s, d):
        return lax.rem(self.p + 2 * self.chips - s, self.chips) if d % 2 == 0 else lax.rem(self.p + s, self.chips)

    def swap(self, c):
        return self.remote(
            self.x.at[1 - self.core, c], self.near.at[c], self.core_sem.at[0, c], self.core_sem.at[1, c], self.peer
        )

    def reduce(self, s, d):
        return self.remote(
            self.part.at[self.chunk(s, d), d], self.far.at[s, d], self.rs_send.at[s, d], self.rs_recv.at[s, d], self.ends[d % 2]
        )

    def gather(self, s, d):
        ref = self.full.at[self.chunk(self.chips - 1 + s, d), d]
        return self.remote(ref, ref, self.ag_send.at[s, d], self.ag_recv.at[s, d], self.ends[d % 2])

    def across(self, s, d, half):
        c = self.chunk(self.chips - 1 + s, d)
        return self.remote(self.full.at[c, d], self.out.at[half, c, d], self.fin_send.at[s, d], self.fin_recv.at[s, d], self.peer)

    def mine(self):
        return pltpu.make_async_copy(self.x.at[self.core], self.part, self.own_sem.at[0])

    def keep(self):
        return pltpu.make_async_copy(self.full, self.out.at[self.core], self.keep_sem.at[0])

    @staticmethod
    def add(a, b):
        return (a.astype(F32) + b.astype(F32)).astype(BF)

    def meet(self):
        barrier = pltpu.get_barrier_semaphore()
        for t in (*self.ends, self.peer):
            pl.semaphore_signal(barrier, inc=1, device_id={"dp": t}, device_id_type=pl.DeviceIdType.MESH)
        pl.semaphore_wait(barrier, 3)

    def sum_begin(self):
        self.mine().start()
        for c in range(self.chips):
            self.swap(c).start()

    def sum_step(self, s, place):
        chips, parts, part, far = self.chips, range(self.parts), self.part, self.far

        @pl.when(s == 0)
        def _():
            self.mine().wait()

            def settle(c, carry):
                self.swap(c).wait_recv()
                part[c] = self.add(part[c], self.near[c])
                return carry

            lax.fori_loop(0, chips, settle, 0)
            for d in parts:
                self.reduce(0, d).start()

        @pl.when((s > 0) & (s < chips - 1))
        def _():
            for d in parts:
                self.reduce(s - 1, d).wait_recv()
                c = self.chunk(s, d)
                part[c, d] = self.add(part[c, d], far[s - 1, d])
                self.reduce(s, d).start()

        @pl.when(s == chips - 1)
        def _():
            for d in parts:
                self.reduce(chips - 2, d).wait_recv()
                place(d, self.add(part[self.chunk(chips - 1, d), d], far[chips - 2, d]))

    def sum_finish(self):
        for c in range(self.chips):
            self.swap(c).wait_send()
        for d in range(self.parts):
            for s in range(self.chips - 1):
                self.reduce(s, d).wait_send()

    def spread_part(self, d):
        self.gather(0, d).start()
        self.across(0, d, self.core).start()

    def spread_step(self, s):
        chips, parts = self.chips, range(self.parts)

        @pl.when((s > 0) & (s < chips - 1))
        def _():
            for d in parts:
                self.gather(s - 1, d).wait_recv()
                self.gather(s, d).start()
                self.across(s, d, self.core).start()

        @pl.when(s == chips - 1)
        def _():
            for d in parts:
                self.gather(chips - 2, d).wait_recv()
                self.across(chips - 1, d, self.core).start()

    def spread_finish(self):
        for d in range(self.parts):
            for s in range(self.chips - 1):
                self.gather(s, d).wait_send()
            for s in range(self.chips):
                self.across(s, d, self.core).wait_send()
                self.across(s, d, 1 - self.core).wait_recv()
        self.keep().wait()


def paced(place, places, limit, step):
    upto = lambda k: (k * limit + places - 1) // places
    lax.fori_loop(upto(place), upto(place + 1), lambda s, carry: (step(s), carry)[1], 0)


class Places:
    def __init__(self, points, work, per_grid, limit, step):
        self.points, self.total, self.work, self.limit, self.step = points, points * per_grid, work, limit, step
        self.done = self.point = 0

    def add(self, work):
        self.done += work
        if self.done * self.points >= (self.point + 1) * self.work:
            paced(pl.program_id(0) * self.points + self.point, self.total, self.limit, self.step)
            self.point += 1


def tail_kernel(steps, n_dp, n_mp, counts, shapes, gqkv, context, wqkv, wout, scale, back, update, hidden, again, dy, *refs):
    refs = list(refs)
    take = lambda k: [refs.pop(0) for _ in range(k)]
    others, squares = n_mp - 1, counts
    sent, shares, acts, (ctx_sq,), xs = take(others), take(others), take(squares), take(1), take(len(shapes))
    result, grad, sums = take(3)
    outs = take(len(shapes))
    own_grad, own_context, sems, share, got, ex_send, ex_recv, sq, gain, bias, held, kept, send, recv = take(14)
    names = Ring.SUM + Ring.SPREAD
    rings = [Ring(shape, x=x, out=out, **dict(zip(names, take(len(names))))) for shape, x, out in zip(shapes, xs, outs)]
    chips = rings[0].chips
    i = pl.program_id(0)
    rows, d = share.shape
    height, tall = back.shape[0], again.shape[0]
    first, late = rows // height, steps - rows // tall
    mp = lax.axis_index("mp")
    me = lax.axis_index("dp") * n_mp + mp
    rounds = held.shape[0]
    base = pl.ds(mp * rows, rows)
    fetch = [
        pltpu.make_async_copy(gqkv.at[base], own_grad, sems.at[0]),
        pltpu.make_async_copy(context.at[base], own_context, sems.at[1]),
    ]

    def owner(s):
        return dict(device_id={"mp": lax.rem(mp + s, n_mp)}, device_id_type=pl.DeviceIdType.MESH)

    def partner(k):
        t = me + 2**k * (1 - 2 * lax.rem(me // 2**k, 2))
        return dict(device_id={"dp": t // n_mp, "mp": lax.rem(t, n_mp)}, device_id_type=pl.DeviceIdType.MESH)

    exchange = [
        pltpu.make_async_remote_copy(
            src_ref=shares[s - 1], dst_ref=got.at[s - 1], send_sem=ex_send.at[s - 1], recv_sem=ex_recv.at[s - 1], **owner(s)
        )
        for s in range(1, n_mp)
    ]

    @pl.when(i == 0)
    def _():
        for c in fetch:
            c.start()
        barrier = pltpu.get_barrier_semaphore()
        for t in (*rings[0].ends, rings[0].peer):
            pl.semaphore_signal(barrier, inc=1, device_id={"dp": t}, device_id_type=pl.DeviceIdType.MESH)
        for t in [owner(s) for s in range(1, n_mp)] + [partner(k) for k in range(rounds)]:
            pl.semaphore_signal(barrier, inc=1, **t)
        pl.semaphore_wait(barrier, 3 + others + rounds)
        for ring in rings:
            ring.sum_begin()
        for c in exchange:
            c.start()
        for ref in (sq, gain, bias):
            ref[...] = jnp.zeros_like(ref)
        for c in fetch:
            c.wait()

    def advance(s):
        for ring in rings:

            def place(d, value, ring=ring):
                ring.full[ring.chunk(chips - 1, d), d] = value
                ring.spread_part(d)

            ring.sum_step(s, place)
            ring.spread_step(s - (chips - 1))

    fold = lambda v: jnp.sum(v.reshape(v.shape[0] // 8, 8, -1), axis=0)
    paced(i, steps, 2 * chips - 1, advance)

    @pl.when(i < first)
    def _():
        here = pl.ds(i * height, height)
        share[here, :] = (nt(own_grad[here, :], wqkv[...]) + back[...]).astype(BF)
        y = (nn(own_context[here, :], wout[...]) + update[...]).astype(BF).astype(F32)
        y = hidden[...].astype(F32) + (y + sum(p[...].astype(F32) for p in sent))
        result[...] = y.astype(BF)
        sq[...] += fold(y * y)

    @pl.when(i == late)
    def _():
        for c in exchange:
            c.wait()

    @pl.when(i >= late)
    def _():
        here = pl.ds((i - late) * tall, tall)
        x = again[...].astype(F32)
        mean = jnp.mean(x, axis=1, keepdims=True)
        centred = x - mean
        var = jnp.mean(centred * centred, axis=1, keepdims=True)
        inv = lax.rsqrt(var + epsilon)
        unit = centred * inv
        full = share[here, :].astype(F32) + sum(got[s, here, :].astype(F32) for s in range(others))
        g = full * scale[...]
        grad[...] = dy[...].astype(F32) + inv * (
            g - jnp.mean(g, axis=1, keepdims=True) - unit * jnp.mean(g * unit, axis=1, keepdims=True)
        )
        gain[...] += fold(full * unit)
        bias[...] += fold(full)

    @pl.when(i == steps - 1)
    def _():
        for ring in rings:
            ring.keep().start()
        lane = lax.broadcasted_iota(jnp.int32, (1, d), 1)
        stats = [jnp.sum(sq[...]), jnp.sum(ctx_sq[...]), sum(jnp.sum(a[...]) for a in acts)]
        kept[0, 0:1, :] = jnp.sum(gain[...], axis=0, keepdims=True)
        kept[0, 1:2, :] = jnp.sum(bias[...], axis=0, keepdims=True)
        kept[0, 2:3, :] = jnp.where(lane == 0, stats[0], jnp.where(lane == 1, stats[1], jnp.where(lane == 2, stats[2], 0.0)))
        kept[0, 3:8, :] = jnp.zeros((5, d), F32)
        for k in range(rounds):
            copy = pltpu.make_async_remote_copy(
                src_ref=kept.at[k], dst_ref=held.at[k], send_sem=send.at[k], recv_sem=recv.at[k], **partner(k)
            )
            copy.start()
            copy.wait()
            kept[k + 1] = kept[k] + held[k]
        sums[...] = kept[rounds]
        for ring in rings:
            ring.sum_finish()
            ring.spread_finish()


def tail(xs, gqkv, context, wqkv, wout, scale, back, update, hidden, dy, sent, shares, acts, ctx_sq, collective_id):
    n_dp, n_mp = lax.axis_size("dp"), lax.axis_size("mp")
    rounds = (n_dp * n_mp).bit_length() - 1
    cuts = [Ring.cut(x) for x in xs]
    shapes = [c.shape for c in cuts]
    rows, d = hidden.shape
    steps, first, late = 16, 8, 4
    any_ = pl.BlockSpec(memory_space=pl.ANY)
    early = pl.BlockSpec((rows // first, d), lambda i: (jnp.minimum(i, first - 1), 0))
    after = pl.BlockSpec((rows // late, d), lambda i: (jnp.maximum(i - (steps - late), 0), 0))
    dma = pltpu.SemaphoreType.DMA
    acc = pltpu.VMEM((8, d), F32)
    result, grad, sums, *totals = pl.pallas_call(
        functools.partial(tail_kernel, steps, n_dp, n_mp, len(acts), shapes),
        grid=(steps,),
        in_specs=[any_, any_, whole(wqkv.shape), whole(wout.shape), whole(scale.shape), early, early, early, after, after]
        + [early] * len(sent) + [any_] * len(shares)
        + [whole(a.shape) for a in acts] + [whole(ctx_sq.shape)] + [any_] * len(xs),
        out_specs=[early, after, pl.BlockSpec((8, d), lambda i: (0, 0))] + [any_] * len(xs),
        out_shape=[struct((rows, d), BF), struct((rows, d), F32), struct((8, d), F32)] + [struct(c, BF) for c in shapes],
        scratch_shapes=[
            pltpu.VMEM((rows, gqkv.shape[1]), BF), pltpu.VMEM((rows, context.shape[1]), BF), dma((2,)),
            pltpu.VMEM((rows, d), BF), pltpu.VMEM((n_mp - 1, rows, d), BF), dma((n_mp - 1,)), dma((n_mp - 1,)),
            acc, acc, acc,
            pltpu.VMEM((rounds, 8, d), F32), pltpu.VMEM((rounds + 1, 8, d), F32), dma((rounds,)), dma((rounds,)),
        ]
        + [r for c in shapes for r in Ring.sum_scratch(c) + Ring.spread_scratch(c)],
        compiler_params=params(collective_id=collective_id, has_side_effects=True),
        cost_estimate=cost(2 * rows * d * (gqkv.shape[1] + context.shape[1]), sum(4 * x.size for x in xs) + 30 * rows * d),
        name="tail",
    )(gqkv, context, wqkv, wout, scale, back, update, hidden, hidden, dy, *sent, *shares, *acts, ctx_sq, *cuts)
    return result, grad, sums, *[t.reshape(x.shape) for t, x in zip(totals, xs)]


def widen_kernel(x, y, x_out, y_out):
    x_out[...] = x[...].astype(F32)
    y_out[...] = jnp.transpose(y[...].astype(F32))


def widen(x, y):
    rows = x.shape[0]
    tile = TILE
    return pl.pallas_call(
        widen_kernel,
        grid=(rows // tile,),
        in_specs=[pl.BlockSpec((tile, x.shape[1]), lambda i: (i, 0)), pl.BlockSpec((tile, y.shape[1]), lambda i: (i, 0))],
        out_specs=[pl.BlockSpec((tile, x.shape[1]), lambda i: (i, 0)), pl.BlockSpec((y.shape[1], tile), lambda i: (0, i))],
        out_shape=[struct(x.shape, F32), struct(y.shape[::-1], F32)],
        compiler_params=params(),
        cost_estimate=cost(0, 6 * (x.size + y.size)),
        name="widen",
    )(x, y)


def norm_kernel(x_ref, scale, bias, out):
    x = x_ref[...].astype(F32)
    mean = jnp.mean(x, axis=1, keepdims=True)
    centred = x - mean
    var = jnp.mean(centred * centred, axis=1, keepdims=True)
    out[...] = (centred * lax.rsqrt(var + epsilon) * scale[...] + bias[...]).astype(BF)


def norm(x, scale, bias):
    rows, d = x.shape
    tile = pl.BlockSpec((min(CHUNK, rows), d), lambda i: (i, 0))
    return pl.pallas_call(
        norm_kernel,
        grid=(rows // min(CHUNK, rows),),
        in_specs=[tile, whole((1, d)), whole((1, d))],
        out_specs=tile,
        out_shape=struct((rows, d), BF),
        compiler_params=params(),
        cost_estimate=cost(10 * rows * d, 4 * rows * d),
        name="norm",
    )(x, scale, bias)


def table_kernel(ends_ref, lens_ref, freq, cos, fwd, back, hot, neg):
    rows = cos.shape[0]
    half = ROT // 2

    def segments(where):
        segment = jnp.zeros(where.shape, jnp.int32)
        start = jnp.zeros(where.shape, jnp.int32)
        for j in range(ends_ref.shape[0]):
            closed = where >= ends_ref[j]
            segment = segment + closed.astype(jnp.int32)
            start = start + jnp.where(closed, lens_ref[j], 0)
        return segment, where - start

    _, offset = segments(lax.broadcasted_iota(jnp.int32, (half, rows), 1))
    angle = offset.astype(F32) * freq[...]
    dim = lax.rem(lax.broadcasted_iota(jnp.int32, (half, LANES), 1), HEAD)
    unit = lax.broadcasted_iota(jnp.int32, (half, LANES), 0)

    def spread(table, mask):
        return lax.dot_general(
            table, jnp.where(mask, 1.0, 0.0), (((0,), (0,)), ((), ())),
            precision=lax.Precision.HIGHEST, preferred_element_type=F32,
        )

    sin = jnp.sin(angle)
    lane = lane_ids(rows)
    cos[...] = jnp.where(lax.rem(lane, HEAD) < ROT, spread(jnp.cos(angle), (dim == unit) | (dim == unit + half)), 1.0)
    fwd[...] = spread(-sin, dim == unit)
    back[...] = spread(sin, dim == unit + half)
    segment, _ = segments(lax.broadcasted_iota(jnp.int32, (rows, LANES), 0))
    same = lane - HEAD == segment
    hot[...] = jnp.where(same, 1.0, 0.0).astype(BF)
    neg[...] = jnp.where(same | (lane < HEAD) | (lane >= HEAD + ends_ref.shape[0]), 0.0, excluded).astype(BF)


def tables(lengths, group_rows):
    half = ROT // 2
    freq = jnp.power(rope_base, -2.0 * jnp.arange(half, dtype=F32) / ROT)[:, None]
    block = pl.BlockSpec((group_rows, LANES), lambda i, *_: (0, 0))
    return pl.pallas_call(
        table_kernel,
        grid_spec=pltpu.PrefetchScalarGridSpec(
            num_scalar_prefetch=2,
            grid=(1,),
            in_specs=[whole((half, 1))],
            out_specs=[block] * 5,
        ),
        out_shape=[struct((group_rows, LANES), F32)] * 3 + [struct((group_rows, LANES), BF)] * 2,
        compiler_params=params(),
        name="tables",
    )(jnp.cumsum(lengths).astype(jnp.int32), lengths, freq)


def on_device(hidden_in, seq_lengths, ln_scale, ln_bias, wqkv, wout, win, wdown, out_grad):
    rows, d = hidden_in.shape
    n = lax.axis_size("mp")
    me = lax.axis_index("mp")
    total = rows * n
    heads = wout.shape[0] // HEAD
    f = win.shape[1]
    after = lambda x, *deps: lax.optimization_barrier((x, *deps))[0]

    normed = norm(hidden_in, ln_scale[None, :], ln_bias[None, :])
    pieces = 2 if rows >= 2 * CHUNK else 1
    high = rows // pieces
    ring = lambda s: [((i + s) % n, i) for i in range(n)]
    slot = [((me + s) % n).astype(jnp.int32)[None] for s in range(n)]
    x_all, dy_all, place = [normed], [out_grad], [slot[0]]
    gate = None
    for s in range(1, n):
        for p in range(pieces):
            mine = [v[p * high : (p + 1) * high] for v in (normed, out_grad)]
            if gate is not None:
                mine = list(lax.optimization_barrier((*mine, *gate))[:2])
            gate = [lax.ppermute(v, "mp", ring(s)) for v in mine]
            x_all.append(gate[0])
            dy_all.append(gate[1])
            place.append(slot[s] * pieces + p)
    index = jnp.concatenate(place)
    table = None

    do, up, back, gdown, gin, sq = feed(slot[0], 0, 1, total, heads, [], normed, out_grad, win, wdown, wout)
    ups, backs, sqs = [up], [back], [sq]
    qkv = []
    order = gdown
    for k in range(1, len(x_all)):
        s, p = 1 + (k - 1) // pieces, (k - 1) % pieces
        last = k == len(x_all) - 1
        if last:
            table = tables(after(seq_lengths[0], order), total)
            for t in range(k):
                qkv = project(place[t], total, heads, qkv, after(x_all[t], order), wqkv, *table)
        prior = [gdown, gin, after(do, *qkv[:1])] + ([ups[s], backs[s]] if p else [])
        do, up, back, gdown, gin, sq = feed(
            place[k], p, pieces, total, heads, prior, x_all[k], dy_all[k], win, wdown, wout
        )
        order = gdown
        ups[s:] = [up]
        backs[s:] = [back]
        sqs.append(sq)
        if last:
            qkv = project(place[k], total, heads, qkv, after(x_all[k], order), wqkv, *table)
    context, wide, keep, ctx_sq, *done = attend(*qkv, [gdown, gin], 4)
    joined = [join(slot[s], False, context, wout, ups[s]) for s in range(1, n)]
    sent = [lax.ppermute(v, "mp", ring(n - s)) for s, v in enumerate(joined, 1)]
    gqkv, gdown, gin = attend_back(*qkv, after(do, *joined), wide, keep, *table[:3], done, [gdown, gin], 3)
    shares = [join(slot[s], True, gqkv, wqkv, backs[s]) for s in range(1, n)]
    gqw, gow, gdown, gin = weight_grads(index, x_all, gqkv, dy_all, context, [gdown, gin])
    result, grad_hidden, sums, gqw, gow = tail(
        [gqw, gow], gqkv, context, wqkv, wout, ln_scale[None, :], backs[0], ups[0], hidden_in, out_grad,
        sent, shares, sqs, ctx_sq, 1,
    )
    gqw, gow = widen(gqw, gow)
    devices = lax.axis_size("dp") * n
    counts = jnp.array([rows * d * devices, rows * d * devices, rows * f * n * devices], F32)
    return (
        result,
        grad_hidden,
        sums[0],
        sums[1],
        gqw,
        gow,
        gin,
        gdown,
        jnp.sqrt(sums[2, :3] / counts),
    )


def solution(mesh):
    tok = P(("dp", "mp"), None)
    cols, rows = P(None, "mp"), P("mp", None)
    return jax.shard_map(
        on_device,
        mesh=mesh,
        in_specs=(tok, P("dp", None), P(), P(), cols, rows, cols, rows, tok),
        out_specs=(tok, tok, P(), P(), cols, rows, cols, rows, P()),
        check_vma=False,
    )
```

```python
import functools

import jax
import jax.numpy as jnp
from jax import lax
from jax.experimental import pallas as pl
from jax.experimental.pallas import tpu as pltpu
from jax.sharding import PartitionSpec as P

HEAD = 64
ROT = 16
LANES = 128
TILE = 256
CHUNK = 512
POINTS = 2
BACK_POINTS = 2
F32 = jnp.float32
BF = jnp.bfloat16

epsilon = 1e-05
rope_base = 10000.0
excluded = -1e20


def nn(a, b):
    return jnp.dot(a, b, preferred_element_type=F32)


def nt(a, b):
    return lax.dot_general(a, b, (((1,), (1,)), ((), ())), preferred_element_type=F32)


def tn(a, b):
    return lax.dot_general(a, b, (((0,), (0,)), ((), ())), preferred_element_type=F32)


def whole(shape):
    zeros = (0,) * len(shape)
    return pl.BlockSpec(shape, lambda *_: zeros, pipeline_mode=pl.Buffered(1))


def struct(shape, dtype):
    return jax.ShapeDtypeStruct(shape, dtype)


def cost(flops, nbytes, trans=0):
    return pl.CostEstimate(flops=int(flops), bytes_accessed=int(nbytes), transcendentals=int(trans))


def params(**kw):
    return pltpu.CompilerParams(vmem_limit_bytes=60 * 2**20, **kw)


def lane_ids(rows):
    return lax.broadcasted_iota(jnp.int32, (rows, LANES), 1)


def turn(x, cos, fwd, back):
    return x * cos + pltpu.roll(x, LANES - ROT // 2, 1) * fwd + pltpu.roll(x, ROT // 2, 1) * back


def gelu_parts(v):
    cdf = 0.5 + 0.5 * lax.erf(v * 0.7071067811865476)
    return v * cdf, cdf + v * jnp.exp(v * v * (-0.5)) * 0.3989422804014327


def ahead(count, product, use):
    held = product(0)
    for i in range(count):
        later = product(i + 1) if i + 1 < count else None
        use(i, held)
        held = later


def project_kernel(slot, nrm, wqkv, cos, fwd, back, hot, neg, *rest):
    q_out, k_out, v_out = rest[-3:]
    rows = nrm.shape[0]
    chunk = min(CHUNK, rows)
    lane = lane_ids(chunk)
    low = lane < HEAD
    one = jnp.where(lane < HEAD + 2, 1.0, 0.0)

    def place(y, r):
        blocks = [y[:, i : i + LANES] for i in range(0, y.shape[1], LANES)]
        sides = []
        for g0, g1, g2 in zip(blocks[::3], blocks[1::3], blocks[2::3]):
            r1, r2 = pltpu.roll(g1, HEAD, 1), pltpu.roll(g2, HEAD, 1)
            sides += [(g0, g1), (jnp.where(low, r1, r2), r2)]
        for h, (qk, v) in enumerate(sides):
            qk = turn(qk, cos[r, :], fwd[r, :], back[r, :])
            q_out[h, r, :] = jnp.where(low, qk * HEAD**-0.5, hot[r, :].astype(F32)).astype(BF)
            k_out[h, r, :] = jnp.where(low, pltpu.roll(qk, HEAD, 1), neg[r, :].astype(F32)).astype(BF)
            v_out[h, r, :] = jnp.where(low, v, one).astype(BF)

    ahead(
        rows // chunk,
        lambda i: nn(nrm[i * chunk : (i + 1) * chunk, :], wqkv[...]),
        lambda i, y: place(y, pl.ds(i * chunk, chunk)),
    )


def project(slot, total, heads, prior, nrm, wqkv, cos, fwd, back, hot, neg):
    rows, d = nrm.shape
    per = 4 if heads % 4 == 0 else 2
    at = pl.BlockSpec((rows, LANES), lambda j, slot: (slot[0], 0), pipeline_mode=pl.Buffered(1))
    hd = pl.BlockSpec((per, rows, LANES), lambda j, slot: (j, slot[0], 0))
    big = struct((heads, total, LANES), BF)
    return pl.pallas_call(
        project_kernel,
        grid_spec=pltpu.PrefetchScalarGridSpec(
            num_scalar_prefetch=1,
            grid=(heads // per,),
            in_specs=[whole(nrm.shape), pl.BlockSpec((d, per * 3 * HEAD), lambda j, slot: (0, j)), at, at, at, at, at]
            + [pl.BlockSpec(memory_space=pl.ANY)] * len(prior),
            out_specs=[hd, hd, hd],
        ),
        out_shape=[big, big, big],
        input_output_aliases={8 + i: i for i in range(len(prior))},
        compiler_params=params(),
        cost_estimate=cost(2 * rows * d * wqkv.shape[1], 2 * (d * wqkv.shape[1] + 6 * rows * d)),
        name="project",
    )(slot, nrm, wqkv, cos, fwd, back, hot, neg, *prior)


def feed_kernel(extra, slot, nrm, dy, win, wdown, wout, *refs):
    prior = refs[:2] if extra else ()
    do_out, update, back, gdown, gin, sq, turned, act, gpre = refs[extra:]
    j = pl.program_id(0)
    rows, d = nrm.shape
    chunk = min(TILE, rows)
    span = [pl.ds(i * chunk, chunk) for i in range(rows // chunk)]

    @pl.when(j == 0)
    def _():
        sq[...] = jnp.zeros_like(sq)
        update[...] = jnp.zeros_like(update)
        back[...] = jnp.zeros_like(back)
        turned[...] = jnp.transpose(nrm[...])
        low = lane_ids(chunk) < HEAD
        for r in span:
            g = nt(dy[r, :], wout[...])
            for p in range(g.shape[1] // LANES):
                y = g[:, p * LANES : (p + 1) * LANES]
                do_out[2 * p, r, :] = jnp.where(low, y, 0.0).astype(BF)
                do_out[2 * p + 1, r, :] = jnp.where(low, pltpu.roll(y, HEAD, 1), 0.0).astype(BF)

    def products(i):
        return nn(nrm[span[i], :], win[...]), nt(dy[span[i], :], wdown[...])

    def use(i, held):
        r = span[i]
        a, slope = gelu_parts(held[0])
        a = a.astype(BF)
        g = (held[1] * slope).astype(BF)
        act[r, :] = a
        gpre[r, :] = g
        wide = a.astype(F32)
        sq[...] += jnp.sum((wide * wide).reshape(chunk // 8, 8, -1), axis=0)
        pass

    ahead(len(span), products, use)
    update[...] += nn(act[...], wdown[...])
    back[...] += nt(gpre[...], win[...])
    down, into = tn(act[...], dy[...]), nn(turned[...], gpre[...])
    if extra:
        down, into = down + prior[0][...].astype(F32), into + prior[1][...].astype(F32)
    gdown[...] = down.astype(BF)
    gin[...] = into.astype(BF)


def feed(slot, piece, pieces, total, heads, prior, nrm, dy, win, wdown, wout):
    rows, d = nrm.shape
    f = win.shape[1]
    tile = min(512, f)
    by_row = pl.BlockSpec((tile, d), lambda j, slot: (j, 0))
    by_col = pl.BlockSpec((d, tile), lambda j, slot: (0, j))
    stay = pl.BlockSpec((rows, d), lambda j, slot: (piece, 0), pipeline_mode=pl.Buffered(1))
    any_ = pl.BlockSpec(memory_space=pl.ANY)
    return pl.pallas_call(
        functools.partial(feed_kernel, len(prior)),
        grid_spec=pltpu.PrefetchScalarGridSpec(
            num_scalar_prefetch=1,
            grid=(f // tile,),
            in_specs=[whole(nrm.shape), whole(dy.shape), by_col, by_row, whole(wout.shape)]
            + [by_row, by_col, any_, any_, any_][: len(prior)],
            out_specs=[
                pl.BlockSpec((heads, rows, LANES), lambda j, slot: (0, slot[0], 0), pipeline_mode=pl.Buffered(1)),
                stay, stay, by_row, by_col,
                pl.BlockSpec((8, tile), lambda j, slot: (0, 0)),
            ],
            scratch_shapes=[pltpu.VMEM((d, rows), BF), pltpu.VMEM((rows, tile), BF), pltpu.VMEM((rows, tile), BF)],
        ),
        out_shape=[
            struct((heads, total, LANES), BF),
            struct((rows * pieces, d), F32), struct((rows * pieces, d), F32),
            struct((f, d), BF), struct((d, f), BF),
            struct((8, tile), F32),
        ],
        input_output_aliases={8 + i: i for i in range(len(prior) - 2)},
        compiler_params=params(),
        cost_estimate=cost(12 * rows * d * f, 12 * d * f + 20 * rows * d),
        name="feed",
    )(slot, nrm, dy, win, wdown, wout, *prior)


def attend_kernel(pairs, shapes, q_ref, k_ref, v_ref, *refs):
    count = len(shapes)
    xs, (ctx, wide, keep, sq), done, refs = refs[:count], refs[count : count + 4], refs[count + 4 : 2 * count + 4], refs[2 * count + 4 :]
    hold, (sems,), refs = refs[:count], refs[count : count + 1], refs[count + 1 :]
    names = Ring.SUM
    rings = [
        Ring(shape, x=xs[k], **dict(zip(names, refs[k * len(names) : (k + 1) * len(names)])))
        for k, shape in enumerate(shapes)
    ]
    chips = rings[0].chips

    def advance(s):
        for k, ring in enumerate(rings):

            def place(d, value, k=k):
                hold[k][d] = value

            ring.sum_step(s, place)

    @pl.when(pl.program_id(0) == 0)
    def _():
        rings[0].meet()
        for ring in rings:
            ring.sum_begin()

    total = q_ref.shape[1]
    b = TILE
    tri = lax.broadcasted_iota(jnp.int32, (b, b), 0) >= lax.broadcasted_iota(jnp.int32, (b, b), 1)
    low = lane_ids(b) < HEAD

    @pl.when(pl.program_id(0) == 0)
    def _():
        sq[...] = jnp.zeros_like(sq)

    def scores(h, i):
        return nt(q_ref[h, i * b : (i + 1) * b, :], k_ref[h, : (i + 1) * b, :])

    def weights(s, h, i):
        s_diag = jnp.where(tri, s[:, i * b :], excluded)
        top = jnp.max(s_diag, axis=1, keepdims=True)
        if i:
            top = jnp.maximum(top, jnp.max(s[:, : i * b], axis=1, keepdims=True))
        w = jnp.exp(s_diag - top).astype(BF)
        if i:
            w = jnp.concatenate([jnp.exp(s[:, : i * b] - top).astype(BF), w], axis=1)
        for j in range(i + 1):
            keep[h, i * (i + 1) // 2 + j] = w[:, j * b : (j + 1) * b]
        return w

    def finish(w, h, i):
        rows = pl.ds(i * b, b)
        acc = nn(w, v_ref[h, : (i + 1) * b, :])
        inv = 1.0 / acc[:, HEAD : HEAD + 1]
        acc = acc * inv
        wide[h, rows, :] = jnp.where(low, acc, inv)
        return acc

    items = [(h, i) for i in range(total // b) for h in range(2)]
    places = Places(POINTS, sum(i + 1 for _, i in items), pairs, chips, advance)
    s = scores(*items[0])
    left = None
    for t, (h, i) in enumerate(items):
        s_next = scores(*items[t + 1]) if t + 1 < len(items) else None
        acc = finish(weights(s, h, i), h, i)
        if h == 0:
            left = acc
        else:
            both = jnp.where(low, left, pltpu.roll(acc, HEAD, 1)).astype(BF)
            ctx[i * b : (i + 1) * b, :] = both
            both = both.astype(F32)
            sq[...] += jnp.sum((both * both).reshape(b // 8, 8, LANES), axis=0)
        s = s_next
        places.add(i + 1)

    @pl.when(pl.program_id(0) == pairs - 1)
    def _():
        out = [pltpu.make_async_copy(hold[k], done[k], sems.at[k]) for k in range(count)]
        for c in out:
            c.start()
        for ring in rings:
            ring.sum_finish()
        for c in out:
            c.wait()


def attend(q, k, v, xs, collective_id):
    cuts = [Ring.cut(x) for x in xs]
    shapes = [c.shape for c in cuts]
    any_ = pl.BlockSpec(memory_space=pl.ANY)
    heads, total, _ = q.shape
    tiles = total // TILE
    tiles = tiles * (tiles + 1) // 2
    hd = pl.BlockSpec((2, total, LANES), lambda p: (p, 0, 0))
    return pl.pallas_call(
        functools.partial(attend_kernel, heads // 2, shapes),
        grid=(heads // 2,),
        in_specs=[hd, hd, hd] + [any_] * len(xs),
        out_specs=[
            pl.BlockSpec((total, LANES), lambda p: (0, p)),
            hd,
            pl.BlockSpec((2, tiles, TILE, TILE), lambda p: (p, 0, 0, 0)),
            pl.BlockSpec((8, LANES), lambda p: (0, 0)),
        ]
        + [any_] * len(xs),
        out_shape=[
            struct((total, heads * HEAD), BF),
            struct((heads, total, LANES), F32),
            struct((heads, tiles, TILE, TILE), BF),
            struct((8, LANES), F32),
        ]
        + [struct(c[2:], BF) for c in shapes],
        scratch_shapes=[pltpu.VMEM(c[2:], BF) for c in shapes]
        + [pltpu.SemaphoreType.DMA((len(xs),))]
        + [r for c in shapes for r in Ring.sum_scratch(c)],
        compiler_params=params(collective_id=collective_id, has_side_effects=True),
        cost_estimate=cost(4 * heads * tiles * TILE * TILE * 256, heads * total * LANES * 20, heads * tiles * TILE * TILE),
        name="attend",
    )(q, k, v, *cuts)


def attend_back_kernel(pairs, shapes, q_ref, k_ref, v_ref, do_ref, wide, keep, cos, fwd, back, *refs):
    count = len(shapes)
    done, out, totals, refs = refs[:count], refs[count], refs[count + 1 : 2 * count + 1], refs[2 * count + 1 :]
    (dk_acc, dv_acc, dq_acc, sems), refs = refs[:4], refs[4:]
    hold, refs = refs[:count], refs[count:]
    names = Ring.SPREAD
    rings = [
        Ring(shape, out=totals[k], **dict(zip(names, refs[k * len(names) : (k + 1) * len(names)])))
        for k, shape in enumerate(shapes)
    ]
    chips = rings[0].chips

    @pl.when(pl.program_id(0) == 0)
    def _():
        loads = [pltpu.make_async_copy(done[k], hold[k], sems.at[k]) for k in range(count)]
        for c in loads:
            c.start()
        rings[0].meet()
        for k, ring in enumerate(rings):
            loads[k].wait()
            for d in range(ring.parts):
                ring.full[ring.chunk(chips - 1, d), d] = hold[k][d]
                ring.spread_part(d)

    def advance(s):
        for ring in rings:
            ring.spread_step(s + 1)

    total = q_ref.shape[1]
    b = TILE
    lane = lane_ids(b)
    low = lane < HEAD

    def probs(h, i):
        w = [keep[h, i * (i + 1) // 2 + j] for j in range(i + 1)]
        return w[0] if i == 0 else jnp.concatenate(w, axis=1)

    def begin(h, i):
        rows = pl.ds(i * b, b)
        context = wide[h, rows, :]
        inv = context[:, HEAD : HEAD + 1]
        scaled = (do_ref[h, rows, :].astype(F32) * inv).astype(BF)
        grad = scaled.astype(F32)
        delta = jnp.sum(jnp.where(low, grad * context, 0.0), axis=1, keepdims=True)
        delta_hi = delta.astype(BF).astype(F32)
        delta_lo = delta - delta_hi
        joined = jnp.where(lane == HEAD, -delta_hi, jnp.where(lane == HEAD + 1, -delta_lo, grad)).astype(BF)
        return scaled, nt(joined, v_ref[h, : (i + 1) * b, :])

    def finish(h, i, scaled, dp):
        n = (i + 1) * b
        rows = pl.ds(i * b, b)
        w = probs(h, i)
        ds = w * dp.astype(BF)
        dq_acc[h, rows, :] = nn(ds, k_ref[h, :n, :]) * HEAD**-0.5
        dk = tn(ds, q_ref[h, rows, :])
        dv = tn(w, scaled)
        if i:
            dk_acc[h, : i * b, :] += dk[: i * b]
            dv_acc[h, : i * b, :] += dv[: i * b]
        dk_acc[h, rows, :] = dk[i * b :]
        dv_acc[h, rows, :] = dv[i * b :]

    items = [(h, i) for i in range(total // b) for h in range(2)]
    places = Places(BACK_POINTS, sum(i + 1 for _, i in items), pairs, chips - 1, advance)
    state = begin(*items[0])
    for t, item in enumerate(items):
        later = begin(*items[t + 1]) if t + 1 < len(items) else None
        finish(*item, *state)
        state = later
        places.add(item[1] + 1)
    for i in range(total // b):
        rows = pl.ds(i * b, b)
        x = [
            turn(
                jnp.where(low, dq_acc[h, rows, :], pltpu.roll(dk_acc[h, rows, :], HEAD, 1)),
                cos[rows, :], -fwd[rows, :], -back[rows, :],
            )
            for h in range(2)
        ]
        r = pltpu.roll(x[1], HEAD, 1)
        out[rows, :LANES] = x[0].astype(BF)
        out[rows, LANES : 2 * LANES] = jnp.where(low, dv_acc[0, rows, :], r).astype(BF)
        out[rows, 2 * LANES :] = jnp.where(low, r, pltpu.roll(dv_acc[1, rows, :], HEAD, 1)).astype(BF)

    @pl.when(pl.program_id(0) == pairs - 1)
    def _():
        for ring in rings:
            ring.keep().start()
        for ring in rings:
            ring.spread_finish()


def attend_back(q, k, v, do, wide, keep, cos, fwd, back, done, likes, collective_id):
    shapes = [jax.eval_shape(Ring.cut, x).shape for x in likes]
    any_ = pl.BlockSpec(memory_space=pl.ANY)
    heads, total, _ = q.shape
    hd = pl.BlockSpec((2, total, LANES), lambda p: (p, 0, 0))
    acc = pltpu.VMEM((2, total, LANES), F32)
    tiles = keep.shape[1]
    grad, *totals = pl.pallas_call(
        functools.partial(attend_back_kernel, heads // 2, shapes),
        grid=(heads // 2,),
        in_specs=[hd, hd, hd, hd, hd, pl.BlockSpec((2,) + keep.shape[1:], lambda p: (p, 0, 0, 0))]
        + [whole(cos.shape)] * 3
        + [any_] * len(done),
        out_specs=[pl.BlockSpec((total, 384), lambda p: (0, p))] + [any_] * len(done),
        out_shape=[struct((total, heads * 3 * HEAD), BF)] + [struct(c, BF) for c in shapes],
        scratch_shapes=[acc] * 3
        + [pltpu.SemaphoreType.DMA((len(done),))]
        + [pltpu.VMEM(c[2:], BF) for c in shapes]
        + [r for c in shapes for r in Ring.spread_scratch(c)],
        compiler_params=params(collective_id=collective_id, has_side_effects=True),
        cost_estimate=cost(8 * heads * tiles * TILE * TILE * 256, heads * total * LANES * 40),
        name="attend_back",
    )(q, k, v, do, wide, keep, cos, fwd, back, *done)
    return grad, *[t.reshape(x.shape) for t, x in zip(totals, likes)]


def join_kernel(transposed, slot, a, b, c, out):
    out[...] = ((nt if transposed else nn)(a[...], b[...]) + c[...]).astype(BF)


def join(slot, transposed, a, b, c):
    rows, width = c.shape
    tile = min(CHUNK, rows)
    step = pl.BlockSpec((tile, width), lambda i, slot: (i, 0))
    return pl.pallas_call(
        functools.partial(join_kernel, transposed),
        grid_spec=pltpu.PrefetchScalarGridSpec(
            num_scalar_prefetch=1,
            grid=(rows // tile,),
            in_specs=[
                pl.BlockSpec((tile, a.shape[1]), lambda i, slot: (slot[0] * (rows // tile) + i, 0)),
                whole(b.shape),
                step,
            ],
            out_specs=step,
        ),
        out_shape=struct((rows, width), BF),
        compiler_params=params(),
        cost_estimate=cost(2 * rows * width * a.shape[1], 2 * (b.size + rows * (3 * width + a.shape[1]))),
        name="join",
    )(slot, a, b, c)


def weight_kernel(n, index, *refs):
    groups, (widen, outs) = [refs[i * n : (i + 1) * n] for i in range(4)], (refs[4 * n : 4 * n + 2], refs[4 * n + 2 :])
    for x, out in zip(widen, outs[2:]):
        out[...] = x[...].astype(F32)
    for xs, ys, out in ((groups[0], groups[1], outs[0]), (groups[2], groups[3], outs[1])):
        width = out.shape[1]
        step = 512 if width % 512 == 0 else 128
        for c in range(width // step):
            cols = pl.ds(c * step, step)
            out[:, cols] = sum(tn(x[...], y[:, cols]) for x, y in zip(xs, ys)).astype(BF)


def weight_grads(index, x1, y1, x2, y2, widen):
    n, d = len(x1), x1[0].shape[1]
    tile = 256
    left = [pl.BlockSpec((x.shape[0], tile), lambda j, index: (0, j)) for x in x1]
    right = lambda y: [
        pl.BlockSpec(
            (x.shape[0], y.shape[1]), functools.partial(lambda s, j, index: (index[s], 0), s), pipeline_mode=pl.Buffered(1)
        )
        for s, x in enumerate(x1)
    ]
    widths = (y1.shape[1], y2.shape[1])
    wide = [pl.BlockSpec((x.shape[0] * tile // d, x.shape[1]), lambda j, index: (j, 0)) for x in widen]
    return pl.pallas_call(
        functools.partial(weight_kernel, n),
        grid_spec=pltpu.PrefetchScalarGridSpec(
            num_scalar_prefetch=1,
            grid=(d // tile,),
            in_specs=left + right(y1) + left + right(y2) + wide,
            out_specs=[pl.BlockSpec((tile, w), lambda j, index: (j, 0)) for w in widths] + wide,
        ),
        out_shape=[struct((d, w), BF) for w in widths] + [struct(x.shape, F32) for x in widen],
        compiler_params=params(),
        cost_estimate=cost(2 * y1.shape[0] * d * sum(widths), 2 * y1.shape[0] * (2 * d + sum(widths)) + 2 * d * sum(widths)),
        name="weight_grads",
    )(index, *x1, *[y1] * n, *x2, *[y2] * n, *widen)


class Ring:
    SUM = ("near", "part", "far", "own_sem", "core_sem", "rs_send", "rs_recv")
    SPREAD = ("full", "keep_sem", "ag_send", "ag_recv", "fin_send", "fin_recv")

    def __init__(self, shape, **refs):
        self.__dict__.update(refs)
        self.chips, self.parts = shape[1], shape[2]
        dp = lax.axis_index("dp")
        self.core, chip = lax.rem(dp, 2), dp // 2
        y, z = lax.rem(chip, 2), chip // 2
        self.p = z * (1 - y) + (self.chips - 1 - z) * y
        self.peer = dp + 1 - 2 * self.core
        self.ends = [self.device(lax.rem(self.p + 1, self.chips)), self.device(lax.rem(self.p + self.chips - 1, self.chips))]

    @staticmethod
    def sum_scratch(shape):
        chips, parts = shape[1], shape[2]
        dma = pltpu.SemaphoreType.DMA
        half = pltpu.VMEM(shape[1:], BF)
        return [half, half, pltpu.VMEM((chips - 1,) + shape[2:], BF), dma((1,)), dma((2, chips)), dma((chips - 1, parts)), dma((chips - 1, parts))]

    @staticmethod
    def spread_scratch(shape):
        chips, parts = shape[1], shape[2]
        dma = pltpu.SemaphoreType.DMA
        return [pltpu.VMEM(shape[1:], BF), dma((1,))] + [dma((chips - 1, parts))] * 2 + [dma((chips, parts))] * 2

    @staticmethod
    def cut(x):
        chips = lax.axis_size("dp") // 2
        rows, d = x.shape
        parts = min(4, rows // (32 * chips))
        return x.reshape(2, chips, parts, rows // (2 * chips * parts), d)

    def device(self, pos):
        high = pos // (self.chips // 2)
        return ((1 - high) * 2 * pos + high * (2 * (self.chips - 1 - pos) + 1)) * 2 + self.core

    def remote(self, src, dst, send, recv, t):
        return pltpu.make_async_remote_copy(
            src_ref=src, dst_ref=dst, send_sem=send, recv_sem=recv,
            device_id={"dp": t}, device_id_type=pl.DeviceIdType.MESH,
        )

    def chunk(self, s, d):
        return lax.rem(self.p + 2 * self.chips - s, self.chips) if d % 2 == 0 else lax.rem(self.p + s, self.chips)

    def swap(self, c):
        return self.remote(
            self.x.at[1 - self.core, c], self.near.at[c], self.core_sem.at[0, c], self.core_sem.at[1, c], self.peer
        )

    def reduce(self, s, d):
        return self.remote(
            self.part.at[self.chunk(s, d), d], self.far.at[s, d], self.rs_send.at[s, d], self.rs_recv.at[s, d], self.ends[d % 2]
        )

    def gather(self, s, d):
        ref = self.full.at[self.chunk(self.chips - 1 + s, d), d]
        return self.remote(ref, ref, self.ag_send.at[s, d], self.ag_recv.at[s, d], self.ends[d % 2])

    def across(self, s, d, half):
        c = self.chunk(self.chips - 1 + s, d)
        return self.remote(self.full.at[c, d], self.out.at[half, c, d], self.fin_send.at[s, d], self.fin_recv.at[s, d], self.peer)

    def mine(self):
        return pltpu.make_async_copy(self.x.at[self.core], self.part, self.own_sem.at[0])

    def keep(self):
        return pltpu.make_async_copy(self.full, self.out.at[self.core], self.keep_sem.at[0])

    @staticmethod
    def add(a, b):
        return (a.astype(F32) + b.astype(F32)).astype(BF)

    def meet(self):
        barrier = pltpu.get_barrier_semaphore()
        for t in (*self.ends, self.peer):
            pl.semaphore_signal(barrier, inc=1, device_id={"dp": t}, device_id_type=pl.DeviceIdType.MESH)
        pl.semaphore_wait(barrier, 3)

    def sum_begin(self):
        self.mine().start()
        for c in range(self.chips):
            self.swap(c).start()

    def sum_step(self, s, place):
        chips, parts, part, far = self.chips, range(self.parts), self.part, self.far

        @pl.when(s == 0)
        def _():
            self.mine().wait()

            def settle(c, carry):
                self.swap(c).wait_recv()
                part[c] = self.add(part[c], self.near[c])
                return carry

            lax.fori_loop(0, chips, settle, 0)
            for d in parts:
                self.reduce(0, d).start()

        @pl.when((s > 0) & (s < chips - 1))
        def _():
            for d in parts:
                self.reduce(s - 1, d).wait_recv()
                c = self.chunk(s, d)
                part[c, d] = self.add(part[c, d], far[s - 1, d])
                self.reduce(s, d).start()

        @pl.when(s == chips - 1)
        def _():
            for d in parts:
                self.reduce(chips - 2, d).wait_recv()
                place(d, self.add(part[self.chunk(chips - 1, d), d], far[chips - 2, d]))

    def sum_finish(self):
        for c in range(self.chips):
            self.swap(c).wait_send()
        for d in range(self.parts):
            for s in range(self.chips - 1):
                self.reduce(s, d).wait_send()

    def spread_part(self, d):
        self.gather(0, d).start()
        self.across(0, d, self.core).start()

    def spread_step(self, s):
        chips, parts = self.chips, range(self.parts)

        @pl.when((s > 0) & (s < chips - 1))
        def _():
            for d in parts:
                self.gather(s - 1, d).wait_recv()
                self.gather(s, d).start()
                self.across(s, d, self.core).start()

        @pl.when(s == chips - 1)
        def _():
            for d in parts:
                self.gather(chips - 2, d).wait_recv()
                self.across(chips - 1, d, self.core).start()

    def spread_finish(self):
        for d in range(self.parts):
            for s in range(self.chips - 1):
                self.gather(s, d).wait_send()
            for s in range(self.chips):
                self.across(s, d, self.core).wait_send()
                self.across(s, d, 1 - self.core).wait_recv()
        self.keep().wait()


def paced(place, places, limit, step):
    upto = lambda k: (k * limit + places - 1) // places
    lax.fori_loop(upto(place), upto(place + 1), lambda s, carry: (step(s), carry)[1], 0)


class Places:
    def __init__(self, points, work, per_grid, limit, step):
        self.points, self.total, self.work, self.limit, self.step = points, points * per_grid, work, limit, step
        self.done = self.point = 0

    def add(self, work):
        self.done += work
        if self.done * self.points >= (self.point + 1) * self.work:
            paced(pl.program_id(0) * self.points + self.point, self.total, self.limit, self.step)
            self.point += 1


def tail_kernel(steps, n_dp, n_mp, counts, shapes, gqkv, context, wqkv, wout, scale, back, update, hidden, again, dy, *refs):
    refs = list(refs)
    take = lambda k: [refs.pop(0) for _ in range(k)]
    others, squares = n_mp - 1, counts
    sent, shares, acts, (ctx_sq,), xs = take(others), take(others), take(squares), take(1), take(len(shapes))
    result, grad, sums = take(3)
    outs = take(len(shapes))
    own_grad, own_context, sems, share, got, ex_send, ex_recv, sq, gain, bias, held, kept, send, recv = take(14)
    names = Ring.SUM + Ring.SPREAD
    rings = [Ring(shape, x=x, out=out, **dict(zip(names, take(len(names))))) for shape, x, out in zip(shapes, xs, outs)]
    chips = rings[0].chips
    i = pl.program_id(0)
    rows, d = share.shape
    height, tall = back.shape[0], again.shape[0]
    first, late = rows // height, steps - rows // tall
    mp = lax.axis_index("mp")
    me = lax.axis_index("dp") * n_mp + mp
    rounds = held.shape[0]
    base = pl.ds(mp * rows, rows)
    fetch = [
        pltpu.make_async_copy(gqkv.at[base], own_grad, sems.at[0]),
        pltpu.make_async_copy(context.at[base], own_context, sems.at[1]),
    ]

    def owner(s):
        return dict(device_id={"mp": lax.rem(mp + s, n_mp)}, device_id_type=pl.DeviceIdType.MESH)

    def partner(k):
        t = me + 2**k * (1 - 2 * lax.rem(me // 2**k, 2))
        return dict(device_id={"dp": t // n_mp, "mp": lax.rem(t, n_mp)}, device_id_type=pl.DeviceIdType.MESH)

    exchange = [
        pltpu.make_async_remote_copy(
            src_ref=shares[s - 1], dst_ref=got.at[s - 1], send_sem=ex_send.at[s - 1], recv_sem=ex_recv.at[s - 1], **owner(s)
        )
        for s in range(1, n_mp)
    ]

    @pl.when(i == 0)
    def _():
        for c in fetch:
            c.start()
        barrier = pltpu.get_barrier_semaphore()
        for t in (*rings[0].ends, rings[0].peer):
            pl.semaphore_signal(barrier, inc=1, device_id={"dp": t}, device_id_type=pl.DeviceIdType.MESH)
        for t in [owner(s) for s in range(1, n_mp)] + [partner(k) for k in range(rounds)]:
            pl.semaphore_signal(barrier, inc=1, **t)
        pl.semaphore_wait(barrier, 3 + others + rounds)
        for ring in rings:
            ring.sum_begin()
        for c in exchange:
            c.start()
        for ref in (sq, gain, bias):
            ref[...] = jnp.zeros_like(ref)
        for c in fetch:
            c.wait()

    def advance(s):
        for ring in rings:

            def place(d, value, ring=ring):
                ring.full[ring.chunk(chips - 1, d), d] = value
                ring.spread_part(d)

            ring.sum_step(s, place)
            ring.spread_step(s - (chips - 1))

    fold = lambda v: jnp.sum(v.reshape(v.shape[0] // 8, 8, -1), axis=0)
    paced(i, steps, 2 * chips - 1, advance)

    @pl.when(i < first)
    def _():
        here = pl.ds(i * height, height)
        share[here, :] = (nt(own_grad[here, :], wqkv[...]) + back[...]).astype(BF)
        y = (nn(own_context[here, :], wout[...]) + update[...]).astype(BF).astype(F32)
        y = hidden[...].astype(F32) + (y + sum(p[...].astype(F32) for p in sent))
        result[...] = y.astype(BF)
        sq[...] += fold(y * y)

    @pl.when(i == late)
    def _():
        for c in exchange:
            c.wait()

    @pl.when(i >= late)
    def _():
        here = pl.ds((i - late) * tall, tall)
        x = again[...].astype(F32)
        mean = jnp.mean(x, axis=1, keepdims=True)
        centred = x - mean
        var = jnp.mean(centred * centred, axis=1, keepdims=True)
        inv = lax.rsqrt(var + epsilon)
        unit = centred * inv
        full = share[here, :].astype(F32) + sum(got[s, here, :].astype(F32) for s in range(others))
        g = full * scale[...]
        grad[...] = dy[...].astype(F32) + inv * (
            g - jnp.mean(g, axis=1, keepdims=True) - unit * jnp.mean(g * unit, axis=1, keepdims=True)
        )
        gain[...] += fold(full * unit)
        bias[...] += fold(full)

    @pl.when(i == steps - 1)
    def _():
        for ring in rings:
            ring.keep().start()
        lane = lax.broadcasted_iota(jnp.int32, (1, d), 1)
        stats = [jnp.sum(sq[...]), jnp.sum(ctx_sq[...]), sum(jnp.sum(a[...]) for a in acts)]
        kept[0, 0:1, :] = jnp.sum(gain[...], axis=0, keepdims=True)
        kept[0, 1:2, :] = jnp.sum(bias[...], axis=0, keepdims=True)
        kept[0, 2:3, :] = jnp.where(lane == 0, stats[0], jnp.where(lane == 1, stats[1], jnp.where(lane == 2, stats[2], 0.0)))
        kept[0, 3:8, :] = jnp.zeros((5, d), F32)
        for k in range(rounds):
            copy = pltpu.make_async_remote_copy(
                src_ref=kept.at[k], dst_ref=held.at[k], send_sem=send.at[k], recv_sem=recv.at[k], **partner(k)
            )
            copy.start()
            copy.wait()
            kept[k + 1] = kept[k] + held[k]
        sums[...] = kept[rounds]
        for ring in rings:
            ring.sum_finish()
            ring.spread_finish()


def tail(xs, gqkv, context, wqkv, wout, scale, back, update, hidden, dy, sent, shares, acts, ctx_sq, collective_id):
    n_dp, n_mp = lax.axis_size("dp"), lax.axis_size("mp")
    rounds = (n_dp * n_mp).bit_length() - 1
    cuts = [Ring.cut(x) for x in xs]
    shapes = [c.shape for c in cuts]
    rows, d = hidden.shape
    steps, first, late = 16, 8, 4
    any_ = pl.BlockSpec(memory_space=pl.ANY)
    early = pl.BlockSpec((rows // first, d), lambda i: (jnp.minimum(i, first - 1), 0))
    after = pl.BlockSpec((rows // late, d), lambda i: (jnp.maximum(i - (steps - late), 0), 0))
    dma = pltpu.SemaphoreType.DMA
    acc = pltpu.VMEM((8, d), F32)
    result, grad, sums, *totals = pl.pallas_call(
        functools.partial(tail_kernel, steps, n_dp, n_mp, len(acts), shapes),
        grid=(steps,),
        in_specs=[any_, any_, whole(wqkv.shape), whole(wout.shape), whole(scale.shape), early, early, early, after, after]
        + [early] * len(sent) + [any_] * len(shares)
        + [whole(a.shape) for a in acts] + [whole(ctx_sq.shape)] + [any_] * len(xs),
        out_specs=[early, after, pl.BlockSpec((8, d), lambda i: (0, 0))] + [any_] * len(xs),
        out_shape=[struct((rows, d), BF), struct((rows, d), F32), struct((8, d), F32)] + [struct(c, BF) for c in shapes],
        scratch_shapes=[
            pltpu.VMEM((rows, gqkv.shape[1]), BF), pltpu.VMEM((rows, context.shape[1]), BF), dma((2,)),
            pltpu.VMEM((rows, d), BF), pltpu.VMEM((n_mp - 1, rows, d), BF), dma((n_mp - 1,)), dma((n_mp - 1,)),
            acc, acc, acc,
            pltpu.VMEM((rounds, 8, d), F32), pltpu.VMEM((rounds + 1, 8, d), F32), dma((rounds,)), dma((rounds,)),
        ]
        + [r for c in shapes for r in Ring.sum_scratch(c) + Ring.spread_scratch(c)],
        compiler_params=params(collective_id=collective_id, has_side_effects=True),
        cost_estimate=cost(2 * rows * d * (gqkv.shape[1] + context.shape[1]), sum(4 * x.size for x in xs) + 30 * rows * d),
        name="tail",
    )(gqkv, context, wqkv, wout, scale, back, update, hidden, hidden, dy, *sent, *shares, *acts, ctx_sq, *cuts)
    return result, grad, sums, *[t.reshape(x.shape) for t, x in zip(totals, xs)]


def widen_kernel(x, y, x_out, y_out):
    x_out[...] = x[...].astype(F32)
    y_out[...] = jnp.transpose(y[...].astype(F32))


def widen(x, y):
    rows = x.shape[0]
    tile = TILE
    return pl.pallas_call(
        widen_kernel,
        grid=(rows // tile,),
        in_specs=[pl.BlockSpec((tile, x.shape[1]), lambda i: (i, 0)), pl.BlockSpec((tile, y.shape[1]), lambda i: (i, 0))],
        out_specs=[pl.BlockSpec((tile, x.shape[1]), lambda i: (i, 0)), pl.BlockSpec((y.shape[1], tile), lambda i: (0, i))],
        out_shape=[struct(x.shape, F32), struct(y.shape[::-1], F32)],
        compiler_params=params(),
        cost_estimate=cost(0, 6 * (x.size + y.size)),
        name="widen",
    )(x, y)


def norm_kernel(x_ref, dy, scale, bias, out, *copies):
    x = x_ref[...].astype(F32)
    mean = jnp.mean(x, axis=1, keepdims=True)
    centred = x - mean
    var = jnp.mean(centred * centred, axis=1, keepdims=True)
    y = (centred * lax.rsqrt(var + epsilon) * scale[...] + bias[...]).astype(BF)
    out[...] = y
    for p in range(len(copies) // 2):

        @pl.when(pl.program_id(0) == p)
        def _(p=p):
            copies[2 * p][...] = y
            copies[2 * p + 1][...] = dy[...]


def norm(x, dy, scale, bias, pieces):
    rows, d = x.shape
    high = rows // pieces
    tile = pl.BlockSpec((high, d), lambda i: (i, 0))
    copies = 2 * pieces if pieces > 1 else 0
    return pl.pallas_call(
        norm_kernel,
        grid=(pieces,),
        in_specs=[tile, tile, whole((1, d)), whole((1, d))],
        out_specs=[tile] + [whole((high, d))] * copies,
        out_shape=[struct((rows, d), BF)] + [struct((high, d), BF)] * copies,
        compiler_params=params(),
        cost_estimate=cost(10 * rows * d, 10 * rows * d),
        name="norm",
    )(x, dy, scale, bias)


def table_kernel(ends_ref, lens_ref, freq, cos, fwd, back, hot, neg):
    rows = cos.shape[0]
    half = ROT // 2

    def segments(where):
        segment = jnp.zeros(where.shape, jnp.int32)
        start = jnp.zeros(where.shape, jnp.int32)
        for j in range(ends_ref.shape[0]):
            closed = where >= ends_ref[j]
            segment = segment + closed.astype(jnp.int32)
            start = start + jnp.where(closed, lens_ref[j], 0)
        return segment, where - start

    _, offset = segments(lax.broadcasted_iota(jnp.int32, (half, rows), 1))
    angle = offset.astype(F32) * freq[...]
    dim = lax.rem(lax.broadcasted_iota(jnp.int32, (half, LANES), 1), HEAD)
    unit = lax.broadcasted_iota(jnp.int32, (half, LANES), 0)

    def spread(table, mask):
        return lax.dot_general(
            table, jnp.where(mask, 1.0, 0.0), (((0,), (0,)), ((), ())),
            precision=lax.Precision.HIGHEST, preferred_element_type=F32,
        )

    sin = jnp.sin(angle)
    lane = lane_ids(rows)
    cos[...] = jnp.where(lax.rem(lane, HEAD) < ROT, spread(jnp.cos(angle), (dim == unit) | (dim == unit + half)), 1.0)
    fwd[...] = spread(-sin, dim == unit)
    back[...] = spread(sin, dim == unit + half)
    segment, _ = segments(lax.broadcasted_iota(jnp.int32, (rows, LANES), 0))
    same = lane - HEAD == segment
    hot[...] = jnp.where(same, 1.0, 0.0).astype(BF)
    neg[...] = jnp.where(same | (lane < HEAD) | (lane >= HEAD + ends_ref.shape[0]), 0.0, excluded).astype(BF)


def tables(lengths, group_rows):
    half = ROT // 2
    freq = jnp.power(rope_base, -2.0 * jnp.arange(half, dtype=F32) / ROT)[:, None]
    block = pl.BlockSpec((group_rows, LANES), lambda i, *_: (0, 0))
    return pl.pallas_call(
        table_kernel,
        grid_spec=pltpu.PrefetchScalarGridSpec(
            num_scalar_prefetch=2,
            grid=(1,),
            in_specs=[whole((half, 1))],
            out_specs=[block] * 5,
        ),
        out_shape=[struct((group_rows, LANES), F32)] * 3 + [struct((group_rows, LANES), BF)] * 2,
        compiler_params=params(),
        name="tables",
    )(jnp.cumsum(lengths).astype(jnp.int32), lengths, freq)


def on_device(hidden_in, seq_lengths, ln_scale, ln_bias, wqkv, wout, win, wdown, out_grad):
    rows, d = hidden_in.shape
    n = lax.axis_size("mp")
    me = lax.axis_index("mp")
    total = rows * n
    heads = wout.shape[0] // HEAD
    f = win.shape[1]
    after = lambda x, *deps: lax.optimization_barrier((x, *deps))[0]

    pieces = 2 if rows >= 2 * CHUNK else 1
    normed, *copies = norm(hidden_in, out_grad, ln_scale[None, :], ln_bias[None, :], pieces)
    copies = copies or [normed, out_grad]
    ring = lambda s: [((i + s) % n, i) for i in range(n)]
    slot = [((me + s) % n).astype(jnp.int32)[None] for s in range(n)]
    x_all, dy_all, place = [normed], [out_grad], [slot[0]]
    gate = None
    for s in range(1, n):
        for p in range(pieces):
            mine = copies[2 * p : 2 * p + 2]
            if gate is not None:
                mine = list(lax.optimization_barrier((*mine, *gate))[:2])
            gate = [lax.ppermute(v, "mp", ring(s)) for v in mine]
            x_all.append(gate[0])
            dy_all.append(gate[1])
            place.append(slot[s] * pieces + p)
    index = jnp.concatenate(place)
    table = None

    do, up, back, gdown, gin, sq = feed(slot[0], 0, 1, total, heads, [], normed, out_grad, win, wdown, wout)
    ups, backs, sqs = [up], [back], [sq]
    qkv = []
    order = gdown
    for k in range(1, len(x_all)):
        s, p = 1 + (k - 1) // pieces, (k - 1) % pieces
        last = k == len(x_all) - 1
        if last:
            table = tables(after(seq_lengths[0], order), total)
            for t in range(k):
                qkv = project(place[t], total, heads, qkv, after(x_all[t], order), wqkv, *table)
        prior = [gdown, gin, after(do, *qkv[:1])] + ([ups[s], backs[s]] if p else [])
        do, up, back, gdown, gin, sq = feed(
            place[k], p, pieces, total, heads, prior, x_all[k], dy_all[k], win, wdown, wout
        )
        order = gdown
        ups[s:] = [up]
        backs[s:] = [back]
        sqs.append(sq)
        if last:
            qkv = project(place[k], total, heads, qkv, after(x_all[k], order), wqkv, *table)
    context, wide, keep, ctx_sq, *done = attend(*qkv, [gdown, gin], 4)
    joined = [join(slot[s], False, context, wout, ups[s]) for s in range(1, n)]
    sent = [lax.ppermute(v, "mp", ring(n - s)) for s, v in enumerate(joined, 1)]
    gqkv, gdown, gin = attend_back(*qkv, after(do, *joined), wide, keep, *table[:3], done, [gdown, gin], 3)
    shares = [join(slot[s], True, gqkv, wqkv, backs[s]) for s in range(1, n)]
    gqw, gow, gdown, gin = weight_grads(index, x_all, gqkv, dy_all, context, [gdown, gin])
    result, grad_hidden, sums, gqw, gow = tail(
        [gqw, gow], gqkv, context, wqkv, wout, ln_scale[None, :], backs[0], ups[0], hidden_in, out_grad,
        sent, shares, sqs, ctx_sq, 1,
    )
    gqw, gow = widen(gqw, gow)
    devices = lax.axis_size("dp") * n
    counts = jnp.array([rows * d * devices, rows * d * devices, rows * f * n * devices], F32)
    return (
        result,
        grad_hidden,
        sums[0],
        sums[1],
        gqw,
        gow,
        gin,
        gdown,
        jnp.sqrt(sums[2, :3] / counts),
    )


def solution(mesh):
    tok = P(("dp", "mp"), None)
    cols, rows = P(None, "mp"), P("mp", None)
    return jax.shard_map(
        on_device,
        mesh=mesh,
        in_specs=(tok, P("dp", None), P(), P(), cols, rows, cols, rows, tok),
        out_specs=(tok, tok, P(), P(), cols, rows, cols, rows, P()),
        check_vma=False,
    )
```
